256 devices in a mesh: grp: 2 (over z_lo), gy: 16 (over y, x), gx: 8 (over z_hi, core).
Axes of the slice: x: 4, y: 4, z: 8 (z_hi: 4, z_lo: 2; z = z_hi * 2 + z_lo), core: 2. Of those that a mesh axis runs over, the one named last changes fastest.
Arguments:
- state_in: float32 [2, 60, 160, 320], P('grp', None, 'gy', 'gx'), may hold values from -6 to 6
- cotangent: float32 [2, 60, 160, 320], P('grp', None, 'gy', 'gx'), may hold values from -6 to 6
- faces: float32 [2, 2, 160, 320], P('grp', None, 'gy', 'gx'), may hold values from 0.02 to 0.2
- mixing: float32 [2, 60, 60], P('grp'), may hold values from 0 to 0.008
- anchor_row: int32 [1], replicated, may hold values from 0 to 144
- anchor_col: int32 [1], replicated, may hold values from 0 to 288
Outputs:
- tangent_out: float32 [2, 60, 160, 320], P('grp', None, 'gy', 'gx')
- adjoint_out: float32 [2, 60, 160, 320], P('grp', None, 'gy', 'gx')
The draws below stay inside these ranges and needn't reach their ends.
Inputs may be any that keep to these rules, and one draw needn't show every extreme that they name: `anchor_row`: the zoom region lies wholly inside the parent grid. `anchor_col`: the zoom region lies wholly inside the parent grid.
All inputs are finite; a program needn't handle non-finite values.
Results may differ from the reference program's by a relative error of at most 0.0001.
Values sent between devices are 32-bit elements; how exact they have to be, the bound alone decides.
A program may use at most 64 MiB of HBM per device.

```python
import jax
import jax.numpy as jnp
from jax import lax

L = 60
SUB = 10
R = 10
FRAME = 2
NY = 160
NX = 320
BY = 16
BX = 32


def shard_levels(own_key, shape, cuts, smallest, high):
    loudness, own = 1.0, jax.random.fold_in(own_key, 6)
    for dim, shards_of in cuts:
        steps = jnp.exp(jax.random.uniform(jax.random.fold_in(own, dim), (shards_of,), jnp.float32, smallest / len(cuts), high / len(cuts)))
        loudness = loudness * jnp.repeat(steps, shape[dim] // shards_of).reshape([-1 if axis == dim else 1 for axis in range(len(shape))])
    return loudness


def gaussian(key, shape, width, reach, shards=(), dtype=jnp.bfloat16):
    values = width * jax.random.normal(key, shape, jnp.float32)
    if shards:
        values = values * shard_levels(key, shape, shards, -0.22, 0.18)
    return jnp.clip(values, -reach, reach).astype(dtype)


def setup_inputs(seed: int = 0) -> dict:
    arg_keys = jax.random.split(jax.random.key(seed), 7)
    state_in = gaussian(arg_keys[0], (2, L, NY, NX), 1.0, 6.0, ((0, 2), (2, 16), (3, 8)), jnp.float32)
    cotangent = gaussian(arg_keys[1], (2, L, NY, NX), 1.0, 6.0, ((0, 2), (2, 16), (3, 8)), jnp.float32)
    faces = jnp.clip(0.02 + 0.18 * jax.random.uniform(arg_keys[2], (2, 2, NY, NX), jnp.float32) ** shard_levels(arg_keys[2], (2, 2, NY, NX), ((0, 2), (2, 16), (3, 8)), -0.2, 0.2), 0.02, 0.2)
    mixing = jnp.clip(0.008 * jax.random.uniform(arg_keys[3], (2, L, L), jnp.float32) ** shard_levels(arg_keys[3], (2, L, L), ((0, 2),), -0.2, 0.2), 0.0, 0.008)
    anchor_row = jax.random.randint(arg_keys[4], (1,), 0, NY - BY + 1).astype(jnp.int32)
    anchor_col = jax.random.randint(arg_keys[5], (1,), 0, NX - BX + 1).astype(jnp.int32)
    return {"state_in": state_in, "cotangent": cotangent, "faces": faces, "mixing": mixing, "anchor_row": anchor_row, "anchor_col": anchor_col}


def edge_faces(pair):
    rows = jnp.arange(NY)[:, None]
    cols = jnp.arange(NX)[None, :]
    east_face = jnp.where(cols == NX - 1, jnp.float32(0.0), pair[0])
    north_face = jnp.where(rows == NY - 1, jnp.float32(0.0), pair[1])
    return east_face, north_face


def diffuse(field, east_face, north_face):
    zero_col = jnp.zeros_like(field[:, :, :1])
    east_flux = east_face * (jnp.concatenate([field[:, :, 1:], zero_col], 2) - field)
    west_flux = jnp.concatenate([zero_col, east_flux[:, :, :-1]], 2)
    zero_row = jnp.zeros_like(field[:, :1, :])
    north_flux = north_face * (jnp.concatenate([field[:, 1:, :], zero_row], 1) - field)
    south_flux = jnp.concatenate([zero_row, north_flux[:, :-1, :]], 1)
    return field + east_flux - west_flux + north_flux - south_flux


def mix_down(field, matrix):
    return jnp.einsum("lm,myx->lyx", matrix, field, precision=lax.Precision.HIGHEST) + 0.75 * field


def mix_up(field, matrix):
    return jnp.einsum("ml,myx->lyx", matrix, field, precision=lax.Precision.HIGHEST) + 0.75 * field


def inject(box):
    return jnp.repeat(jnp.repeat(box, R, axis=1), R, axis=2)


def reference(state_in, cotangent, faces, mixing, anchor_row, anchor_col):
    starts = (jnp.zeros((), jnp.int32), anchor_row[0].astype(jnp.int32), anchor_col[0].astype(jnp.int32))
    global_east, global_north = edge_faces(faces[0])
    zoom_east, zoom_north = edge_faces(faces[1])
    rows = jnp.arange(NY)[:, None]
    cols = jnp.arange(NX)[None, :]
    edge = (rows < FRAME) | (rows >= NY - FRAME) | (cols < FRAME) | (cols >= NX - FRAME)
    frame = edge.astype(jnp.float32)
    inside = 1.0 - frame
    coarse = mix_down(diffuse(state_in[0], global_east, global_north), mixing[0])
    boundary = inject(lax.dynamic_slice(coarse, starts, (L, BY, BX)))
    fine = state_in[1]
    for substep in range(SUB):
        fine = mix_down(diffuse(fine, zoom_east, zoom_north), mixing[1])
        fine = fine * inside + boundary * frame
    averages = fine.reshape(L, BY, R, BX, R).mean(axis=(2, 4))
    coarse_out = lax.dynamic_update_slice(coarse, averages, starts)
    forcing = cotangent[0]
    forcing_box = lax.dynamic_slice(forcing, starts, (L, BY, BX))
    adjoint_fine = cotangent[1] + inject(forcing_box) / (R * R)
    collected = jnp.zeros((L, BY, BX), jnp.float32)
    for substep in range(SUB):
        collected = collected + (adjoint_fine * frame).reshape(L, BY, R, BX, R).sum(axis=(2, 4))
        adjoint_fine = diffuse(mix_up(adjoint_fine * inside, mixing[1]), zoom_east, zoom_north)
    widened = lax.dynamic_update_slice(forcing, collected, starts)
    adjoint_coarse = diffuse(mix_up(widened, mixing[0]), global_east, global_north)
    return jnp.stack([coarse_out, fine]), jnp.stack([adjoint_coarse, adjoint_fine])
```

```python
import functools

import jax
import jax.numpy as jnp
from jax import lax
from jax.experimental import pallas as pl
from jax.experimental.pallas import tpu as pltpu
from jax.sharding import PartitionSpec as P

MESH = pl.DeviceIdType.MESH
HIGHEST = lax.Precision.HIGHEST
F32 = jnp.float32
VMEM = pltpu.VMEM
L = 60
H = 10
W = 40
NY = 160
NX = 320
GY = 16
GX = 8
FRAME = 2
LV = 64
NB = 24
YS = LV + NB


def dot(a, b):
    return lax.dot_general(a, b, (((1,), (0,)), ((), ())), precision=HIGHEST, preferred_element_type=F32)


def dot_t(a, b):
    return lax.dot_general(a, b, (((1,), (1,)), ((), ())), precision=HIGHEST, preferred_element_type=F32)


def gather_kernel(
    anchor_ref, z_ref, chunk_ref, own_ref, cols_ref,
    ext_ref, patch_ref, north_ref, south_ref, east_ref, west_ref,
    strip_out, strip_in, part, pad, send, got,
    strip_s, strip_r, ns_s, ns_r, a_s, a_r, ring_s, ring_r, b_s, b_r,
):
    grp = lax.axis_index("grp")
    gy = lax.axis_index("gy")
    gx = lax.axis_index("gx")
    up = lax.rem(gy + 1, GY)
    down = lax.rem(gy + GY - 1, GY)
    right = lax.rem(gx + 1, GX)
    left = lax.rem(gx + GX - 1, GX)
    barrier = pltpu.get_barrier_semaphore()

    def hello(*where):
        pl.semaphore_signal(barrier, inc=1, device_id=where, device_id_type=MESH)

    def cross(j, c):
        hello(1 - grp, j, gx)
        return c

    lax.fori_loop(0, GY, cross, 0)
    hello(grp, up, gx)
    hello(grp, down, gx)

    @pl.when(grp == 1)
    def _():
        hello(grp, gy, left)
        hello(grp, gy, right)
        pl.semaphore_wait(barrier, GY + 4)

    @pl.when(grp == 0)
    def _():
        def peer(k, c):
            hello(grp, gy, lax.rem(gx + k, GX))
            return c

        lax.fori_loop(1, GX, peer, 0)
        pl.semaphore_wait(barrier, GY + 2 + GX - 1)

    def b_copy(zy, py):
        return pltpu.make_async_remote_copy(
            src_ref=send.at[zy], dst_ref=got.at[py], send_sem=b_s.at[zy], recv_sem=b_r.at[py],
            device_id=(1, zy, gx), device_id_type=MESH,
        )

    @pl.when(grp == 1)
    def _():
        lane = lax.broadcasted_iota(jnp.int32, (LV, 128), 1) % 64
        for q in range(2):
            east = jnp.zeros((LV, 128), F32)
            west = jnp.zeros((LV, 128), F32)
            for k in range(5):
                row = z_ref[5 * q + k]
                here = (lane >= 10 * k) & (lane < 10 * k + 10)
                east = jnp.where(here, pltpu.roll(row, (10 * k - 40) % 128, 1), east)
                west = jnp.where(here, pltpu.roll(row, (10 * k - 10) % 128, 1), west)
            strip_out[0, q] = east
            strip_out[1, q] = west
        sides = []
        for s, to in ((0, right), (1, left)):
            copy = pltpu.make_async_remote_copy(
                src_ref=strip_out.at[s], dst_ref=strip_in.at[s], send_sem=strip_s.at[s], recv_sem=strip_r.at[s],
                device_id=(1, gy, to), device_id_type=MESH,
            )
            copy.start()
            sides.append(copy)
        for copy in sides:
            copy.wait()
        for q in range(2):
            from_west = strip_in[0, q]
            from_east = strip_in[1, q]
            for k in range(5):
                row = z_ref[5 * q + k]
                row = jnp.where(lane < 10, pltpu.roll(from_west, (-10 * k) % 128, 1), row)
                row = jnp.where((lane >= 50) & (lane < 60), pltpu.roll(from_east, (50 - 10 * k) % 128, 1), row)
                ext_ref[H + 5 * q + k] = row
        ends = []
        for s, to in ((0, up), (1, down)):
            copy = pltpu.make_async_remote_copy(
                src_ref=ext_ref.at[pl.ds(H, H)], dst_ref=ext_ref.at[pl.ds(2 * H * s, H)],
                send_sem=ns_s.at[s], recv_sem=ns_r.at[s],
                device_id=(1, to, gx), device_id_type=MESH,
            )
            copy.start()
            ends.append(copy)

        def arrive(py, total):
            b_copy(gy, py).wait_recv()
            return total + got[py]

        patch_ref[...] = lax.fori_loop(0, GY, arrive, jnp.zeros((5, 8, 128), F32))
        for copy in ends:
            copy.wait()

    @pl.when(grp == 0)
    def _():
        def a_copy(to, sender):
            return pltpu.make_async_remote_copy(
                src_ref=chunk_ref.at[to], dst_ref=part.at[sender], send_sem=a_s.at[to], recv_sem=a_r.at[sender],
                device_id=(0, gy, to), device_id_type=MESH,
            )

        def a_start(k, c):
            a_copy(lax.rem(gx + k, GX), gx).start()
            return c

        lax.fori_loop(1, GX, a_start, 0)
        ring = []
        for s, (src, dst, where) in enumerate((
            (own_ref.at[H - 1], south_ref, (0, up, gx)),
            (own_ref.at[0], north_ref, (0, down, gx)),
            (cols_ref.at[1], west_ref, (0, gy, right)),
            (cols_ref.at[0], east_ref, (0, gy, left)),
        )):
            copy = pltpu.make_async_remote_copy(
                src_ref=src, dst_ref=dst, send_sem=ring_s.at[s], recv_sem=ring_r.at[s],
                device_id=where, device_id_type=MESH,
            )
            copy.start()
            ring.append(copy)

        def a_arrive(k, total):
            sender = lax.rem(gx + k, GX)
            a_copy(gx, sender).wait_recv()
            return total + part[sender]

        total = lax.fori_loop(1, GX, a_arrive, chunk_ref[gx])
        pad[0:5] = jnp.zeros((5, 8, 128), F32)
        pad[15:20] = jnp.zeros((5, 8, 128), F32)
        pad[5:15] = total
        offset = anchor_ref[0] - 2 - H * gy + 5

        def b_start(zy, c):
            start = jnp.clip(zy + offset, 0, 15)
            for i in range(5):
                send[zy, i] = pad[start + i]
            b_copy(zy, gy).start()
            return c

        lax.fori_loop(0, GY, b_start, 0)

        def a_sent(k, c):
            a_copy(lax.rem(gx + k, GX), gx).wait_send()
            return c

        lax.fori_loop(1, GX, a_sent, 0)
        for copy in ring:
            copy.wait()

        def b_sent(zy, c):
            b_copy(zy, gy).wait_send()
            return c

        lax.fori_loop(0, GY, b_sent, 0)


def vmem(n):
    return [pl.BlockSpec(memory_space=VMEM)] * n


def smem():
    return pl.BlockSpec(memory_space=pltpu.SMEM)


def gather(anchor, z, chunks, own, cols):
    dma = pltpu.SemaphoreType.DMA
    return pl.pallas_call(
        gather_kernel,
        name="gather",
        out_shape=(
            jax.ShapeDtypeStruct((3 * H, LV, 128), F32),
            jax.ShapeDtypeStruct((5, 8, 128), F32),
            jax.ShapeDtypeStruct((W, 128), F32),
            jax.ShapeDtypeStruct((W, 128), F32),
            jax.ShapeDtypeStruct((16, 128), F32),
            jax.ShapeDtypeStruct((16, 128), F32),
        ),
        in_specs=[smem()] + vmem(4),
        out_specs=tuple(vmem(6)),
        scratch_shapes=[
            VMEM((2, 2, LV, 128), F32),
            VMEM((2, 2, LV, 128), F32),
            VMEM((GX, H, 8, 128), F32),
            VMEM((20, 8, 128), F32),
            VMEM((GY, 5, 8, 128), F32),
            VMEM((GY, 5, 8, 128), F32),
            dma((2,)), dma((2,)), dma((2,)), dma((2,)),
            dma((GX,)), dma((GX,)), dma((4,)), dma((4,)), dma((GY,)), dma((GY,)),
        ],
        compiler_params=pltpu.CompilerParams(collective_id=0, has_side_effects=True, vmem_limit_bytes=32 * 2**20),
    )(anchor, z, chunks, own, cols)


def zoom_kernel(pos_ref, ext_ref, patch_ref, mix_ref, tan_ref, adj_ref, msg_ref, ya, yb, cf, en, bs, ss):
    zy = pos_ref[1]
    zx = pos_ref[2]

    @pl.when(pos_ref[0] == 1)
    def _():
        zoom_body(zy, zx, ext_ref, patch_ref, mix_ref, tan_ref, adj_ref, msg_ref, ya, yb, cf, en, bs, ss)


def zoom_body(zy, zx, ext_ref, patch_ref, mix_ref, tan_ref, adj_ref, msg_ref, ya, yb, cf, en, bs, ss):
    rows = 3 * H
    row2 = lax.broadcasted_iota(jnp.int32, (rows, 128), 0)
    lane2 = lax.broadcasted_iota(jnp.int32, (rows, 128), 1)
    col2 = lane2 % 64
    tangent = lane2 < 64

    def interior(dr, dc):
        gr = row2 + (dr - H) + zy * H
        gc = col2 + (dc - H) + zx * W
        keep = (gr >= FRAME) & (gr < NY - FRAME) & (gc >= FRAME) & (gc < NX - FRAME)
        return jnp.where(keep, F32(1.0), F32(0.0))

    def incoming(dr, dc):
        return jnp.where(tangent, F32(1.0), interior(dr, dc))

    inside = interior(0, 0)
    outgoing = jnp.where(tangent, inside, F32(1.0))
    for i in range(2):
        en[i] = jnp.zeros((48, 128), F32)
    for r in range(rows):
        en[0, 8 + r : 9 + r] = ext_ref[r, L : L + 1]
        en[1, 8 + r : 9 + r] = ext_ref[r, L + 1 : L + 2]
    east = en[0, 8:38]
    west = pltpu.roll(east, 1, 1)
    north = en[1, 8:38]
    south = en[1, 7:37]
    cf[0, 0:rows] = outgoing * incoming(0, 0) * (1.0 - east - west - north - south)
    cf[1, 0:rows] = outgoing * incoming(0, 1) * east
    cf[2, 0:rows] = outgoing * incoming(0, -1) * west
    cf[3, 0:rows] = outgoing * incoming(1, 0) * north
    cf[4, 0:rows] = outgoing * incoming(-1, 0) * south
    cf[5, 0:rows] = 1.0 - inside

    b3 = lax.broadcasted_iota(jnp.int32, (NB, 128), 0)
    lane3 = lax.broadcasted_iota(jnp.int32, (NB, 128), 1)
    column3 = (lane3 % 64) // 10
    for r in range(rows):
        match = (b3 // 8 == r // H) & (b3 % 8 == column3 + 1) & (lane3 % 64 < 60)
        level = jnp.where(lane3 < 64, cf[5, r : r + 1], F32(0.01))
        ya[r, 0:LV] = ext_ref[r]
        ya[r, LV:YS] = jnp.where(match, level, F32(0.0))

    for k in range(10):
        src, dst = (ya, yb) if k % 2 == 0 else (yb, ya)

        def collect(i, total, src=src, k=k):
            line = src[H + i]
            bs[i, k * NB : (k + 1) * NB] = line[LV:YS]
            return total + cf[5, pl.ds(H + i, 1)] * line

        ss[k, 0:YS] = lax.fori_loop(0, H, collect, jnp.zeros((YS, 128), F32))
        ss[k, YS:128] = jnp.zeros((128 - YS, 128), F32)

        def update(r, c, src=src, dst=dst):
            line = src[r]
            dst[r] = (
                cf[0, pl.ds(r, 1)] * line
                + cf[1, pl.ds(r, 1)] * pltpu.roll(line, 127, 1)
                + cf[2, pl.ds(r, 1)] * pltpu.roll(line, 1, 1)
                + cf[3, pl.ds(r, 1)] * src[r + 1]
                + cf[4, pl.ds(r, 1)] * src[r - 1]
            )
            return c

        lax.fori_loop(k + 1, rows - 1 - k, update, 0)

    m1 = mix_ref[...]
    m2 = dot(m1, m1)
    m4 = dot(m2, m2)
    m8 = dot(m4, m4)
    m10 = dot(m8, m2)

    patch = patch_ref[...]
    e3 = jnp.broadcast_to(patch[:, :, L : L + 1], patch.shape)
    n3 = jnp.broadcast_to(patch[:, :, L + 1 : L + 2], patch.shape)
    here = patch[1:4]
    e_here = e3[1:4]
    coarse = (
        here
        + e_here * (pltpu.roll(here, 7, 1) - here)
        - pltpu.roll(e_here, 1, 1) * (here - pltpu.roll(here, 1, 1))
        + n3[1:4] * (patch[2:5] - here)
        - n3[0:3] * (here - patch[0:3])
    ).reshape(NB, 128)
    v0 = jnp.where(lane3 < L, coarse, F32(0.0))
    forcing = jnp.where(lane3 < L, pltpu.roll(here.reshape(NB, 128), 64, 1), F32(0.0))
    v01 = jnp.concatenate([v0, dot_t(v0, m1)], 0)
    v03 = jnp.concatenate([v01, dot_t(v01, m2)], 0)
    v09 = jnp.concatenate([v03, dot_t(v03, m4), dot_t(v01, m8), jnp.zeros((16, 128), F32)], 0)
    boundary_left = jnp.transpose(v09)
    both = m10.T + pltpu.roll(m10, 64, 1)
    force = pltpu.roll(dot(forcing, m10), 64, 1)
    main_left = jnp.transpose(jnp.concatenate([both[0:LV], force, jnp.zeros((128 - YS, 128), F32)], 0))[:, 0:YS]

    total = jnp.zeros((LV, 128), F32)
    for r in range(H):
        bs[r, 240:256] = jnp.zeros((16, 128), F32)
        out = dot(main_left, ya[H + r])
        fine = out[0:LV] + dot(boundary_left[0:LV], bs[r])
        total = total + fine
        tan_ref[:, r, :] = pltpu.roll(fine, 118, 1)[0:L, 0:W]
        adj_ref[:, r, :] = pltpu.roll(out[LV:128], 54, 1)[0:L, 0:W]

    i8 = lax.broadcasted_iota(jnp.int32, (8, 128), 0)
    lane8 = lax.broadcasted_iota(jnp.int32, (8, 128), 1)
    block8 = i8 - 4 * lax.rem(zy, 2)
    pick_tan = jnp.where((lane8 >= 10) & (lane8 < 50) & (lane8 // 10 - 1 == block8), F32(1.0), F32(0.0))
    pick_adj = jnp.where((lane8 >= 74) & (lane8 < 114) & ((lane8 - 64) // 10 - 1 == block8), F32(1.0), F32(0.0))
    averages = dot_t(pick_tan, jnp.concatenate([total, jnp.zeros((64, 128), F32)], 0)) * F32(0.01)
    sums = jnp.concatenate([dot_t(pick_adj, ss[k]) for k in range(10)], 0)
    lane80 = lax.broadcasted_iota(jnp.int32, (80, 128), 1)
    forcing_pad = jnp.concatenate([forcing, jnp.zeros((128 - NB, 128), F32)], 0)
    u = jnp.where(lane80 < L, sums, F32(0.0)) + dot(pltpu.roll(sums, 64, 1), forcing_pad)
    u = [u[8 * k : 8 * k + 8] for k in range(10)]
    p = jnp.concatenate(u[0::2], 0) + dot(jnp.concatenate(u[1::2], 0), m1)
    q = dot(jnp.concatenate([p[8:16], p[24:32]], 0), m2)
    collected = p[0:8] + q[0:8] + dot(p[16:24] + q[8:16], m4) + dot(p[32:40], m8)
    msg_ref[...] = jnp.where(lane8 < L, averages, F32(0.0)) + pltpu.roll(jnp.where(lane8 < L, collected, F32(0.0)), 64, 1)


def zoom(pos, ext, patch, mix):
    field = jax.ShapeDtypeStruct((L, H, W), F32)
    return pl.pallas_call(
        zoom_kernel,
        name="zoom",
        out_shape=(field, field, jax.ShapeDtypeStruct((8, 128), F32)),
        in_specs=[smem()] + vmem(3),
        out_specs=tuple(vmem(3)),
        scratch_shapes=[
            VMEM((3 * H, YS, 128), F32),
            VMEM((3 * H, YS, 128), F32),
            VMEM((6, 32, 128), F32),
            VMEM((2, 48, 128), F32),
            VMEM((H, 256, 128), F32),
            VMEM((10, 128, 128), F32),
        ],
        compiler_params=pltpu.CompilerParams(vmem_limit_bytes=32 * 2**20),
    )(pos, ext, patch, mix)


def spread_kernel(msg_ref, box_ref, got, c_s, c_r, d_s, d_r):
    grp = lax.axis_index("grp")
    gy = lax.axis_index("gy")
    gx = lax.axis_index("gx")
    barrier = pltpu.get_barrier_semaphore()

    def hello(*where):
        pl.semaphore_signal(barrier, inc=1, device_id=where, device_id_type=MESH)

    def cross(j, c):
        hello(1 - grp, j, gx)
        return c

    lax.fori_loop(0, GY, cross, 0)

    @pl.when(grp == 1)
    def _():
        pl.semaphore_wait(barrier, GY)

    @pl.when(grp == 0)
    def _():
        def peer(k, c):
            hello(grp, gy, lax.rem(gx + k, GX))
            return c

        lax.fori_loop(1, GX, peer, 0)
        pl.semaphore_wait(barrier, GY + GX - 1)

    def c_copy(py, zy):
        return pltpu.make_async_remote_copy(
            src_ref=msg_ref, dst_ref=got.at[zy], send_sem=c_s.at[py], recv_sem=c_r.at[zy],
            device_id=(0, py, gx), device_id_type=MESH,
        )

    @pl.when(grp == 1)
    def _():
        def start(k, c):
            c_copy(k, gy).start()
            return c

        lax.fori_loop(0, GY, start, 0)

        def sent(k, c):
            c_copy(k, gy).wait_send()
            return c

        lax.fori_loop(0, GY, sent, 0)

    @pl.when(grp == 0)
    def _():
        def arrive(k, c):
            c_copy(gy, 2 * k).wait_recv()
            c_copy(gy, 2 * k + 1).wait_recv()
            box_ref[gx, k] = got[2 * k] + got[2 * k + 1]
            return c

        lax.fori_loop(0, GY // 2, arrive, 0)

        def d_copy(to, sender):
            return pltpu.make_async_remote_copy(
                src_ref=box_ref.at[gx], dst_ref=box_ref.at[sender], send_sem=d_s.at[to], recv_sem=d_r.at[sender],
                device_id=(0, gy, to), device_id_type=MESH,
            )

        def start(k, c):
            d_copy(lax.rem(gx + k, GX), gx).start()
            return c

        lax.fori_loop(1, GX, start, 0)

        def finish(k, c):
            other = lax.rem(gx + k, GX)
            d_copy(gx, other).wait_recv()
            d_copy(other, gx).wait_send()
            return c

        lax.fori_loop(1, GX, finish, 0)


def spread(msg):
    dma = pltpu.SemaphoreType.DMA
    return pl.pallas_call(
        spread_kernel,
        name="spread",
        out_shape=jax.ShapeDtypeStruct((GX, GY // 2, 8, 128), F32),
        in_specs=vmem(1),
        out_specs=vmem(1)[0],
        scratch_shapes=[VMEM((GY, 8, 128), F32), dma((GY,)), dma((GY,)), dma((GX,)), dma((GX,))],
        compiler_params=pltpu.CompilerParams(collective_id=1, has_side_effects=True),
    )(msg)


def final_kernel(
    pos_ref, box_ref, own_ref, north_ref, south_ref, east_ref, west_ref, mix_ref, tan_ref, adj_ref,
    tan_out, adj_out, g, boxpad,
):
    @pl.when(pos_ref[0] == 1)
    def _():
        tan_out[...] = tan_ref[...]
        adj_out[...] = adj_ref[...]

    @pl.when(pos_ref[0] == 0)
    def _():
        py = pos_ref[1]
        px = pos_ref[2]
        row0 = py * H - 1 - pos_ref[3]
        col0 = px * W - 8 - pos_ref[4]
        for i in range(16):
            boxpad[i, 0:56] = jnp.zeros((56, 128), F32)
            boxpad[i, 88:144] = jnp.zeros((56, 128), F32)
            for z in range(GX):
                half = 4 * (i % 2)
                boxpad[i, 56 + 4 * z : 60 + 4 * z] = box_ref[z, i // 2, half : half + 4]
        g[...] = jnp.zeros(g.shape, F32)
        for r in range(H):
            g[1 + r, 8:48] = own_ref[r]
            g[1 + r, 7:8] = west_ref[r : r + 1]
            g[1 + r, 48:49] = east_ref[r : r + 1]
        g[0, 8:48] = south_ref[...]
        g[H + 1, 8:48] = north_ref[...]

        sub = lax.broadcasted_iota(jnp.int32, (56, 128), 0)
        lane = lax.broadcasted_iota(jnp.int32, (56, 128), 1)
        in_cols = (sub + col0 >= 0) & (sub + col0 < 32)
        start = jnp.clip(col0 + 56, 0, 88)
        r128 = lax.broadcasted_iota(jnp.int32, (128, 128), 0)
        c128 = lax.broadcasted_iota(jnp.int32, (128, 128), 1)
        unit = jnp.where((r128 == c128) & (r128 < 64), F32(1.0), F32(0.0))
        mix = unit + pltpu.roll(jnp.concatenate([jnp.zeros((64, 128), F32), mix_ref[0:64]], 0), 64, 1)

        def one(i, c):
            br = row0 + i
            within = in_cols & (br >= 0) & (br < 16)
            window = boxpad[jnp.clip(br, 0, 15), pl.ds(start, 56)]
            w = jnp.where(within & (lane >= 64), window, g[i])
            g[i] = dot(w, mix)
            return c

        lax.fori_loop(0, H + 2, one, 0)

        def two(r, c):
            y = g[r + 1]
            upper = g[r + 2]
            lower = g[r]
            e = jnp.broadcast_to(y[:, L : L + 1], y.shape)
            n = jnp.broadcast_to(y[:, L + 1 : L + 2], y.shape)
            s = jnp.broadcast_to(lower[:, L + 1 : L + 2], y.shape)
            out = (
                y
                + e * (pltpu.roll(y, 55, 0) - y)
                - pltpu.roll(e, 1, 0) * (y - pltpu.roll(y, 1, 0))
                + n * (upper - y)
                - s * (y - lower)
            )
            br = row0 + r + 1
            within = in_cols & (br >= 0) & (br < 16)
            window = boxpad[jnp.clip(br, 0, 15), pl.ds(start, 56)]
            out = jnp.where(within & (lane < 64), window, out)
            g[r] = out
            return c

        lax.fori_loop(0, H, two, 0)
        for r in range(H):
            flat = jnp.transpose(jnp.concatenate([g[r, 8:48], jnp.zeros((88, 128), F32)], 0))
            tan_out[:, r, :] = flat[0:L, 0:W]
            adj_out[:, r, :] = flat[64 : 64 + L, 0:W]


def final(pos, box, own, north, south, east, west, mix, tan, adj):
    field = jax.ShapeDtypeStruct((L, H, W), F32)
    return pl.pallas_call(
        final_kernel,
        name="final",
        out_shape=(field, field),
        in_specs=[smem()] + vmem(9),
        out_specs=tuple(vmem(2)),
        scratch_shapes=[VMEM((12, 56, 128), F32), VMEM((16, 144, 128), F32)],
        compiler_params=pltpu.CompilerParams(vmem_limit_bytes=32 * 2**20),
    )(pos, box, own, north, south, east, west, mix, tan, adj)


def shards(state_in, cotangent, faces, mixing, anchor_row, anchor_col):
    grp = lax.axis_index("grp")
    gy = lax.axis_index("gy")
    gx = lax.axis_index("gx")
    pos = jnp.stack([grp, gy, gx, anchor_row[0], anchor_col[0]]).astype(jnp.int32)
    state = state_in[0]
    forcing = cotangent[0]
    rows = gy * H + jnp.arange(H, dtype=jnp.int32)
    cols = gx * W + jnp.arange(W, dtype=jnp.int32)
    east = jnp.where(cols[None, :] == NX - 1, F32(0.0), faces[0, 0])
    north = jnp.where(rows[:, None] == NY - 1, F32(0.0), faces[0, 1])
    both = jnp.stack([east, north])
    zeros2 = jnp.zeros((2, H, W), F32)
    mix = jnp.pad(mixing[0] + 0.75 * jnp.eye(L, dtype=F32), ((0, 128 - L), (0, 128 - L)))

    z_tan = jnp.pad(jnp.concatenate([state, both, zeros2], 0), ((0, 0), (0, 0), (H, 64 - H - W)))
    z_adj = jnp.pad(jnp.concatenate([forcing, both, zeros2], 0), ((0, 0), (0, 0), (H, 64 - H - W)))
    z = jnp.concatenate([z_tan, z_adj], 2).transpose(1, 0, 2)

    mixed = jnp.einsum("lm,myx->lyx", mixing[0], state, precision=HIGHEST) + 0.75 * state
    cells = jnp.concatenate([mixed, both, zeros2, forcing, jnp.zeros((4, H, W), F32)], 0)
    own = cells.transpose(1, 2, 0)
    start = jnp.clip(anchor_col[0] - 2 - W * gx, -36, W) + 36
    zero = jnp.zeros((), jnp.int32)
    window = lax.dynamic_slice(jnp.pad(own, ((0, 0), (36, 36), (0, 0))), (zero, start, zero), (H, 36, 128))
    chunks = jnp.stack([window[:, 4 * k : 4 * k + 8] for k in range(GX)])
    ends = jnp.stack([jnp.pad(own[:, 0], ((0, 6), (0, 0))), jnp.pad(own[:, W - 1], ((0, 6), (0, 0)))])

    ext, patch, ring_n, ring_s, ring_e, ring_w = gather(anchor_row, z, chunks, own, ends)
    tan, adj, msg = zoom(pos, ext, patch, mix)
    box = spread(msg)
    tan, adj = final(pos, box, own, ring_n, ring_s, ring_e, ring_w, mix, tan, adj)
    return tan[None], adj[None]


def solution(mesh):
    placed = (
        P("grp", None, "gy", "gx"),
        P("grp", None, "gy", "gx"),
        P("grp", None, "gy", "gx"),
        P("grp", None, None),
        P(),
        P(),
    )
    return jax.shard_map(
        shards,
        mesh=mesh,
        in_specs=placed,
        out_specs=(P("grp", None, "gy", "gx"), P("grp", None, "gy", "gx")),
        check_vma=False,
    )
```

```python
import jax
import jax.numpy as jnp
from jax import lax
from jax.experimental import pallas as pl
from jax.experimental.pallas import tpu as pltpu
from jax.sharding import PartitionSpec as P

MESH = pl.DeviceIdType.MESH
HIGHEST = lax.Precision.HIGHEST
F32 = jnp.float32
VMEM = pltpu.VMEM
L = 60
H = 10
W = 40
NY = 160
NX = 320
GY = 16
GX = 8
FRAME = 2
SUB = 10
CHUNKS = 4
ROWS = 3 * H
BLOCK = 6
BOX0 = 56


def dot(a, b):
    return lax.dot_general(a, b, (((1,), (0,)), ((), ())), precision=HIGHEST, preferred_element_type=F32)


def dot_t(a, b):
    return lax.dot_general(a, b, (((1,), (1,)), ((), ())), precision=HIGHEST, preferred_element_type=F32)


def iota(shape, dim):
    return lax.broadcasted_iota(jnp.int32, shape, dim)


def only(keep, value=1.0):
    return jnp.where(keep, F32(value), F32(0.0))


def padded_rows(a, rows):
    return jnp.concatenate([a, jnp.zeros((rows - a.shape[0], a.shape[1]), F32)], 0)


def lanes_to_rows(a, count):
    return jnp.concatenate([a[:, 128 * k : 128 * k + 128] for k in range(count)], 0)


def rows_to_lanes(a, count):
    return jnp.concatenate([a[8 * k : 8 * k + 8] for k in range(count)], 1)


def kernel(
    arow_ref, acol_ref, state_hbm, cot_hbm, faces_hbm, mix_hbm,
    out_ref,
    state, cot, faces, mixing, load_s, raw_t, raw_x, square,
    ya, yb, yc, yd, cf, cfb, en, bs, ss, mp, npow, strip_out, strip_in, got, msg,
    cells, pc, ends, part, pad, send, g, ring_n, ring_s, ring_e, ring_w, faces_b, coarse, box, boxpad,
    strip_s, strip_r, ns_s, ns_r, a_s, a_r, ring_snd, ring_rcv, b_s, b_r, c_s, c_r,
):
    grp = lax.axis_index("grp")
    gy = lax.axis_index("gy")
    gx = lax.axis_index("gx")
    up = lax.rem(gy + 1, GY)
    down = lax.rem(gy + GY - 1, GY)
    right = lax.rem(gx + 1, GX)
    left = lax.rem(gx + GX - 1, GX)
    loads = [
        pltpu.make_async_copy(src, dst, load_s.at[i])
        for i, (src, dst) in enumerate(((state_hbm, state), (cot_hbm, cot), (faces_hbm, faces), (mix_hbm, mixing)))
    ]
    for copy in loads:
        copy.start()
    barrier = pltpu.get_barrier_semaphore()

    def hello(*where):
        pl.semaphore_signal(barrier, inc=1, device_id=where, device_id_type=MESH)

    def cross(j, c):
        hello(1 - grp, lax.rem(gy + j, GY), gx)
        return c

    hello(grp, up, gx)
    hello(grp, down, gx)

    @pl.when(grp == 1)
    def _():
        hello(grp, gy, left)
        hello(grp, gy, right)

    @pl.when(grp == 0)
    def _():
        def peer(k, c):
            hello(grp, gy, lax.rem(gx + k, GX))
            return c

        lax.fori_loop(1, GX, peer, 0)

    lax.fori_loop(0, GY, cross, 0)

    raw_t[...] = jnp.zeros(raw_t.shape, F32)
    raw_x[...] = jnp.zeros(raw_x.shape, F32)
    square[...] = jnp.zeros((128, 128), F32)
    for copy in loads:
        copy.wait()
    last_col = gx * W + iota((1, W), 1) == NX - 1
    for r in range(H):
        raw_t[r, 0:L, 0:W] = state[0, :, r, :]
        raw_x[r, 0:L, 0:W] = cot[0, :, r, :]
        east = jnp.where(last_col, F32(0.0), faces[0, 0, r : r + 1, :])
        north = faces[0, 1, r : r + 1, :]
        if r == H - 1:
            north = jnp.where(gy * H + r + 0 * iota((1, W), 1) == NY - 1, F32(0.0), north)
        for raw in (raw_t, raw_x):
            raw[r, L : L + 1, 0:W] = east
            raw[r, L + 1 : L + 2, 0:W] = north
    square[0:L, 0:L] = mixing[0] + only(iota((L, L), 0) == iota((L, L), 1), 0.75)

    def b_copy(zy, py):
        return pltpu.make_async_remote_copy(
            src_ref=send.at[zy], dst_ref=got.at[py], send_sem=b_s.at[zy], recv_sem=b_r.at[py],
            device_id=(1, zy, gx), device_id_type=MESH,
        )

    @pl.when(grp == 1)
    def _():
        zoom(
            gy, gx, up, down, left, right, barrier, b_copy, out_ref, raw_t, raw_x, square,
            ya, yb, yc, yd, cf, cfb, en, bs, ss, mp, npow, strip_out, strip_in, got, msg, box,
            strip_s, strip_r, ns_s, ns_r, c_s, c_r,
        )

    @pl.when(grp == 0)
    def _():
        parent(
            gy, gx, up, down, left, right, barrier, b_copy, arow_ref, acol_ref, out_ref, raw_t, raw_x, square,
            cells, pc, ends, part, pad, send, g, ring_n, ring_s, ring_e, ring_w, faces_b, coarse, msg, box, boxpad,
            a_s, a_r, ring_snd, ring_rcv, c_s, c_r,
        )


def sweep(src, dst, cfb, k):
    low, high = k + 1, ROWS - 1 - k
    while low < high:
        n = min(BLOCK, high - low)
        line = src[low : low + n]
        dst[low : low + n] = (
            cfb[0, low : low + n] * line
            + cfb[1, low : low + n] * pltpu.roll(line, 127, 3)
            + cfb[2, low : low + n] * pltpu.roll(line, 1, 3)
            + cfb[3, low : low + n] * src[low + 1 : low + n + 1]
            + cfb[4, low : low + n] * src[low - 1 : low + n - 1]
        )
        low += n


def frame_sum(src, cfb):
    return jnp.sum(cfb[5, H : 2 * H] * src[H : 2 * H], axis=0)


def zoom(
    zy, zx, up, down, left, right, barrier, b_copy, out_ref, raw_t, raw_x, square,
    ya, yb, yc, yd, cf, cfb, en, bs, ss, mp, npow, strip_out, strip_in, got, msg, box,
    strip_s, strip_r, ns_s, ns_r, c_s, c_r,
):
    lane = iota((64, 128), 1)
    lane64 = lane % 64
    for r in range(H):
        row = jnp.where((lane >= 10) & (lane < 50), pltpu.roll(raw_t[r], 10, 1), F32(0.0))
        row = jnp.where((lane >= 74) & (lane < 114), pltpu.roll(raw_x[r], 74, 1), row)
        raw_t[r] = row
    for q in range(2):
        east = jnp.zeros((64, 128), F32)
        west = jnp.zeros((64, 128), F32)
        for k in range(5):
            row = raw_t[5 * q + k]
            here = (lane64 >= 10 * k) & (lane64 < 10 * k + 10)
            east = jnp.where(here, pltpu.roll(row, (10 * k - 40) % 128, 1), east)
            west = jnp.where(here, pltpu.roll(row, (10 * k - 10) % 128, 1), west)
        strip_out[0, :, q] = east.reshape(CHUNKS, 2, 8, 128)
        strip_out[1, :, q] = west.reshape(CHUNKS, 2, 8, 128)
    pl.semaphore_wait(barrier, GY + 4)

    def strip_copy(s, c):
        return pltpu.make_async_remote_copy(
            src_ref=strip_out.at[s, c], dst_ref=strip_in.at[s, c], send_sem=strip_s.at[s, c], recv_sem=strip_r.at[s, c],
            device_id=(1, zy, (right, left)[s]), device_id_type=MESH,
        )

    def end_copy(s, c):
        return pltpu.make_async_remote_copy(
            src_ref=ya.at[c, pl.ds(H, H)], dst_ref=ya.at[c, pl.ds(2 * H * s, H)],
            send_sem=ns_s.at[s, c], recv_sem=ns_r.at[s, c],
            device_id=(1, (up, down)[s], zx), device_id_type=MESH,
        )

    order = (3, 0, 1, 2)
    for c in order:
        for s in range(2):
            strip_copy(s, c).start()
    lane16 = iota((2, 8, 128), 2)
    for c in order:
        for s in range(2):
            strip_copy(s, c).wait_recv()
        for q in range(2):
            from_west = strip_in[0, c, q]
            from_east = strip_in[1, c, q]
            for k in range(5):
                row = raw_t[5 * q + k, 16 * c : 16 * c + 16].reshape(2, 8, 128)
                row = jnp.where(lane16 % 64 < 10, pltpu.roll(from_west, (-10 * k) % 128, 2), row)
                here = (lane16 % 64 >= 50) & (lane16 % 64 < 60)
                row = jnp.where(here, pltpu.roll(from_east, (50 - 10 * k) % 128, 2), row)
                ya[c, H + 5 * q + k] = row
        for s in range(2):
            end_copy(s, c).start()

    m1 = square[...]
    unit = only(iota((128, 128), 0) == iota((128, 128), 1))
    p01 = jnp.concatenate([unit, m1], 0)
    mp[0:256] = p01
    m2 = dot(m1, m1)
    mp[256:512] = dot(p01, m2)
    m4 = dot(m2, m2)
    mp[512:1024] = dot(mp[0:512], m4)
    m8 = dot(m4, m4)
    mp[1024:1280] = dot(p01, m8)
    mp[1280:1408] = dot(m8, m2)

    def flip(k, c):
        npow[k] = jnp.transpose(mp[pl.ds(pl.multiple_of(128 * k, 128), 128)])
        return c

    lax.fori_loop(0, SUB + 1, flip, 0)

    row2 = iota((ROWS, 128), 0)
    lane2 = iota((ROWS, 128), 1)
    tangent = lane2 < 64

    def interior(dr, dc):
        gr = row2 + (dr - H) + zy * H
        gc = lane2 % 64 + (dc - H) + zx * W
        return only((gr >= FRAME) & (gr < NY - FRAME) & (gc >= FRAME) & (gc < NX - FRAME))

    def incoming(dr, dc):
        return jnp.where(tangent, F32(1.0), interior(dr, dc))

    inside = interior(0, 0)
    outgoing = jnp.where(tangent, inside, F32(1.0))
    edge = 1.0 - inside
    for r in range(ROWS):
        cfb[5, r, 0] = jnp.broadcast_to(edge[r : r + 1], (8, 128))
    star = jnp.where(zy == 1, 0, jnp.where(zy == GY - 2, 2, 1))
    other0 = jnp.where(zy == 1, 1, 0)
    other1 = jnp.where(zy == GY - 2, 1, 2)
    corner = jnp.where(zx == 0, 2, 5)
    sub8 = iota((8, 128), 0)
    lane8 = iota((8, 128), 1)
    column8 = (lane8 % 64) // 10 + 1
    for r in range(ROWS):
        br = r // H
        middle = (sub8 >= 1) & (sub8 <= 6) & (column8 == sub8) & (star + 0 * sub8 == br)
        first = (sub8 == 0) & (column8 == corner) & (other0 + 0 * sub8 == br)
        second = (sub8 == 7) & (column8 == corner) & (other1 + 0 * sub8 == br)
        tan_slot = jnp.where((middle | first | second) & (lane8 < 60), cfb[5, r, 0], F32(0.0))
        adj_slot = only((column8 == sub8) & (lane8 >= 64) & (lane8 < 124), 0.01)
        for b in range(3):
            value = adj_slot if b == br else jnp.zeros((8, 128), F32)
            yc[r, b] = value + tan_slot if b == 0 else value

    for s in range(2):
        end_copy(s, 3).wait()
    for i in range(2):
        en[i] = jnp.zeros((48, 128), F32)
        for r in range(ROWS):
            en[i, 8 + r : 9 + r] = ya[3, r, 1, 4 + i : 5 + i]
    east = en[0, 8:38]
    west = pltpu.roll(east, 1, 1)
    north = en[1, 8:38]
    south = en[1, 7:37]
    cf[0, 0:ROWS] = outgoing * incoming(0, 0) * (1.0 - east - west - north - south)
    cf[1, 0:ROWS] = outgoing * incoming(0, 1) * east
    cf[2, 0:ROWS] = outgoing * incoming(0, -1) * west
    cf[3, 0:ROWS] = outgoing * incoming(1, 0) * north
    cf[4, 0:ROWS] = outgoing * incoming(-1, 0) * south
    for i in range(5):
        for r in range(ROWS):
            cfb[i, r, 0] = jnp.broadcast_to(cf[i, r : r + 1], (8, 128))

    for k in range(SUB):
        src, dst = (yc, yd) if k % 2 == 0 else (yd, yc)
        bs[:, k] = src[H : 2 * H, 0]
        ss[k, 8:11] = frame_sum(src, cfb)
        ss[k, 11:16] = jnp.zeros((5, 8, 128), F32)
        sweep(src, dst, cfb, k)

    def chunk(i, carry):
        c = lax.rem(i + 3, CHUNKS)

        @pl.when(i > 0)
        def _():
            for s in range(2):
                end_copy(s, c).wait()

        for k in range(SUB):
            src, dst = (ya.at[c], yb) if k % 2 == 0 else (yb, ya.at[c])
            ss[k, pl.ds(2 * c, 2)] = frame_sum(src, cfb)
            sweep(src, dst, cfb, k)
        return carry

    lax.fori_loop(0, CHUNKS, chunk, 0)

    pick_tan = only((lane8 >= 10) & (lane8 < 50) & (lane8 // 10 - 1 == sub8), 0.01)
    pick_adj = only((lane8 >= 74) & (lane8 < 114) & ((lane8 - 64) // 10 - 1 == sub8))
    sums = dot_t(pick_adj, ss[...].reshape(SUB * 128, 128))
    lanes = iota((8, SUB * 128), 1) % 128
    own_sum = dot(jnp.where(lanes < L, sums, F32(0.0)), mp[0 : SUB * 128])
    share = pltpu.roll(lanes_to_rows(sums, SUB), 64, 1)
    level_sum = jnp.sum(ya[:, H : 2 * H], axis=1).reshape(64, 128)
    slot_sum = jnp.sum(bs[...], axis=0).reshape(8 * SUB, 128)
    mean_of = dot_t(pick_tan, jnp.concatenate([level_sum, slot_sum[0:64]], 0))
    tail_of = dot_t(pick_tan, padded_rows(slot_sum[64:80], 128))
    own_mean = dot(jnp.where(lane8 < L, mean_of, F32(0.0)), npow[SUB])
    slot_mean = jnp.where(lane8 < 64, pltpu.roll(mean_of, 64, 1), pltpu.roll(tail_of, 64, 1))

    def arrive(py, total):
        b_copy(zy, py).wait_recv()
        return total + got[py]

    patch = lax.fori_loop(0, GY, arrive, jnp.zeros((5, 8, 128), F32))
    e3 = jnp.broadcast_to(patch[:, :, L : L + 1], patch.shape)
    n3 = jnp.broadcast_to(patch[:, :, L + 1 : L + 2], patch.shape)
    here = patch[1:4]
    e_here = e3[1:4]
    values = (
        here
        + e_here * (pltpu.roll(here, 7, 1) - here)
        - pltpu.roll(e_here, 1, 1) * (here - pltpu.roll(here, 1, 1))
        + n3[1:4] * (patch[2:5] - here)
        - n3[0:3] * (here - patch[0:3])
    )
    values = jnp.where(iota((3, 8, 128), 2) < L, values, F32(0.0))
    flag = zy + 0 * sub8
    main = jnp.where(flag == 1, values[0], jnp.where(flag == GY - 2, values[2], values[1]))
    side0 = jnp.where(flag == 1, values[1], values[0])
    side1 = jnp.where(flag == GY - 2, values[1], values[2])
    west_most = zx + 0 * iota((1, 128), 1) == 0
    side0 = jnp.where(west_most, side0[2:3], side0[5:6])
    side1 = jnp.where(west_most, side1[2:3], side1[5:6])
    v0 = jnp.where(sub8 == 0, side0, jnp.where(sub8 == 7, side1, main))
    forcing = jnp.where(iota((24, 128), 1) < L, pltpu.roll(here.reshape(24, 128), 64, 1), F32(0.0))
    powers = jnp.concatenate([dot(v0, npow[k]) for k in range(SUB)], 0)
    given = dot(share, padded_rows(forcing, 128))
    collected = own_sum + dot(rows_to_lanes(given, SUB), mp[0 : SUB * 128])
    averages = own_mean + dot(slot_mean, padded_rows(powers, 128))
    line = jnp.where(lane8 < 64, averages, pltpu.roll(collected, 64, 1))
    msg[...] = line[0:4]
    me = zy * GX + zx

    def c_start(i, c):
        pltpu.make_async_remote_copy(
            src_ref=msg, dst_ref=box.at[me], send_sem=c_s.at[0], recv_sem=c_r.at[0],
            device_id=(0, lax.rem(zy + i // GX, GY), lax.rem(zx + i, GX)), device_id_type=MESH,
        ).start()
        return c

    lax.fori_loop(0, GY * GX, c_start, 0)

    m10 = mp[1280:1408]
    both = npow[SUB] + pltpu.roll(m10, 64, 1)
    force = pltpu.roll(dot(forcing, m10), 64, 1)
    head = jnp.concatenate([both[0:64], force, powers[0:40]], 0)
    left_side = jnp.concatenate([jnp.transpose(head), jnp.transpose(padded_rows(powers[40:80], 128))], 1)[:, 0:168]
    for r in range(H):
        right_side = jnp.concatenate(
            [ya[:, H + r].reshape(64, 128), yc[H + r].reshape(24, 128), bs[r].reshape(80, 128)], 0
        )
        res = dot(left_side, right_side)
        out_ref[r, 0:64] = pltpu.roll(res[0:64], 118, 1)
        out_ref[r, 64:128] = pltpu.roll(res[64:128], 54, 1)
    for c in order:
        for s in range(2):
            strip_copy(s, c).wait_send()
    pltpu.make_async_remote_copy(
        src_ref=box, dst_ref=box, send_sem=c_s.at[0], recv_sem=c_r.at[0], device_id=(0, zy, zx), device_id_type=MESH
    ).wait_send()


def parent(
    py, px, up, down, left, right, barrier, b_copy, arow_ref, acol_ref, out_ref, raw_t, raw_x, square,
    cells, pc, ends, part, pad, send, g, ring_n, ring_s, ring_e, ring_w, faces_b, coarse, msg, box, boxpad,
    a_s, a_r, ring_snd, ring_rcv, c_s, c_r,
):
    r128 = iota((128, 128), 0)
    c128 = iota((128, 128), 1)
    for r in range(H):
        cells[r * W : (r + 1) * W] = jnp.transpose(jnp.concatenate([raw_t[r], raw_x[r]], 0))[0:W]
        pc[r, 0:40] = jnp.zeros((40, 128), F32)
        pc[r, 80:120] = jnp.zeros((40, 128), F32)
    mixed = dot(cells[...], jnp.transpose(square[...]) + only((r128 == c128) & (r128 >= L)))
    for r in range(H):
        pc[r, 40:80] = mixed[r * W : (r + 1) * W]
    ends[...] = jnp.zeros((2, 16, 128), F32)
    for r in range(H):
        ends[0, r : r + 1] = pc[r, 40:41]
        ends[1, r : r + 1] = pc[r, 79:80]
    start = jnp.clip(acol_ref[0] - 2 - W * px, -36, W) + 40
    for z in range(GX):
        part[z] = pc[:, pl.ds(start + 4 * z, 8)]
    g[...] = jnp.zeros(g.shape, F32)
    pl.semaphore_wait(barrier, GY + 2 + GX - 1)

    def a_copy(to, sender):
        return pltpu.make_async_remote_copy(
            src_ref=part.at[to], dst_ref=part.at[GX + sender], send_sem=a_s.at[to], recv_sem=a_r.at[sender],
            device_id=(0, py, to), device_id_type=MESH,
        )

    def a_start(k, c):
        a_copy(lax.rem(px + k, GX), px).start()
        return c

    lax.fori_loop(1, GX, a_start, 0)
    ring = []
    for s, (src, dst, where) in enumerate((
        (pc.at[H - 1, pl.ds(40, W)], ring_s, (0, up, px)),
        (pc.at[0, pl.ds(40, W)], ring_n, (0, down, px)),
        (ends.at[1], ring_w, (0, py, right)),
        (ends.at[0], ring_e, (0, py, left)),
    )):
        copy = pltpu.make_async_remote_copy(
            src_ref=src, dst_ref=dst, send_sem=ring_snd.at[s], recv_sem=ring_rcv.at[s],
            device_id=where, device_id_type=MESH,
        )
        copy.start()
        ring.append(copy)
    pad[0:5] = jnp.zeros((5, 8, 128), F32)
    pad[15:20] = jnp.zeros((5, 8, 128), F32)

    def a_arrive(k, total):
        sender = lax.rem(px + k, GX)
        a_copy(px, sender).wait_recv()
        return total + part[GX + sender]

    pad[5:15] = lax.fori_loop(1, GX, a_arrive, part[px])
    offset = arow_ref[0] - 2 - H * py + 5

    def b_start(j, c):
        zy = lax.rem(py + j, GY)
        first = jnp.clip(zy + offset, 0, 15)
        for i in range(5):
            send[zy, i] = pad[first + i]
        b_copy(zy, py).start()
        return c

    lax.fori_loop(0, GY, b_start, 0)

    for copy in ring:
        copy.wait()
    g[0, 8:48] = ring_s[...]
    g[H + 1, 8:48] = ring_n[...]
    for r in range(H):
        g[1 + r, 8:48] = pc[r, 40:80]
        g[1 + r, 7:8] = ring_w[r : r + 1]
        g[1 + r, 48:49] = ring_e[r : r + 1]
    for r in range(H):
        y = g[r + 1]
        e = jnp.broadcast_to(y[:, L : L + 1], y.shape)
        n = jnp.broadcast_to(y[:, L + 1 : L + 2], y.shape)
        s = jnp.broadcast_to(g[r][:, L + 1 : L + 2], y.shape)
        w = pltpu.roll(e, 1, 0)
        faces_b[0, r] = e
        faces_b[1, r] = w
        faces_b[2, r] = n
        faces_b[3, r] = s
        coarse[r] = (
            y + e * (pltpu.roll(y, 55, 0) - y) - w * (y - pltpu.roll(y, 1, 0)) + n * (g[r + 2] - y) - s * (y - g[r])
        )
    for i in range(16):
        boxpad[i, 0:BOX0] = jnp.zeros((BOX0, 128), F32)
        boxpad[i, BOX0 + 32 : 144] = jnp.zeros((56, 128), F32)
    down_mix = pltpu.roll(jnp.concatenate([jnp.zeros((64, 128), F32), square[0:64]], 0), 64, 1)
    row0 = py * H - 1 - arow_ref[0]
    col0 = px * W - 8 - acol_ref[0]
    sub = iota((56, 128), 0)
    lane = iota((56, 128), 1)
    in_cols = (sub + col0 >= 0) & (sub + col0 < 32)
    first = jnp.clip(col0 + BOX0, 0, 88)

    def a_sent(k, c):
        a_copy(lax.rem(px + k, GX), px).wait_send()
        return c

    lax.fori_loop(1, GX, a_sent, 0)

    def b_sent(zy, c):
        b_copy(zy, py).wait_send()
        return c

    lax.fori_loop(0, GY, b_sent, 0)

    pltpu.make_async_remote_copy(
        src_ref=box, dst_ref=box, send_sem=c_s.at[0], recv_sem=c_r.at[0], device_id=(1, py, px), device_id_type=MESH
    ).wait_recv()
    for i in range(16):
        for z in range(GX):
            boxpad[i, BOX0 + 4 * z : BOX0 + 4 + 4 * z] = box[GX * i + z]
    windows = []
    for i in range(H + 2):
        br = row0 + i
        within = in_cols & (br + 0 * sub >= 0) & (br + 0 * sub < 16)
        window = boxpad[jnp.clip(br, 0, 15), pl.ds(first, 56)]
        w = jnp.where(within, window, g[i])
        g[i] = w
        if 1 <= i <= H:
            coarse[i - 1] = jnp.where(within, window, coarse[i - 1])
    y_all = dot(g[...].reshape((H + 2) * 56, 128), down_mix).reshape(H + 2, 56, 128)
    for r in range(H):
        y = y_all[r + 1]
        res = (
            y
            + faces_b[0, r] * (pltpu.roll(y, 55, 0) - y)
            - faces_b[1, r] * (y - pltpu.roll(y, 1, 0))
            + faces_b[2, r] * (y_all[r + 2] - y)
            - faces_b[3, r] * (y - y_all[r])
        )
        res = jnp.where(lane < 64, coarse[r], res)
        out_ref[r] = jnp.transpose(padded_rows(res[8:48], 128))


def shards(state_in, cotangent, faces, mixing, anchor_row, anchor_col):
    dma = pltpu.SemaphoreType.DMA
    smem = pl.BlockSpec(memory_space=pltpu.SMEM)
    hbm = pl.BlockSpec(memory_space=pl.ANY)
    out = pl.pallas_call(
        kernel,
        name="step",
        out_shape=jax.ShapeDtypeStruct((H, 128, 128), F32),
        in_specs=[smem, smem, hbm, hbm, hbm, hbm],
        out_specs=pl.BlockSpec(memory_space=VMEM),
        scratch_shapes=[
            VMEM((1, L, H, W), F32),
            VMEM((1, L, H, W), F32),
            VMEM((1, 2, H, W), F32),
            VMEM((1, L, L), F32),
            dma((4,)),
            VMEM((H, 64, 128), F32),
            VMEM((H, 64, 128), F32),
            VMEM((128, 128), F32),
            VMEM((CHUNKS, ROWS, 2, 8, 128), F32),
            VMEM((ROWS, 2, 8, 128), F32),
            VMEM((ROWS, 3, 8, 128), F32),
            VMEM((ROWS, 3, 8, 128), F32),
            VMEM((5, 32, 128), F32),
            VMEM((6, ROWS, 1, 8, 128), F32),
            VMEM((2, 48, 128), F32),
            VMEM((H, SUB, 8, 128), F32),
            VMEM((SUB, 16, 8, 128), F32),
            VMEM((11 * 128, 128), F32),
            VMEM((11, 128, 128), F32),
            VMEM((2, CHUNKS, 2, 2, 8, 128), F32),
            VMEM((2, CHUNKS, 2, 2, 8, 128), F32),
            VMEM((GY, 5, 8, 128), F32),
            VMEM((4, 128), F32),
            VMEM((H * W, 128), F32),
            VMEM((H, 120, 128), F32),
            VMEM((2, 16, 128), F32),
            VMEM((2 * GX, H, 8, 128), F32),
            VMEM((20, 8, 128), F32),
            VMEM((GY, 5, 8, 128), F32),
            VMEM((H + 2, 56, 128), F32),
            VMEM((W, 128), F32),
            VMEM((W, 128), F32),
            VMEM((16, 128), F32),
            VMEM((16, 128), F32),
            VMEM((4, H, 56, 128), F32),
            VMEM((H, 56, 128), F32),
            VMEM((GY * GX, 4, 128), F32),
            VMEM((16, 144, 128), F32),
            dma((2, CHUNKS)), dma((2, CHUNKS)), dma((2, CHUNKS)), dma((2, CHUNKS)),
            dma((GX,)), dma((GX,)), dma((4,)), dma((4,)), dma((GY,)), dma((GY,)), dma((1,)), dma((1,)),
        ],
        compiler_params=pltpu.CompilerParams(collective_id=0, has_side_effects=True, vmem_limit_bytes=40 * 2**20),
    )(anchor_row, anchor_col, state_in, cotangent, faces, mixing)
    tangent = out[:, 0:L, 0:W].transpose(1, 0, 2)
    adjoint = out[:, 64 : 64 + L, 0:W].transpose(1, 0, 2)
    return tangent[None], adjoint[None]


def solution(mesh):
    placed = (
        P("grp", None, "gy", "gx"),
        P("grp", None, "gy", "gx"),
        P("grp", None, "gy", "gx"),
        P("grp", None, None),
        P(),
        P(),
    )
    return jax.shard_map(
        shards,
        mesh=mesh,
        in_specs=placed,
        out_specs=(P("grp", None, "gy", "gx"), P("grp", None, "gy", "gx")),
        check_vma=False,
    )
```

```python
import jax
import jax.numpy as jnp
from jax import lax
from jax.experimental import pallas as pl
from jax.experimental.pallas import tpu as pltpu
from jax.sharding import PartitionSpec as P

MESH = pl.DeviceIdType.MESH
HIGHEST = lax.Precision.HIGHEST
F32 = jnp.float32
VMEM = pltpu.VMEM
L = 60
H = 10
W = 40
NY = 160
NX = 320
GY = 16
GX = 8
FRAME = 2
SUB = 10
CHUNKS = 4
ROWS = 3 * H
BLOCK = 6
BOX0 = 56


def dot(a, b):
    return lax.dot_general(a, b, (((1,), (0,)), ((), ())), precision=HIGHEST, preferred_element_type=F32)


def dot_t(a, b):
    return lax.dot_general(a, b, (((1,), (1,)), ((), ())), precision=HIGHEST, preferred_element_type=F32)


def iota(shape, dim):
    return lax.broadcasted_iota(jnp.int32, shape, dim)


def only(keep, value=1.0):
    return jnp.where(keep, F32(value), F32(0.0))


def padded_rows(a, rows):
    return jnp.concatenate([a, jnp.zeros((rows - a.shape[0], a.shape[1]), F32)], 0)


def lanes_to_rows(a, count):
    return jnp.concatenate([a[:, 128 * k : 128 * k + 128] for k in range(count)], 0)


def rows_to_lanes(a, count):
    return jnp.concatenate([a[8 * k : 8 * k + 8] for k in range(count)], 1)


def kernel(
    arow_ref, acol_ref, state_hbm, cot_hbm, faces_hbm, mix_hbm,
    out_ref,
    state, cot, faces, mixing, load_s, raw, mixed_rows, wide, square,
    ya, yb, yc, yd, cf, cfb, en, bs, ss, power, strip_out, strip_in, got, msg,
    cells, pc, ends, part, pad, send, g, ring_n, ring_s, ring_e, ring_w, faces_b, coarse, box, boxpad,
    strip_s, strip_r, ns_s, ns_r, a_s, a_r, ring_snd, ring_rcv, b_s, b_r, c_s, c_r,
):
    grp = lax.axis_index("grp")
    gy = lax.axis_index("gy")
    gx = lax.axis_index("gx")
    up = lax.rem(gy + 1, GY)
    down = lax.rem(gy + GY - 1, GY)
    right = lax.rem(gx + 1, GX)
    left = lax.rem(gx + GX - 1, GX)
    loads = [
        pltpu.make_async_copy(src, dst, load_s.at[i])
        for i, (src, dst) in enumerate(((state_hbm, state), (cot_hbm, cot), (faces_hbm, faces), (mix_hbm, mixing)))
    ]
    for copy in loads:
        copy.start()
    barrier = pltpu.get_barrier_semaphore()

    def hello(*where):
        pl.semaphore_signal(barrier, inc=1, device_id=where, device_id_type=MESH)

    def cross(j, c):
        hello(1 - grp, lax.rem(gy + j, GY), gx)
        return c

    hello(grp, up, gx)
    hello(grp, down, gx)

    @pl.when(grp == 1)
    def _():
        hello(grp, gy, left)
        hello(grp, gy, right)

    @pl.when(grp == 0)
    def _():
        def peer(k, c):
            hello(grp, gy, lax.rem(gx + k, GX))
            return c

        lax.fori_loop(1, GX, peer, 0)

    lax.fori_loop(0, GY, cross, 0)

    square[...] = jnp.zeros((128, 128), F32)
    wide[...] = jnp.zeros(wide.shape, F32)

    @pl.when(grp == 1)
    def _():
        mixed_rows[...] = jnp.zeros(mixed_rows.shape, F32)

    for copy in loads:
        copy.wait()
    diagonal = iota((1, L), 1)
    for i in range(L):
        square[i : i + 1, 0:L] = mixing[i] + only(diagonal == i, 0.75)
    col = gx * W + iota((H, 2, W), 2)
    row = gy * H + iota((H, 2, W), 0)
    kind = iota((H, 2, W), 1)
    closed = ((kind == 0) & (col == NX - 1)) | ((kind == 1) & (row == NY - 1))
    wide[:, :, 0:W] = jnp.where(closed, F32(0.0), faces[...])

    def b_copy(zy, py):
        return pltpu.make_async_remote_copy(
            src_ref=send.at[zy], dst_ref=got.at[py], send_sem=b_s.at[zy], recv_sem=b_r.at[py],
            device_id=(1, zy, gx), device_id_type=MESH,
        )

    @pl.when(grp == 1)
    def _():
        zoom(
            gy, gx, up, down, left, right, barrier, b_copy, out_ref, state, cot, wide, mixed_rows, raw, square,
            ya, yb, yc, yd, cf, cfb, en, bs, ss, power, strip_out, strip_in, got, msg, box,
            strip_s, strip_r, ns_s, ns_r, c_s, c_r,
        )

    @pl.when(grp == 0)
    def _():
        parent(
            gy, gx, up, down, left, right, barrier, b_copy, arow_ref, acol_ref, out_ref, state, cot, wide, square,
            cells, pc, ends, part, pad, send, g, ring_n, ring_s, ring_e, ring_w, faces_b, coarse, msg, box, boxpad,
            a_s, a_r, ring_snd, ring_rcv, c_s, c_r,
        )


def sweep(src, dst, cfb, k):
    low, high = k + 1, ROWS - 1 - k
    while low < high:
        n = min(BLOCK, high - low)
        line = src[low : low + n]
        dst[low : low + n] = (
            cfb[0, low : low + n] * line
            + cfb[1, low : low + n] * pltpu.roll(line, 127, 3)
            + cfb[2, low : low + n] * pltpu.roll(line, 1, 3)
            + cfb[3, low : low + n] * src[low + 1 : low + n + 1]
            + cfb[4, low : low + n] * src[low - 1 : low + n - 1]
        )
        low += n


def frame_sum(src, cfb):
    return jnp.sum(cfb[5, H : 2 * H] * src[H : 2 * H], axis=0)


def zoom(
    zy, zx, up, down, left, right, barrier, b_copy, out_ref, state, cot, wide, mixed_rows, raw, square,
    ya, yb, yc, yd, cf, cfb, en, bs, ss, power, strip_out, strip_in, got, msg, box,
    strip_s, strip_r, ns_s, ns_r, c_s, c_r,
):
    lane = iota((64, 128), 1)
    lane64 = lane % 64
    for q in range(H // 2):
        for i in range(2):
            mixed_rows[q, 10:50, 64 * i : 64 * i + L] = state[2 * q + i]
            mixed_rows[q, 74:114, 64 * i : 64 * i + L] = cot[2 * q + i]
        turned = jnp.transpose(mixed_rows[q])
        for i in range(2):
            face = wide[2 * q + i]
            raw[2 * q + i] = turned[64 * i : 64 * i + 64]
            raw[2 * q + i, L : L + 2] = pltpu.roll(face, 10, 1) + pltpu.roll(face, 74, 1)
    for q in range(2):
        east = jnp.zeros((64, 128), F32)
        west = jnp.zeros((64, 128), F32)
        for k in range(5):
            row = raw[5 * q + k]
            here = (lane64 >= 10 * k) & (lane64 < 10 * k + 10)
            east = jnp.where(here, pltpu.roll(row, (10 * k - 40) % 128, 1), east)
            west = jnp.where(here, pltpu.roll(row, (10 * k - 10) % 128, 1), west)
        strip_out[0, :, q] = east.reshape(CHUNKS, 2, 8, 128)
        strip_out[1, :, q] = west.reshape(CHUNKS, 2, 8, 128)
    pl.semaphore_wait(barrier, GY + 4)

    def strip_copy(s, c):
        return pltpu.make_async_remote_copy(
            src_ref=strip_out.at[s, c], dst_ref=strip_in.at[s, c], send_sem=strip_s.at[s, c], recv_sem=strip_r.at[s, c],
            device_id=(1, zy, (right, left)[s]), device_id_type=MESH,
        )

    def end_copy(s, c):
        return pltpu.make_async_remote_copy(
            src_ref=ya.at[c, pl.ds(H, H)], dst_ref=ya.at[c, pl.ds(2 * H * s, H)],
            send_sem=ns_s.at[s, c], recv_sem=ns_r.at[s, c],
            device_id=(1, (up, down)[s], zx), device_id_type=MESH,
        )

    order = (3, 0, 1, 2)
    for c in order:
        for s in range(2):
            strip_copy(s, c).start()
    lane16 = iota((2, 8, 128), 2)
    for c in order:
        for s in range(2):
            strip_copy(s, c).wait_recv()
        for q in range(2):
            from_west = strip_in[0, c, q]
            from_east = strip_in[1, c, q]
            for k in range(5):
                row = raw[5 * q + k, 16 * c : 16 * c + 16].reshape(2, 8, 128)
                row = jnp.where(lane16 % 64 < 10, pltpu.roll(from_west, (-10 * k) % 128, 2), row)
                here = (lane16 % 64 >= 50) & (lane16 % 64 < 60)
                row = jnp.where(here, pltpu.roll(from_east, (50 - 10 * k) % 128, 2), row)
                ya[c, H + 5 * q + k] = row
        for s in range(2):
            end_copy(s, c).start()

    b1 = jnp.transpose(square[...]) + pltpu.roll(jnp.concatenate([jnp.zeros((64, 128), F32), square[0:64]], 0), 64, 1)
    b2 = dot(b1, b1)
    b4 = dot(b2, b2)
    b8 = dot(b4, b4)
    for i, value in enumerate((b1, b2, b4, b8, dot(b8, b2))):
        power[i] = value

    row2 = iota((ROWS, 128), 0)
    lane2 = iota((ROWS, 128), 1)
    tangent = lane2 < 64

    def interior(dr, dc):
        gr = row2 + (dr - H) + zy * H
        gc = lane2 % 64 + (dc - H) + zx * W
        return only((gr >= FRAME) & (gr < NY - FRAME) & (gc >= FRAME) & (gc < NX - FRAME))

    def incoming(dr, dc):
        return jnp.where(tangent, F32(1.0), interior(dr, dc))

    inside = interior(0, 0)
    outgoing = jnp.where(tangent, inside, F32(1.0))
    edge = 1.0 - inside
    for r in range(ROWS):
        cfb[5, r, 0] = jnp.broadcast_to(edge[r : r + 1], (8, 128))
    star = jnp.where(zy == 1, 0, jnp.where(zy == GY - 2, 2, 1))
    other0 = jnp.where(zy == 1, 1, 0)
    other1 = jnp.where(zy == GY - 2, 1, 2)
    corner = jnp.where(zx == 0, 2, 5)
    sub8 = iota((8, 128), 0)
    lane8 = iota((8, 128), 1)
    column8 = (lane8 % 64) // 10 + 1
    for r in range(ROWS):
        br = r // H
        middle = (sub8 >= 1) & (sub8 <= 6) & (column8 == sub8) & (star + 0 * sub8 == br)
        first = (sub8 == 0) & (column8 == corner) & (other0 + 0 * sub8 == br)
        second = (sub8 == 7) & (column8 == corner) & (other1 + 0 * sub8 == br)
        tan_slot = jnp.where((middle | first | second) & (lane8 < 60), cfb[5, r, 0], F32(0.0))
        adj_slot = only((column8 == sub8) & (lane8 >= 64) & (lane8 < 124), 0.01)
        for b in range(3):
            value = adj_slot if b == br else jnp.zeros((8, 128), F32)
            yc[r, b] = value + tan_slot if b == 0 else value

    for s in range(2):
        end_copy(s, 3).wait()
    for i in range(2):
        en[i] = jnp.zeros((48, 128), F32)
        for r in range(ROWS):
            en[i, 8 + r : 9 + r] = ya[3, r, 1, 4 + i : 5 + i]
    east = en[0, 8:38]
    west = pltpu.roll(east, 1, 1)
    north = en[1, 8:38]
    south = en[1, 7:37]
    cf[0, 0:ROWS] = outgoing * incoming(0, 0) * (1.0 - east - west - north - south)
    cf[1, 0:ROWS] = outgoing * incoming(0, 1) * east
    cf[2, 0:ROWS] = outgoing * incoming(0, -1) * west
    cf[3, 0:ROWS] = outgoing * incoming(1, 0) * north
    cf[4, 0:ROWS] = outgoing * incoming(-1, 0) * south
    for i in range(5):
        for r in range(ROWS):
            cfb[i, r, 0] = jnp.broadcast_to(cf[i, r : r + 1], (8, 128))

    for k in range(SUB):
        src, dst = (yc, yd) if k % 2 == 0 else (yd, yc)
        bs[:, k] = src[H : 2 * H, 0]
        ss[k, 8:11] = frame_sum(src, cfb)
        ss[k, 11:16] = jnp.zeros((5, 8, 128), F32)
        sweep(src, dst, cfb, k)

    def chunk(i, carry):
        c = lax.rem(i + 3, CHUNKS)

        @pl.when(i > 0)
        def _():
            for s in range(2):
                end_copy(s, c).wait()

        for k in range(SUB):
            src, dst = (ya.at[c], yb) if k % 2 == 0 else (yb, ya.at[c])
            ss[k, pl.ds(2 * c, 2)] = frame_sum(src, cfb)
            sweep(src, dst, cfb, k)
        return carry

    lax.fori_loop(0, CHUNKS, chunk, 0)

    pick_tan = only((lane8 >= 10) & (lane8 < 50) & (lane8 // 10 - 1 == sub8), 0.01)
    pick_adj = only((lane8 >= 74) & (lane8 < 114) & ((lane8 - 64) // 10 - 1 == sub8))
    sums = dot_t(pick_adj, ss[...].reshape(SUB * 128, 128))
    sums = lanes_to_rows(sums, SUB)
    lane80 = iota((8 * SUB, 128), 1)
    level_sum = jnp.sum(ya[:, H : 2 * H], axis=1).reshape(64, 128)
    slot_sum = jnp.sum(bs[...], axis=0).reshape(8 * SUB, 128)
    means = dot_t(pick_tan, jnp.concatenate([slot_sum, jnp.zeros((48, 128), F32)], 0))
    means = jnp.concatenate([pltpu.roll(means, (-8 * k) % 128, 1) for k in range(SUB)], 0)
    weights = jnp.where(lane80 < 32, jnp.where(lane80 < 8, means, pltpu.roll(sums, 72, 1)), F32(0.0))
    own_sums = pltpu.roll(jnp.where(lane80 < L, sums, F32(0.0)), 64, 1)
    own_mean = dot_t(pick_tan, padded_rows(level_sum, 128))
    own_mean = jnp.where(lane8 < L, own_mean, F32(0.0))

    def arrive(py, total):
        b_copy(zy, py).wait_recv()
        return total + got[py]

    patch = lax.fori_loop(0, GY, arrive, jnp.zeros((5, 8, 128), F32))
    e3 = jnp.broadcast_to(patch[:, :, L : L + 1], patch.shape)
    n3 = jnp.broadcast_to(patch[:, :, L + 1 : L + 2], patch.shape)
    here = patch[1:4]
    e_here = e3[1:4]
    values = (
        here
        + e_here * (pltpu.roll(here, 7, 1) - here)
        - pltpu.roll(e_here, 1, 1) * (here - pltpu.roll(here, 1, 1))
        + n3[1:4] * (patch[2:5] - here)
        - n3[0:3] * (here - patch[0:3])
    )
    values = jnp.where(iota((3, 8, 128), 2) < L, values, F32(0.0))
    flag = zy + 0 * sub8
    main = jnp.where(flag == 1, values[0], jnp.where(flag == GY - 2, values[2], values[1]))
    side0 = jnp.where(flag == 1, values[1], values[0])
    side1 = jnp.where(flag == GY - 2, values[1], values[2])
    west_most = zx + 0 * iota((1, 128), 1) == 0
    side0 = jnp.where(west_most, side0[2:3], side0[5:6])
    side1 = jnp.where(west_most, side1[2:3], side1[5:6])
    v0 = jnp.where(sub8 == 0, side0, jnp.where(sub8 == 7, side1, main))
    forcing = jnp.where(iota((24, 128), 1) >= 64, here.reshape(24, 128), F32(0.0))
    u = dot(weights, padded_rows(jnp.concatenate([v0, forcing], 0), 128)) + own_sums
    u = [u[8 * k : 8 * k + 8] for k in range(SUB)] + [own_mean]
    p = dot(jnp.concatenate(u[1::2], 0), power[0])
    p = [u[2 * i] + p[8 * i : 8 * i + 8] for i in range(5)] + [own_mean]
    q = dot(jnp.concatenate(p[1::2], 0), power[1])
    q = [p[2 * i] + q[8 * i : 8 * i + 8] for i in range(3)]
    line = q[0] + dot(q[1], power[2]) + dot(q[2], power[3])
    msg[...] = line[0:4]
    me = zy * GX + zx

    def c_start(i, c):
        pltpu.make_async_remote_copy(
            src_ref=msg, dst_ref=box.at[me], send_sem=c_s.at[0], recv_sem=c_r.at[0],
            device_id=(0, lax.rem(zy + i // GX, GY), lax.rem(zx + i, GX)), device_id_type=MESH,
        ).start()
        return c

    lax.fori_loop(0, GY * GX, c_start, 0, unroll=8)

    powers = jnp.concatenate([v0, dot(v0, power[0])], 0)
    last = dot(powers, power[3])
    powers = jnp.concatenate([powers, dot(powers, power[1])], 0)
    powers = jnp.concatenate([powers, dot(powers, power[2]), last], 0)
    both = power[4, 0:64] + power[4, 64:128]
    force = dot(forcing, power[4])
    head = jnp.concatenate([both, force, powers[0:40]], 0)
    left_side = jnp.concatenate([jnp.transpose(head), jnp.transpose(padded_rows(powers[40:80], 128))], 1)[:, 0:168]
    for r in range(H):
        right_side = jnp.concatenate(
            [ya[:, H + r].reshape(64, 128), yc[H + r].reshape(24, 128), bs[r].reshape(80, 128)], 0
        )
        res = dot(left_side, right_side)
        res = jnp.transpose(res)
        out_ref[r] = jnp.where(iota((W, 128), 1) < 64, res[10:50], res[74:114])
    for c in order:
        for s in range(2):
            strip_copy(s, c).wait_send()
    pltpu.make_async_remote_copy(
        src_ref=box, dst_ref=box, send_sem=c_s.at[0], recv_sem=c_r.at[0], device_id=(0, zy, zx), device_id_type=MESH
    ).wait_send()


def parent(
    py, px, up, down, left, right, barrier, b_copy, arow_ref, acol_ref, out_ref, state, cot, wide, square,
    cells, pc, ends, part, pad, send, g, ring_n, ring_s, ring_e, ring_w, faces_b, coarse, msg, box, boxpad,
    a_s, a_r, ring_snd, ring_rcv, c_s, c_r,
):
    r128 = iota((128, 128), 0)
    c128 = iota((128, 128), 1)
    turned = jnp.transpose(jnp.concatenate([wide[...].reshape(2 * H, 128), jnp.zeros((128 - 2 * H, 128), F32)], 0))[0:W]
    lane40 = iota((W, 128), 1)
    for r in range(H):
        cells[r * W : (r + 1) * W] = jnp.where((lane40 >= L) & (lane40 < L + 2), pltpu.roll(turned, L - 2 * r, 1), F32(0.0))
        cells[r * W : (r + 1) * W, 0:L] = state[r]
        cells[r * W : (r + 1) * W, 64 : 64 + L] = cot[r]
        pc[r, 0:40] = jnp.zeros((40, 128), F32)
        pc[r, 80:120] = jnp.zeros((40, 128), F32)
    mixed = dot(cells[...], jnp.transpose(square[...]) + only((r128 == c128) & (r128 >= L)))
    for r in range(H):
        pc[r, 40:80] = mixed[r * W : (r + 1) * W]
    ends[...] = jnp.zeros((2, 16, 128), F32)
    for r in range(H):
        ends[0, r : r + 1] = pc[r, 40:41]
        ends[1, r : r + 1] = pc[r, 79:80]
    start = jnp.clip(acol_ref[0] - 2 - W * px, -36, W) + 40
    for z in range(GX):
        part[z] = pc[:, pl.ds(start + 4 * z, 8)]
    g[...] = jnp.zeros(g.shape, F32)
    pl.semaphore_wait(barrier, GY + 2 + GX - 1)

    def a_copy(to, sender):
        return pltpu.make_async_remote_copy(
            src_ref=part.at[to], dst_ref=part.at[GX + sender], send_sem=a_s.at[to], recv_sem=a_r.at[sender],
            device_id=(0, py, to), device_id_type=MESH,
        )

    def a_start(k, c):
        a_copy(lax.rem(px + k, GX), px).start()
        return c

    lax.fori_loop(1, GX, a_start, 0)
    ring = []
    for s, (src, dst, where) in enumerate((
        (pc.at[H - 1, pl.ds(40, W)], ring_s, (0, up, px)),
        (pc.at[0, pl.ds(40, W)], ring_n, (0, down, px)),
        (ends.at[1], ring_w, (0, py, right)),
        (ends.at[0], ring_e, (0, py, left)),
    )):
        copy = pltpu.make_async_remote_copy(
            src_ref=src, dst_ref=dst, send_sem=ring_snd.at[s], recv_sem=ring_rcv.at[s],
            device_id=where, device_id_type=MESH,
        )
        copy.start()
        ring.append(copy)
    pad[0:5] = jnp.zeros((5, 8, 128), F32)
    pad[15:20] = jnp.zeros((5, 8, 128), F32)

    def a_arrive(k, total):
        sender = lax.rem(px + k, GX)
        a_copy(px, sender).wait_recv()
        return total + part[GX + sender]

    pad[5:15] = lax.fori_loop(1, GX, a_arrive, part[px])
    offset = arow_ref[0] - 2 - H * py + 5

    def b_start(j, c):
        zy = lax.rem(py + j, GY)
        first = jnp.clip(zy + offset, 0, 15)
        for i in range(5):
            send[zy, i] = pad[first + i]
        b_copy(zy, py).start()
        return c

    lax.fori_loop(0, GY, b_start, 0)

    for copy in ring:
        copy.wait()
    g[0, 8:48] = ring_s[...]
    g[H + 1, 8:48] = ring_n[...]
    for r in range(H):
        g[1 + r, 8:48] = pc[r, 40:80]
        g[1 + r, 7:8] = ring_w[r : r + 1]
        g[1 + r, 48:49] = ring_e[r : r + 1]
    for r in range(H):
        y = g[r + 1]
        e = jnp.broadcast_to(y[:, L : L + 1], y.shape)
        n = jnp.broadcast_to(y[:, L + 1 : L + 2], y.shape)
        s = jnp.broadcast_to(g[r][:, L + 1 : L + 2], y.shape)
        w = pltpu.roll(e, 1, 0)
        faces_b[0, r] = e
        faces_b[1, r] = w
        faces_b[2, r] = n
        faces_b[3, r] = s
        coarse[r] = (
            y + e * (pltpu.roll(y, 55, 0) - y) - w * (y - pltpu.roll(y, 1, 0)) + n * (g[r + 2] - y) - s * (y - g[r])
        )
    for i in range(16):
        boxpad[i, 0:BOX0] = jnp.zeros((BOX0, 128), F32)
        boxpad[i, BOX0 + 32 : 144] = jnp.zeros((56, 128), F32)
    down_mix = pltpu.roll(jnp.concatenate([jnp.zeros((64, 128), F32), square[0:64]], 0), 64, 1)
    row0 = py * H - 1 - arow_ref[0]
    col0 = px * W - 8 - acol_ref[0]
    sub = iota((56, 128), 0)
    lane = iota((56, 128), 1)
    in_cols = (sub + col0 >= 0) & (sub + col0 < 32)
    first = jnp.clip(col0 + BOX0, 0, 88)

    def a_sent(k, c):
        a_copy(lax.rem(px + k, GX), px).wait_send()
        return c

    lax.fori_loop(1, GX, a_sent, 0)

    def b_sent(zy, c):
        b_copy(zy, py).wait_send()
        return c

    lax.fori_loop(0, GY, b_sent, 0)

    pltpu.make_async_remote_copy(
        src_ref=box, dst_ref=box, send_sem=c_s.at[0], recv_sem=c_r.at[0], device_id=(1, py, px), device_id_type=MESH
    ).wait_recv()
    for i in range(16):
        for z in range(GX):
            boxpad[i, BOX0 + 4 * z : BOX0 + 4 + 4 * z] = box[GX * i + z]
    windows = []
    for i in range(H + 2):
        br = row0 + i
        within = in_cols & (br + 0 * sub >= 0) & (br + 0 * sub < 16)
        window = boxpad[jnp.clip(br, 0, 15), pl.ds(first, 56)]
        w = jnp.where(within, window, g[i])
        g[i] = w
        if 1 <= i <= H:
            coarse[i - 1] = jnp.where(within, window, coarse[i - 1])
    y_all = dot(g[...].reshape((H + 2) * 56, 128), down_mix).reshape(H + 2, 56, 128)
    for r in range(H):
        y = y_all[r + 1]
        res = (
            y
            + faces_b[0, r] * (pltpu.roll(y, 55, 0) - y)
            - faces_b[1, r] * (y - pltpu.roll(y, 1, 0))
            + faces_b[2, r] * (y_all[r + 2] - y)
            - faces_b[3, r] * (y - y_all[r])
        )
        res = jnp.where(lane < 64, coarse[r], res)
        out_ref[r] = res[8:48]


def shards(state_in, cotangent, faces, mixing, anchor_row, anchor_col):
    dma = pltpu.SemaphoreType.DMA
    smem = pl.BlockSpec(memory_space=pltpu.SMEM)
    hbm = pl.BlockSpec(memory_space=pltpu.HBM)
    out = pl.pallas_call(
        kernel,
        name="step",
        out_shape=jax.ShapeDtypeStruct((H, W, 128), F32),
        in_specs=[smem, smem, hbm, hbm, hbm, hbm],
        out_specs=pl.BlockSpec(memory_space=VMEM),
        scratch_shapes=[
            VMEM((H, W, L), F32),
            VMEM((H, W, L), F32),
            VMEM((H, 2, W), F32),
            VMEM((L, 1, L), F32),
            dma((4,)),
            VMEM((H, 64, 128), F32),
            VMEM((H // 2, 128, 128), F32),
            VMEM((H, 2, 128), F32),
            VMEM((128, 128), F32),
            VMEM((CHUNKS, ROWS, 2, 8, 128), F32),
            VMEM((ROWS, 2, 8, 128), F32),
            VMEM((ROWS, 3, 8, 128), F32),
            VMEM((ROWS, 3, 8, 128), F32),
            VMEM((5, 32, 128), F32),
            VMEM((6, ROWS, 1, 8, 128), F32),
            VMEM((2, 48, 128), F32),
            VMEM((H, SUB, 8, 128), F32),
            VMEM((SUB, 16, 8, 128), F32),
            VMEM((5, 128, 128), F32),
            VMEM((2, CHUNKS, 2, 2, 8, 128), F32),
            VMEM((2, CHUNKS, 2, 2, 8, 128), F32),
            VMEM((GY, 5, 8, 128), F32),
            VMEM((4, 128), F32),
            VMEM((H * W, 128), F32),
            VMEM((H, 120, 128), F32),
            VMEM((2, 16, 128), F32),
            VMEM((2 * GX, H, 8, 128), F32),
            VMEM((20, 8, 128), F32),
            VMEM((GY, 5, 8, 128), F32),
            VMEM((H + 2, 56, 128), F32),
            VMEM((W, 128), F32),
            VMEM((W, 128), F32),
            VMEM((16, 128), F32),
            VMEM((16, 128), F32),
            VMEM((4, H, 56, 128), F32),
            VMEM((H, 56, 128), F32),
            VMEM((GY * GX, 4, 128), F32),
            VMEM((16, 144, 128), F32),
            dma((2, CHUNKS)), dma((2, CHUNKS)), dma((2, CHUNKS)), dma((2, CHUNKS)),
            dma((GX,)), dma((GX,)), dma((4,)), dma((4,)), dma((GY,)), dma((GY,)), dma((1,)), dma((1,)),
        ],
        compiler_params=pltpu.CompilerParams(collective_id=0, has_side_effects=True, vmem_limit_bytes=56291328),
    )(
        anchor_row, anchor_col, state_in[0].transpose(1, 2, 0), cotangent[0].transpose(1, 2, 0),
        faces[0].transpose(1, 0, 2), mixing.transpose(1, 0, 2),
    )
    both = (out[:, :, 0:L], out[:, :, 64 : 64 + L])
    return tuple(half.transpose(2, 0, 1)[None] for half in both)


def solution(mesh):
    placed = (
        P("grp", None, "gy", "gx"),
        P("grp", None, "gy", "gx"),
        P("grp", None, "gy", "gx"),
        P("grp", None, None),
        P(),
        P(),
    )
    return jax.shard_map(
        shards,
        mesh=mesh,
        in_specs=placed,
        out_specs=(P("grp", None, "gy", "gx"), P("grp", None, "gy", "gx")),
        check_vma=False,
    )
```

```python
import jax
import jax.numpy as jnp
from jax import lax
from jax.experimental import pallas as pl
from jax.experimental.pallas import tpu as pltpu
from jax.sharding import PartitionSpec as P

MESH = pl.DeviceIdType.MESH
HIGHEST = lax.Precision.HIGHEST
F32 = jnp.float32
VMEM = pltpu.VMEM
L = 60
H = 10
W = 40
NY = 160
NX = 320
GY = 16
GX = 8
FRAME = 2
SUB = 10
CHUNKS = 4
ROWS = 3 * H
BLOCK = 6
BOX0 = 56


def dot(a, b):
    return lax.dot_general(a, b, (((1,), (0,)), ((), ())), precision=HIGHEST, preferred_element_type=F32)


def dot_t(a, b):
    return lax.dot_general(a, b, (((1,), (1,)), ((), ())), precision=HIGHEST, preferred_element_type=F32)


def iota(shape, dim):
    return lax.broadcasted_iota(jnp.int32, shape, dim)


def only(keep, value=1.0):
    return jnp.where(keep, F32(value), F32(0.0))


def padded_rows(a, rows):
    return jnp.concatenate([a, jnp.zeros((rows - a.shape[0], a.shape[1]), F32)], 0)


def lanes_to_rows(a, count):
    return jnp.concatenate([a[:, 128 * k : 128 * k + 128] for k in range(count)], 0)


def rows_to_lanes(a, count):
    return jnp.concatenate([a[8 * k : 8 * k + 8] for k in range(count)], 1)


def kernel(
    arow_ref, acol_ref, state_hbm, cot_hbm, faces_hbm, mix_hbm,
    out_ref,
    state, cot, faces, mixing, load_s, raw, mixed_rows, wide, square,
    ya, yb, yc, yd, cf, cfb, en, bs, ss, power, strip_out, strip_in, got, msg,
    cells, rows, ends, row_out, row_in, row_pad, window_out, g, ring_n, ring_s, ring_e, ring_w, faces_b, coarse, box, boxpad,
    strip_s, strip_r, ns_s, ns_r, a_s, a_r, ring_snd, ring_rcv, b_s, b_r, c_s, c_r,
):
    grp = lax.axis_index("grp")
    gy = lax.axis_index("gy")
    gx = lax.axis_index("gx")
    up = lax.rem(gy + 1, GY)
    down = lax.rem(gy + GY - 1, GY)
    right = lax.rem(gx + 1, GX)
    left = lax.rem(gx + GX - 1, GX)
    loads = [
        pltpu.make_async_copy(src, dst, load_s.at[i])
        for i, (src, dst) in enumerate(((state_hbm, state), (cot_hbm, cot), (faces_hbm, faces), (mix_hbm, mixing)))
    ]
    for copy in loads:
        copy.start()
    barrier = pltpu.get_barrier_semaphore()

    def hello(*where):
        pl.semaphore_signal(barrier, inc=1, device_id=where, device_id_type=MESH)

    hello(grp, gy, left)
    hello(grp, gy, right)

    @pl.when(grp == 1)
    def _():
        hello(grp, up, gx)
        hello(grp, down, gx)

        def cross(j, c):
            hello(0, lax.rem(gy + GY - 2 + j // GX, GY), lax.rem(gx + j, GX))
            return c

        lax.fori_loop(0, 5 * GX, cross, 0)

    @pl.when(grp == 0)
    def _():
        def peer(k, c):
            hello(0, lax.rem(gy + k, GY), gx)
            return c

        lax.fori_loop(1, GY, peer, 0)

    square[...] = jnp.zeros((128, 128), F32)
    wide[...] = jnp.zeros(wide.shape, F32)

    @pl.when(grp == 1)
    def _():
        mixed_rows[...] = jnp.zeros(mixed_rows.shape, F32)

    for copy in loads:
        copy.wait()
    diagonal = iota((1, L), 1)
    for i in range(L):
        square[i : i + 1, 0:L] = mixing[i] + only(diagonal == i, 0.75)
    col = gx * W + iota((H, 2, W), 2)
    row = gy * H + iota((H, 2, W), 0)
    kind = iota((H, 2, W), 1)
    closed = ((kind == 0) & (col == NX - 1)) | ((kind == 1) & (row == NY - 1))
    wide[:, :, 0:W] = jnp.where(closed, F32(0.0), faces[...])

    @pl.when(grp == 1)
    def _():
        zoom(
            gy, gx, up, down, left, right, barrier, out_ref, state, cot, wide, mixed_rows, raw, square,
            ya, yb, yc, yd, cf, cfb, en, bs, ss, power, strip_out, strip_in, got, msg, box,
            strip_s, strip_r, ns_s, ns_r, b_s, b_r, c_s, c_r,
        )

    @pl.when(grp == 0)
    def _():
        parent(
            gy, gx, up, down, left, right, barrier, arow_ref, acol_ref, out_ref, state, cot, wide, square,
            cells, rows, ends, row_out, row_in, row_pad, window_out, got, g, ring_n, ring_s, ring_e, ring_w, faces_b, coarse, msg, box, boxpad,
            a_s, a_r, ring_snd, ring_rcv, b_s, b_r, c_s, c_r,
        )


def sweep(src, dst, cfb, k):
    low, high = k + 1, ROWS - 1 - k
    while low < high:
        n = min(BLOCK, high - low)
        line = src[low : low + n]
        dst[low : low + n] = (
            cfb[0, low : low + n] * line
            + cfb[1, low : low + n] * pltpu.roll(line, 127, 3)
            + cfb[2, low : low + n] * pltpu.roll(line, 1, 3)
            + cfb[3, low : low + n] * src[low + 1 : low + n + 1]
            + cfb[4, low : low + n] * src[low - 1 : low + n - 1]
        )
        low += n


def frame_sum(src, cfb):
    return jnp.sum(cfb[5, H : 2 * H] * src[H : 2 * H], axis=0)


def far(zy, zx):
    return (zx == 0) | (zx == GX - 1) | (zy <= 1) | (zy >= GY - 2)


def zoom(
    zy, zx, up, down, left, right, barrier, out_ref, state, cot, wide, mixed_rows, raw, square,
    ya, yb, yc, yd, cf, cfb, en, bs, ss, power, strip_out, strip_in, got, msg, box,
    strip_s, strip_r, ns_s, ns_r, b_s, b_r, c_s, c_r,
):
    lane = iota((64, 128), 1)
    lane64 = lane % 64
    for q in range(H // 2):
        for i in range(2):
            mixed_rows[q, 10:50, 64 * i : 64 * i + L] = state[2 * q + i]
            mixed_rows[q, 74:114, 64 * i : 64 * i + L] = cot[2 * q + i]
        turned = jnp.transpose(mixed_rows[q])
        for i in range(2):
            face = wide[2 * q + i]
            raw[2 * q + i] = turned[64 * i : 64 * i + 64]
            raw[2 * q + i, L : L + 2] = pltpu.roll(face, 10, 1) + pltpu.roll(face, 74, 1)
    for q in range(2):
        east = jnp.zeros((64, 128), F32)
        west = jnp.zeros((64, 128), F32)
        for k in range(5):
            row = raw[5 * q + k]
            here = (lane64 >= 10 * k) & (lane64 < 10 * k + 10)
            east = jnp.where(here, pltpu.roll(row, (10 * k - 40) % 128, 1), east)
            west = jnp.where(here, pltpu.roll(row, (10 * k - 10) % 128, 1), west)
        strip_out[0, :, q] = east.reshape(CHUNKS, 2, 8, 128)
        strip_out[1, :, q] = west.reshape(CHUNKS, 2, 8, 128)
    pl.semaphore_wait(barrier, 4)

    def strip_copy(s, c):
        return pltpu.make_async_remote_copy(
            src_ref=strip_out.at[s, c], dst_ref=strip_in.at[s, c], send_sem=strip_s.at[s, c], recv_sem=strip_r.at[s, c],
            device_id=(1, zy, (right, left)[s]), device_id_type=MESH,
        )

    def end_copy(s, c):
        return pltpu.make_async_remote_copy(
            src_ref=ya.at[c, pl.ds(H, H)], dst_ref=ya.at[c, pl.ds(2 * H * s, H)],
            send_sem=ns_s.at[s, c], recv_sem=ns_r.at[s, c],
            device_id=(1, (up, down)[s], zx), device_id_type=MESH,
        )

    order = (3, 0, 1, 2)
    for c in order:
        for s in range(2):
            strip_copy(s, c).start()
    lane16 = iota((2, 8, 128), 2)
    for c in order:
        for s in range(2):
            strip_copy(s, c).wait_recv()
        for q in range(2):
            from_west = strip_in[0, c, q]
            from_east = strip_in[1, c, q]
            for k in range(5):
                row = raw[5 * q + k, 16 * c : 16 * c + 16].reshape(2, 8, 128)
                row = jnp.where(lane16 % 64 < 10, pltpu.roll(from_west, (-10 * k) % 128, 2), row)
                here = (lane16 % 64 >= 50) & (lane16 % 64 < 60)
                row = jnp.where(here, pltpu.roll(from_east, (50 - 10 * k) % 128, 2), row)
                ya[c, H + 5 * q + k] = row
        for s in range(2):
            end_copy(s, c).start()

    b1 = jnp.transpose(square[...]) + pltpu.roll(jnp.concatenate([jnp.zeros((64, 128), F32), square[0:64]], 0), 64, 1)
    b2 = dot(b1, b1)
    b4 = dot(b2, b2)
    b8 = dot(b4, b4)
    for i, value in enumerate((b1, b2, b4, b8, dot(b8, b2))):
        power[i] = value

    row2 = iota((ROWS, 128), 0)
    lane2 = iota((ROWS, 128), 1)
    tangent = lane2 < 64

    def interior(dr, dc):
        gr = row2 + (dr - H) + zy * H
        gc = lane2 % 64 + (dc - H) + zx * W
        return only((gr >= FRAME) & (gr < NY - FRAME) & (gc >= FRAME) & (gc < NX - FRAME))

    def incoming(dr, dc):
        return jnp.where(tangent, F32(1.0), interior(dr, dc))

    inside = interior(0, 0)
    outgoing = jnp.where(tangent, inside, F32(1.0))
    edge = 1.0 - inside
    for r in range(ROWS):
        cfb[5, r, 0] = jnp.broadcast_to(edge[r : r + 1], (8, 128))
    star = jnp.where(zy == 1, 0, jnp.where(zy == GY - 2, 2, 1))
    other0 = jnp.where(zy == 1, 1, 0)
    other1 = jnp.where(zy == GY - 2, 1, 2)
    corner = jnp.where(zx == 0, 2, 5)
    sub8 = iota((8, 128), 0)
    lane8 = iota((8, 128), 1)
    column8 = (lane8 % 64) // 10 + 1
    for r in range(ROWS):
        br = r // H
        middle = (sub8 >= 1) & (sub8 <= 6) & (column8 == sub8) & (star + 0 * sub8 == br)
        first = (sub8 == 0) & (column8 == corner) & (other0 + 0 * sub8 == br)
        second = (sub8 == 7) & (column8 == corner) & (other1 + 0 * sub8 == br)
        tan_slot = jnp.where((middle | first | second) & (lane8 < 60), cfb[5, r, 0], F32(0.0))
        adj_slot = only((column8 == sub8) & (lane8 >= 64) & (lane8 < 124), 0.01)
        for b in range(3):
            value = adj_slot if b == br else jnp.zeros((8, 128), F32)
            yc[r, b] = value + tan_slot if b == 0 else value

    for s in range(2):
        end_copy(s, 3).wait()
    for i in range(2):
        en[i] = jnp.zeros((48, 128), F32)
        for r in range(ROWS):
            en[i, 8 + r : 9 + r] = ya[3, r, 1, 4 + i : 5 + i]
    east = en[0, 8:38]
    west = pltpu.roll(east, 1, 1)
    north = en[1, 8:38]
    south = en[1, 7:37]
    cf[0, 0:ROWS] = outgoing * incoming(0, 0) * (1.0 - east - west - north - south)
    cf[1, 0:ROWS] = outgoing * incoming(0, 1) * east
    cf[2, 0:ROWS] = outgoing * incoming(0, -1) * west
    cf[3, 0:ROWS] = outgoing * incoming(1, 0) * north
    cf[4, 0:ROWS] = outgoing * incoming(-1, 0) * south
    for i in range(5):
        for r in range(ROWS):
            cfb[i, r, 0] = jnp.broadcast_to(cf[i, r : r + 1], (8, 128))

    for k in range(SUB):
        src, dst = (yc, yd) if k % 2 == 0 else (yd, yc)
        bs[:, k] = src[H : 2 * H, 0]
        ss[k, 8:11] = frame_sum(src, cfb)
        ss[k, 11:16] = jnp.zeros((5, 8, 128), F32)
        sweep(src, dst, cfb, k)

    def chunk(i, carry):
        c = lax.rem(i + 3, CHUNKS)

        @pl.when(i > 0)
        def _():
            for s in range(2):
                end_copy(s, c).wait()

        for k in range(SUB):
            src, dst = (ya.at[c], yb) if k % 2 == 0 else (yb, ya.at[c])
            ss[k, pl.ds(2 * c, 2)] = frame_sum(src, cfb)
            sweep(src, dst, cfb, k)
        return carry

    lax.fori_loop(0, CHUNKS, chunk, 0)

    pick_tan = only((lane8 >= 10) & (lane8 < 50) & (lane8 // 10 - 1 == sub8), 0.01)
    pick_adj = only((lane8 >= 74) & (lane8 < 114) & ((lane8 - 64) // 10 - 1 == sub8))
    sums = dot_t(pick_adj, ss[...].reshape(SUB * 128, 128))
    sums = lanes_to_rows(sums, SUB)
    lane80 = iota((8 * SUB, 128), 1)
    level_sum = jnp.sum(ya[:, H : 2 * H], axis=1).reshape(64, 128)
    slot_sum = jnp.sum(bs[...], axis=0).reshape(8 * SUB, 128)
    means = dot_t(pick_tan, jnp.concatenate([slot_sum, jnp.zeros((48, 128), F32)], 0))
    means = jnp.concatenate([pltpu.roll(means, (-8 * k) % 128, 1) for k in range(SUB)], 0)
    weights = jnp.where(lane80 < 32, jnp.where(lane80 < 8, means, pltpu.roll(sums, 72, 1)), F32(0.0))
    own_sums = pltpu.roll(jnp.where(lane80 < L, sums, F32(0.0)), 64, 1)
    own_mean = dot_t(pick_tan, padded_rows(level_sum, 128))
    own_mean = jnp.where(lane8 < L, own_mean, F32(0.0))

    def row_wait(i):
        pltpu.make_async_remote_copy(
            src_ref=got.at[i], dst_ref=got.at[i], send_sem=b_s.at[0], recv_sem=b_r.at[i],
            device_id=(0, zy, zx), device_id_type=MESH,
        ).wait_recv()

    for i, absent in ((0, 0), (4, GY - 1)):
        wanted = far(zy, zx) & (zy != absent)

        @pl.when(wanted)
        def _():
            row_wait(i)

        @pl.when(jnp.logical_not(wanted))
        def _():
            got[i] = jnp.zeros((GX, 8, 128), F32)

    for i in range(1, 4):
        row_wait(i)
    patch = jnp.sum(got[...], axis=1)
    e3 = jnp.broadcast_to(patch[:, :, L : L + 1], patch.shape)
    n3 = jnp.broadcast_to(patch[:, :, L + 1 : L + 2], patch.shape)
    here = patch[1:4]
    e_here = e3[1:4]
    values = (
        here
        + e_here * (pltpu.roll(here, 7, 1) - here)
        - pltpu.roll(e_here, 1, 1) * (here - pltpu.roll(here, 1, 1))
        + n3[1:4] * (patch[2:5] - here)
        - n3[0:3] * (here - patch[0:3])
    )
    values = jnp.where(iota((3, 8, 128), 2) < L, values, F32(0.0))
    flag = zy + 0 * sub8
    main = jnp.where(flag == 1, values[0], jnp.where(flag == GY - 2, values[2], values[1]))
    side0 = jnp.where(flag == 1, values[1], values[0])
    side1 = jnp.where(flag == GY - 2, values[1], values[2])
    west_most = zx + 0 * iota((1, 128), 1) == 0
    side0 = jnp.where(west_most, side0[2:3], side0[5:6])
    side1 = jnp.where(west_most, side1[2:3], side1[5:6])
    v0 = jnp.where(sub8 == 0, side0, jnp.where(sub8 == 7, side1, main))
    forcing = jnp.where(iota((24, 128), 1) >= 64, here.reshape(24, 128), F32(0.0))
    u = dot(weights, padded_rows(jnp.concatenate([v0, forcing], 0), 128)) + own_sums
    u = [u[8 * k : 8 * k + 8] for k in range(SUB)] + [own_mean]
    p = dot(jnp.concatenate(u[1::2], 0), power[0])
    p = [u[2 * i] + p[8 * i : 8 * i + 8] for i in range(5)] + [own_mean]
    q = dot(jnp.concatenate(p[1::2], 0), power[1])
    q = [p[2 * i] + q[8 * i : 8 * i + 8] for i in range(3)]
    line = q[0] + dot(q[1], power[2]) + dot(q[2], power[3])
    msg[...] = line[0:4]
    me = zy * GX + zx

    def c_start(i, c):
        pltpu.make_async_remote_copy(
            src_ref=msg, dst_ref=box.at[me], send_sem=c_s.at[0], recv_sem=c_r.at[0],
            device_id=(0, lax.rem(zy + i // GX, GY), lax.rem(zx + i, GX)), device_id_type=MESH,
        ).start()
        return c

    lax.fori_loop(0, GY * GX, c_start, 0, unroll=8)

    powers = jnp.concatenate([v0, dot(v0, power[0])], 0)
    last = dot(powers, power[3])
    powers = jnp.concatenate([powers, dot(powers, power[1])], 0)
    powers = jnp.concatenate([powers, dot(powers, power[2]), last], 0)
    both = power[4, 0:64] + power[4, 64:128]
    force = dot(forcing, power[4])
    head = jnp.concatenate([both, force, powers[0:40]], 0)
    left_side = jnp.concatenate([jnp.transpose(head), jnp.transpose(padded_rows(powers[40:80], 128))], 1)[:, 0:168]
    for r in range(H):
        right_side = jnp.concatenate(
            [ya[:, H + r].reshape(64, 128), yc[H + r].reshape(24, 128), bs[r].reshape(80, 128)], 0
        )
        res = dot(left_side, right_side)
        res = jnp.transpose(res)
        out_ref[r] = jnp.where(iota((W, 128), 1) < 64, res[10:50], res[74:114])
    for c in order:
        for s in range(2):
            strip_copy(s, c).wait_send()
    pltpu.make_async_remote_copy(
        src_ref=box, dst_ref=box, send_sem=c_s.at[0], recv_sem=c_r.at[0], device_id=(0, zy, zx), device_id_type=MESH
    ).wait_send()


def parent(
    py, px, up, down, left, right, barrier, arow_ref, acol_ref, out_ref, state, cot, wide, square,
    cells, rows, ends, row_out, row_in, row_pad, window_out, got, g, ring_n, ring_s, ring_e, ring_w, faces_b, coarse, msg, box, boxpad,
    a_s, a_r, ring_snd, ring_rcv, b_s, b_r, c_s, c_r,
):
    r128 = iota((128, 128), 0)
    c128 = iota((128, 128), 1)
    turned = jnp.transpose(jnp.concatenate([wide[...].reshape(2 * H, 128), jnp.zeros((128 - 2 * H, 128), F32)], 0))[0:W]
    lane40 = iota((W, 128), 1)
    for r in range(H):
        cells[r * W : (r + 1) * W] = jnp.where((lane40 >= L) & (lane40 < L + 2), pltpu.roll(turned, L - 2 * r, 1), F32(0.0))
        cells[r * W : (r + 1) * W, 0:L] = state[r]
        cells[r * W : (r + 1) * W, 64 : 64 + L] = cot[r]
    mixed = dot(cells[...], jnp.transpose(square[...]) + only((r128 == c128) & (r128 >= L)))
    rows[0] = jnp.zeros((W, 128), F32)
    rows[H + 1] = jnp.zeros((W, 128), F32)
    for r in range(H):
        rows[1 + r] = mixed[r * W : (r + 1) * W]
    ends[...] = jnp.zeros((2, 16, 128), F32)
    for r in range(H):
        ends[0, r : r + 1] = rows[1 + r, 0:1]
        ends[1, r : r + 1] = rows[1 + r, W - 1 : W]
    for t in range(GY + 2):
        row_out[t] = rows[jnp.clip(t - 1 + arow_ref[0] - H * py, -1, H) + 1]
    row_in[0, py] = row_out[py + 1]
    g[...] = jnp.zeros(g.shape, F32)
    row_pad[...] = jnp.zeros(row_pad.shape, F32)
    pl.semaphore_wait(barrier, 5 * GX + GY - 1 + 2)

    def a_copy(t, extra, to):
        return pltpu.make_async_remote_copy(
            src_ref=row_out.at[t], dst_ref=row_in.at[extra, py], send_sem=a_s.at[extra], recv_sem=a_r.at[extra],
            device_id=(0, to, px), device_id_type=MESH,
        )

    def a_start(k, c):
        to = lax.rem(py + k, GY)
        a_copy(to + 1, 0, to).start()
        return c

    for t, to in ((0, 0), (GY + 1, GY - 1)):
        @pl.when(py != to)
        def _():
            a_copy(t, 1, to).start()

        @pl.when(py == to)
        def _():
            row_in[1, to] = row_out[t]

    lax.fori_loop(1, GY, a_start, 0)
    ring = []
    for s, (src, dst, where) in enumerate((
        (rows.at[H], ring_s, (0, up, px)),
        (rows.at[1], ring_n, (0, down, px)),
        (ends.at[1], ring_w, (0, py, right)),
        (ends.at[0], ring_e, (0, py, left)),
    )):
        copy = pltpu.make_async_remote_copy(
            src_ref=src, dst_ref=dst, send_sem=ring_snd.at[s], recv_sem=ring_rcv.at[s],
            device_id=where, device_id_type=MESH,
        )
        copy.start()
        ring.append(copy)
    start = jnp.clip(acol_ref[0] - 2 - W * px, -36, W) + 40

    def all_rows(extra):
        return pltpu.make_async_remote_copy(
            src_ref=row_in.at[extra, pl.ds(0, GY - 1)], dst_ref=row_in.at[extra, pl.ds(0, GY - 1)],
            send_sem=a_s.at[extra], recv_sem=a_r.at[extra], device_id=(0, py, px), device_id_type=MESH,
        )

    def windows_of(extra):
        all_rows(extra).wait_recv()
        row_pad[40:80] = jnp.sum(row_in[extra], axis=0)
        for z in range(GX):
            window_out[extra, z] = row_pad[pl.ds(start + 4 * z, 8)]

    def b_copy(extra, z, zy, i):
        return pltpu.make_async_remote_copy(
            src_ref=window_out.at[extra, z], dst_ref=got.at[i, px], send_sem=b_s.at[0], recv_sem=b_r.at[i],
            device_id=(1, zy, z), device_id_type=MESH,
        )

    def b_each(act):
        def body(k, c):
            z = lax.rem(px + k, GX)
            for d in (-1, 0, 1, -2, 2):
                zy = py + d
                wanted = (zy >= 0) & (zy < GY)

                @pl.when(wanted & far(zy, z) if d in (-2, 2) else wanted)
                def _():
                    act(b_copy(0, z, zy, 2 - d))

            return c

        lax.fori_loop(0, GX, body, 0)

        def extra_body(k, c):
            z = lax.rem(px + k, GX)
            for at, targets in ((0, ((0, 1), (1, 0))), (GY - 1, ((GY - 1, 3), (GY - 2, 4)))):
                @pl.when(py == at)
                def _():
                    for zy, i in targets:
                        act(b_copy(1, z, zy, i))

            return c

        lax.fori_loop(0, GX, extra_body, 0)

    windows_of(0)

    @pl.when((py == 0) | (py == GY - 1))
    def _():
        windows_of(1)

    b_each(lambda copy: copy.start())
    for copy in ring:
        copy.wait()
    g[0, 8:48] = ring_s[...]
    g[H + 1, 8:48] = ring_n[...]
    for r in range(H):
        g[1 + r, 8:48] = rows[1 + r]
        g[1 + r, 7:8] = ring_w[r : r + 1]
        g[1 + r, 48:49] = ring_e[r : r + 1]
    for r in range(H):
        y = g[r + 1]
        e = jnp.broadcast_to(y[:, L : L + 1], y.shape)
        n = jnp.broadcast_to(y[:, L + 1 : L + 2], y.shape)
        s = jnp.broadcast_to(g[r][:, L + 1 : L + 2], y.shape)
        w = pltpu.roll(e, 1, 0)
        faces_b[0, r] = e
        faces_b[1, r] = w
        faces_b[2, r] = n
        faces_b[3, r] = s
        coarse[r] = (
            y + e * (pltpu.roll(y, 55, 0) - y) - w * (y - pltpu.roll(y, 1, 0)) + n * (g[r + 2] - y) - s * (y - g[r])
        )
    for i in range(16):
        boxpad[i, 0:BOX0] = jnp.zeros((BOX0, 128), F32)
        boxpad[i, BOX0 + 32 : 144] = jnp.zeros((56, 128), F32)
    down_mix = pltpu.roll(jnp.concatenate([jnp.zeros((64, 128), F32), square[0:64]], 0), 64, 1)
    row0 = py * H - 1 - arow_ref[0]
    col0 = px * W - 8 - acol_ref[0]
    sub = iota((56, 128), 0)
    lane = iota((56, 128), 1)
    in_cols = (sub + col0 >= 0) & (sub + col0 < 32)
    first = jnp.clip(col0 + BOX0, 0, 88)

    all_rows(0).wait_send()
    for t, to in ((0, 0), (GY + 1, GY - 1)):
        @pl.when(py != to)
        def _():
            a_copy(t, 1, to).wait_send()

    b_each(lambda copy: copy.wait_send())
    pltpu.make_async_remote_copy(
        src_ref=box, dst_ref=box, send_sem=c_s.at[0], recv_sem=c_r.at[0], device_id=(1, py, px), device_id_type=MESH
    ).wait_recv()
    for i in range(16):
        for z in range(GX):
            boxpad[i, BOX0 + 4 * z : BOX0 + 4 + 4 * z] = box[GX * i + z]
    windows = []
    for i in range(H + 2):
        br = row0 + i
        within = in_cols & (br + 0 * sub >= 0) & (br + 0 * sub < 16)
        window = boxpad[jnp.clip(br, 0, 15), pl.ds(first, 56)]
        w = jnp.where(within, window, g[i])
        g[i] = w
        if 1 <= i <= H:
            coarse[i - 1] = jnp.where(within, window, coarse[i - 1])
    y_all = dot(g[...].reshape((H + 2) * 56, 128), down_mix).reshape(H + 2, 56, 128)
    for r in range(H):
        y = y_all[r + 1]
        res = (
            y
            + faces_b[0, r] * (pltpu.roll(y, 55, 0) - y)
            - faces_b[1, r] * (y - pltpu.roll(y, 1, 0))
            + faces_b[2, r] * (y_all[r + 2] - y)
            - faces_b[3, r] * (y - y_all[r])
        )
        res = jnp.where(lane < 64, coarse[r], res)
        out_ref[r] = res[8:48]


def shards(state_in, cotangent, faces, mixing, anchor_row, anchor_col):
    dma = pltpu.SemaphoreType.DMA
    smem = pl.BlockSpec(memory_space=pltpu.SMEM)
    hbm = pl.BlockSpec(memory_space=pltpu.HBM)
    out = pl.pallas_call(
        kernel,
        name="step",
        out_shape=jax.ShapeDtypeStruct((H, W, 128), F32),
        in_specs=[smem, smem, hbm, hbm, hbm, hbm],
        out_specs=pl.BlockSpec(memory_space=VMEM),
        scratch_shapes=[
            VMEM((H, W, L), F32),
            VMEM((H, W, L), F32),
            VMEM((H, 2, W), F32),
            VMEM((L, 1, L), F32),
            dma((4,)),
            VMEM((H, 64, 128), F32),
            VMEM((H // 2, 128, 128), F32),
            VMEM((H, 2, 128), F32),
            VMEM((128, 128), F32),
            VMEM((CHUNKS, ROWS, 2, 8, 128), F32),
            VMEM((ROWS, 2, 8, 128), F32),
            VMEM((ROWS, 3, 8, 128), F32),
            VMEM((ROWS, 3, 8, 128), F32),
            VMEM((5, 32, 128), F32),
            VMEM((6, ROWS, 1, 8, 128), F32),
            VMEM((2, 48, 128), F32),
            VMEM((H, SUB, 8, 128), F32),
            VMEM((SUB, 16, 8, 128), F32),
            VMEM((5, 128, 128), F32),
            VMEM((2, CHUNKS, 2, 2, 8, 128), F32),
            VMEM((2, CHUNKS, 2, 2, 8, 128), F32),
            VMEM((5, GX, 8, 128), F32),
            VMEM((4, 128), F32),
            VMEM((H * W, 128), F32),
            VMEM((H + 2, W, 128), F32),
            VMEM((2, 16, 128), F32),
            VMEM((GY + 2, W, 128), F32),
            VMEM((2, GY, W, 128), F32),
            VMEM((120, 128), F32),
            VMEM((2, GX, 8, 128), F32),
            VMEM((H + 2, 56, 128), F32),
            VMEM((W, 128), F32),
            VMEM((W, 128), F32),
            VMEM((16, 128), F32),
            VMEM((16, 128), F32),
            VMEM((4, H, 56, 128), F32),
            VMEM((H, 56, 128), F32),
            VMEM((GY * GX, 4, 128), F32),
            VMEM((16, 144, 128), F32),
            dma((2, CHUNKS)), dma((2, CHUNKS)), dma((2, CHUNKS)), dma((2, CHUNKS)),
            dma((2,)), dma((2,)), dma((4,)), dma((4,)), dma((1,)), dma((5,)), dma((1,)), dma((1,)),
        ],
        compiler_params=pltpu.CompilerParams(collective_id=0, has_side_effects=True, vmem_limit_bytes=56291328),
    )(
        anchor_row, anchor_col, state_in[0].transpose(1, 2, 0), cotangent[0].transpose(1, 2, 0),
        faces[0].transpose(1, 0, 2), mixing.transpose(1, 0, 2),
    )
    both = (out[:, :, 0:L], out[:, :, 64 : 64 + L])
    return tuple(half.transpose(2, 0, 1)[None] for half in both)


def solution(mesh):
    placed = (
        P("grp", None, "gy", "gx"),
        P("grp", None, "gy", "gx"),
        P("grp", None, "gy", "gx"),
        P("grp", None, None),
        P(),
        P(),
    )
    return jax.shard_map(
        shards,
        mesh=mesh,
        in_specs=placed,
        out_specs=(P("grp", None, "gy", "gx"), P("grp", None, "gy", "gx")),
        check_vma=False,
    )
```

```python
import jax
import jax.numpy as jnp
from jax import lax
from jax.experimental import pallas as pl
from jax.experimental.pallas import tpu as pltpu
from jax.sharding import PartitionSpec as P

MESH = pl.DeviceIdType.MESH
HIGHEST = lax.Precision.HIGHEST
F32 = jnp.float32
VMEM = pltpu.VMEM
L = 60
H = 10
W = 40
NY = 160
NX = 320
GY = 16
GX = 8
FRAME = 2
SUB = 10
CHUNKS = 4
ROWS = 3 * H
BLOCK = 4
BOX0 = 56


def dot(a, b):
    return lax.dot_general(a, b, (((1,), (0,)), ((), ())), precision=HIGHEST, preferred_element_type=F32)


def dot_t(a, b):
    return lax.dot_general(a, b, (((1,), (1,)), ((), ())), precision=HIGHEST, preferred_element_type=F32)


def iota(shape, dim):
    return lax.broadcasted_iota(jnp.int32, shape, dim)


def only(keep, value=1.0):
    return jnp.where(keep, F32(value), F32(0.0))


def padded_rows(a, rows):
    return jnp.concatenate([a, jnp.zeros((rows - a.shape[0], a.shape[1]), F32)], 0)


def lanes_to_rows(a, count):
    return jnp.concatenate([a[:, 128 * k : 128 * k + 128] for k in range(count)], 0)


def rows_to_lanes(a, count):
    return jnp.concatenate([a[8 * k : 8 * k + 8] for k in range(count)], 1)


def kernel(
    arow_ref, acol_ref, state_hbm, cot_hbm, faces_hbm, mix_hbm,
    out_ref,
    state, cot, faces, mixing, load_s, raw, mixed_rows, wide, square,
    ya, yb, yc, yd, cf, cfb, en, bs, ss, power, strip_out, strip_in, got, msg,
    cells, rows, ends, row_out, row_in, row_pad, window_out, g, ring_n, ring_s, ring_e, ring_w, faces_b, coarse, box, boxpad,
    strip_s, strip_r, ns_s, ns_r, a_s, a_r, ring_snd, ring_rcv, b_s, b_r, c_s, c_r,
):
    grp = lax.axis_index("grp")
    gy = lax.axis_index("gy")
    gx = lax.axis_index("gx")
    up = lax.rem(gy + 1, GY)
    down = lax.rem(gy + GY - 1, GY)
    right = lax.rem(gx + 1, GX)
    left = lax.rem(gx + GX - 1, GX)
    loads = [
        pltpu.make_async_copy(src, dst, load_s.at[i])
        for i, (src, dst) in enumerate(((state_hbm, state), (cot_hbm, cot), (faces_hbm, faces), (mix_hbm, mixing)))
    ]
    for copy in loads:
        copy.start()
    barrier = pltpu.get_barrier_semaphore()

    def hello(*where):
        pl.semaphore_signal(barrier, inc=1, device_id=where, device_id_type=MESH)

    hello(grp, gy, left)
    hello(grp, gy, right)

    @pl.when(grp == 1)
    def _():
        hello(grp, up, gx)
        hello(grp, down, gx)

        def cross(j, c):
            hello(0, gy, lax.rem(gx + j, GX))
            return c

        lax.fori_loop(0, GX, cross, 0)

    @pl.when(grp == 0)
    def _():
        def peer(k, c):
            hello(0, lax.rem(gy + k, GY), gx)
            return c

        lax.fori_loop(1, GY, peer, 0)

    square[...] = jnp.zeros((128, 128), F32)
    wide[...] = jnp.zeros(wide.shape, F32)

    @pl.when(grp == 1)
    def _():
        mixed_rows[...] = jnp.zeros(mixed_rows.shape, F32)

    for copy in loads:
        copy.wait()
    diagonal = iota((1, L), 1)
    for i in range(L):
        square[i : i + 1, 0:L] = mixing[i] + only(diagonal == i, 0.75)
    col = gx * W + iota((H, 2, W), 2)
    row = gy * H + iota((H, 2, W), 0)
    kind = iota((H, 2, W), 1)
    closed = ((kind == 0) & (col == NX - 1)) | ((kind == 1) & (row == NY - 1))
    wide[:, :, 0:W] = jnp.where(closed, F32(0.0), faces[...])

    @pl.when(grp == 1)
    def _():
        zoom(
            gy, gx, up, down, left, right, barrier, out_ref, state, cot, wide, mixed_rows, raw, square,
            ya, yb, yc, yd, cf, cfb, en, bs, ss, power, strip_out, strip_in, got, msg, box,
            strip_s, strip_r, ns_s, ns_r, b_s, b_r, c_s, c_r,
        )

    @pl.when(grp == 0)
    def _():
        parent(
            gy, gx, up, down, left, right, barrier, arow_ref, acol_ref, out_ref, state, cot, wide, square,
            cells, rows, ends, row_out, row_in, row_pad, window_out, got, g, ring_n, ring_s, ring_e, ring_w, faces_b, coarse, msg, box, boxpad,
            a_s, a_r, ring_snd, ring_rcv, b_s, b_r, c_s, c_r,
        )


def sweep(src, dst, cfb, k):
    low, high = k + 1, ROWS - 1 - k
    while low < high:
        n = min(BLOCK, high - low)
        tall = src[low - 1 : low + n + 1]
        line = tall[1 : n + 1]
        dst[low : low + n] = (
            cfb[0, low : low + n] * line
            + cfb[1, low : low + n] * pltpu.roll(line, 127, 3)
            + cfb[2, low : low + n] * pltpu.roll(line, 1, 3)
            + cfb[3, low : low + n] * tall[2:]
            + cfb[4, low : low + n] * tall[:n]
        )
        low += n


def frame_sum(src, cfb):
    return jnp.sum(cfb[5, H : 2 * H] * src[H : 2 * H], axis=0)


def far(zy, zx):
    return (zx == 0) | (zx == GX - 1) | (zy <= 1) | (zy >= GY - 2)


def zoom(
    zy, zx, up, down, left, right, barrier, out_ref, state, cot, wide, mixed_rows, raw, square,
    ya, yb, yc, yd, cf, cfb, en, bs, ss, power, strip_out, strip_in, got, msg, box,
    strip_s, strip_r, ns_s, ns_r, b_s, b_r, c_s, c_r,
):
    lane = iota((64, 128), 1)
    lane64 = lane % 64
    for q in range(H // 2):
        for i in range(2):
            mixed_rows[q, 10:50, 64 * i : 64 * i + L] = state[2 * q + i]
            mixed_rows[q, 74:114, 64 * i : 64 * i + L] = cot[2 * q + i]
        turned = jnp.transpose(mixed_rows[q])
        for i in range(2):
            face = wide[2 * q + i]
            raw[2 * q + i] = turned[64 * i : 64 * i + 64]
            raw[2 * q + i, L : L + 2] = pltpu.roll(face, 10, 1) + pltpu.roll(face, 74, 1)
    for q in range(2):
        east = jnp.zeros((64, 128), F32)
        west = jnp.zeros((64, 128), F32)
        for k in range(5):
            row = raw[5 * q + k]
            here = (lane64 >= 10 * k) & (lane64 < 10 * k + 10)
            east = jnp.where(here, pltpu.roll(row, (10 * k - 40) % 128, 1), east)
            west = jnp.where(here, pltpu.roll(row, (10 * k - 10) % 128, 1), west)
        strip_out[0, :, q] = east.reshape(CHUNKS, 2, 8, 128)
        strip_out[1, :, q] = west.reshape(CHUNKS, 2, 8, 128)
    pl.semaphore_wait(barrier, 4)

    def strip_copy(s, c):
        return pltpu.make_async_remote_copy(
            src_ref=strip_out.at[s, c], dst_ref=strip_in.at[s, c], send_sem=strip_s.at[s, c], recv_sem=strip_r.at[s, c],
            device_id=(1, zy, (right, left)[s]), device_id_type=MESH,
        )

    def end_copy(s, c):
        return pltpu.make_async_remote_copy(
            src_ref=ya.at[c, pl.ds(H, H)], dst_ref=ya.at[c, pl.ds(2 * H * s, H)],
            send_sem=ns_s.at[s, c], recv_sem=ns_r.at[s, c],
            device_id=(1, (up, down)[s], zx), device_id_type=MESH,
        )

    order = (3, 0, 1, 2)
    for c in order:
        for s in range(2):
            strip_copy(s, c).start()
    lane16 = iota((2, 8, 128), 2)
    for c in order:
        for s in range(2):
            strip_copy(s, c).wait_recv()
        for q in range(2):
            from_west = strip_in[0, c, q]
            from_east = strip_in[1, c, q]
            for k in range(5):
                row = raw[5 * q + k, 16 * c : 16 * c + 16].reshape(2, 8, 128)
                row = jnp.where(lane16 % 64 < 10, pltpu.roll(from_west, (-10 * k) % 128, 2), row)
                here = (lane16 % 64 >= 50) & (lane16 % 64 < 60)
                row = jnp.where(here, pltpu.roll(from_east, (50 - 10 * k) % 128, 2), row)
                ya[c, H + 5 * q + k] = row
        for s in range(2):
            end_copy(s, c).start()

    b1 = jnp.transpose(square[...]) + pltpu.roll(jnp.concatenate([jnp.zeros((64, 128), F32), square[0:64]], 0), 64, 1)
    b2 = dot(b1, b1)
    b4 = dot(b2, b2)
    b8 = dot(b4, b4)
    for i, value in enumerate((b1, b2, b4, b8, dot(b8, b2))):
        power[i] = value

    row2 = iota((ROWS, 128), 0)
    lane2 = iota((ROWS, 128), 1)
    tangent = lane2 < 64

    def interior(dr, dc):
        gr = row2 + (dr - H) + zy * H
        gc = lane2 % 64 + (dc - H) + zx * W
        return only((gr >= FRAME) & (gr < NY - FRAME) & (gc >= FRAME) & (gc < NX - FRAME))

    def incoming(dr, dc):
        return jnp.where(tangent, F32(1.0), interior(dr, dc))

    inside = interior(0, 0)
    outgoing = jnp.where(tangent, inside, F32(1.0))
    edge = 1.0 - inside
    for r in range(ROWS):
        cfb[5, r, 0] = jnp.broadcast_to(edge[r : r + 1], (8, 128))
    star = jnp.where(zy == 1, 0, jnp.where(zy == GY - 2, 2, 1))
    other0 = jnp.where(zy == 1, 1, 0)
    other1 = jnp.where(zy == GY - 2, 1, 2)
    corner = jnp.where(zx == 0, 2, 5)
    sub8 = iota((8, 128), 0)
    lane8 = iota((8, 128), 1)
    column8 = (lane8 % 64) // 10 + 1
    for r in range(ROWS):
        br = r // H
        middle = (sub8 >= 1) & (sub8 <= 6) & (column8 == sub8) & (star + 0 * sub8 == br)
        first = (sub8 == 0) & (column8 == corner) & (other0 + 0 * sub8 == br)
        second = (sub8 == 7) & (column8 == corner) & (other1 + 0 * sub8 == br)
        tan_slot = jnp.where((middle | first | second) & (lane8 < 60), cfb[5, r, 0], F32(0.0))
        adj_slot = only((column8 == sub8) & (lane8 >= 64) & (lane8 < 124), 0.01)
        for b in range(3):
            value = adj_slot if b == br else jnp.zeros((8, 128), F32)
            yc[r, b] = value + tan_slot if b == 0 else value

    for s in range(2):
        end_copy(s, 3).wait()
    for i in range(2):
        en[i] = jnp.zeros((48, 128), F32)
        for r in range(ROWS):
            en[i, 8 + r : 9 + r] = ya[3, r, 1, 4 + i : 5 + i]
    east = en[0, 8:38]
    west = pltpu.roll(east, 1, 1)
    north = en[1, 8:38]
    south = en[1, 7:37]
    cf[0, 0:ROWS] = outgoing * incoming(0, 0) * (1.0 - east - west - north - south)
    cf[1, 0:ROWS] = outgoing * incoming(0, 1) * east
    cf[2, 0:ROWS] = outgoing * incoming(0, -1) * west
    cf[3, 0:ROWS] = outgoing * incoming(1, 0) * north
    cf[4, 0:ROWS] = outgoing * incoming(-1, 0) * south
    for i in range(5):
        for r in range(ROWS):
            cfb[i, r, 0] = jnp.broadcast_to(cf[i, r : r + 1], (8, 128))

    for k in range(SUB):
        src, dst = (yc, yd) if k % 2 == 0 else (yd, yc)
        bs[:, k] = src[H : 2 * H, 0]
        ss[k, 8:11] = frame_sum(src, cfb)
        ss[k, 11:16] = jnp.zeros((5, 8, 128), F32)
        sweep(src, dst, cfb, k)

    def chunk(i, carry):
        c = lax.rem(i + 3, CHUNKS)

        @pl.when(i > 0)
        def _():
            for s in range(2):
                end_copy(s, c).wait()

        for k in range(SUB):
            src, dst = (ya.at[c], yb) if k % 2 == 0 else (yb, ya.at[c])
            ss[k, pl.ds(2 * c, 2)] = frame_sum(src, cfb)
            sweep(src, dst, cfb, k)
        return carry

    lax.fori_loop(0, CHUNKS, chunk, 0)

    pick_tan = only((lane8 >= 10) & (lane8 < 50) & (lane8 // 10 - 1 == sub8), 0.01)
    pick_adj = only((lane8 >= 74) & (lane8 < 114) & ((lane8 - 64) // 10 - 1 == sub8))
    sums = dot_t(pick_adj, ss[...].reshape(SUB * 128, 128))
    sums = lanes_to_rows(sums, SUB)
    lane80 = iota((8 * SUB, 128), 1)
    level_sum = jnp.sum(ya[:, H : 2 * H], axis=1).reshape(64, 128)
    slot_sum = jnp.sum(bs[...], axis=0).reshape(8 * SUB, 128)
    means = dot_t(pick_tan, jnp.concatenate([slot_sum, jnp.zeros((48, 128), F32)], 0))
    means = jnp.concatenate([pltpu.roll(means, (-8 * k) % 128, 1) for k in range(SUB)], 0)
    weights = jnp.where(lane80 < 32, jnp.where(lane80 < 8, means, pltpu.roll(sums, 72, 1)), F32(0.0))
    own_sums = pltpu.roll(jnp.where(lane80 < L, sums, F32(0.0)), 64, 1)
    own_mean = dot_t(pick_tan, padded_rows(level_sum, 128))
    own_mean = jnp.where(lane8 < L, own_mean, F32(0.0))

    def row_wait(i):
        pltpu.make_async_remote_copy(
            src_ref=got.at[i], dst_ref=got.at[i], send_sem=b_s.at[0], recv_sem=b_r.at[i],
            device_id=(0, zy, zx), device_id_type=MESH,
        ).wait_recv()

    for i, absent in ((0, 0), (4, GY - 1)):
        wanted = far(zy, zx) & (zy != absent)

        @pl.when(wanted)
        def _():
            row_wait(i)

        @pl.when(jnp.logical_not(wanted))
        def _():
            got[i] = jnp.zeros((GX, 8, 128), F32)

    for i in range(1, 4):
        row_wait(i)
    patch = jnp.sum(got[...], axis=1)
    e3 = jnp.broadcast_to(patch[:, :, L : L + 1], patch.shape)
    n3 = jnp.broadcast_to(patch[:, :, L + 1 : L + 2], patch.shape)
    here = patch[1:4]
    e_here = e3[1:4]
    values = (
        here
        + e_here * (pltpu.roll(here, 7, 1) - here)
        - pltpu.roll(e_here, 1, 1) * (here - pltpu.roll(here, 1, 1))
        + n3[1:4] * (patch[2:5] - here)
        - n3[0:3] * (here - patch[0:3])
    )
    values = jnp.where(iota((3, 8, 128), 2) < L, values, F32(0.0))
    flag = zy + 0 * sub8
    main = jnp.where(flag == 1, values[0], jnp.where(flag == GY - 2, values[2], values[1]))
    side0 = jnp.where(flag == 1, values[1], values[0])
    side1 = jnp.where(flag == GY - 2, values[1], values[2])
    west_most = zx + 0 * iota((1, 128), 1) == 0
    side0 = jnp.where(west_most, side0[2:3], side0[5:6])
    side1 = jnp.where(west_most, side1[2:3], side1[5:6])
    v0 = jnp.where(sub8 == 0, side0, jnp.where(sub8 == 7, side1, main))
    forcing = jnp.where(iota((24, 128), 1) >= 64, here.reshape(24, 128), F32(0.0))
    u = dot(weights, padded_rows(jnp.concatenate([v0, forcing], 0), 128)) + own_sums
    u = [u[8 * k : 8 * k + 8] for k in range(SUB)] + [own_mean]
    p = dot(jnp.concatenate(u[1::2], 0), power[0])
    p = [u[2 * i] + p[8 * i : 8 * i + 8] for i in range(5)] + [own_mean]
    q = dot(jnp.concatenate(p[1::2], 0), power[1])
    q = [p[2 * i] + q[8 * i : 8 * i + 8] for i in range(3)]
    line = q[0] + dot(q[1], power[2]) + dot(q[2], power[3])
    msg[...] = line[0:4]
    me = zy * GX + zx

    def c_start(i, c):
        pltpu.make_async_remote_copy(
            src_ref=msg, dst_ref=box.at[me], send_sem=c_s.at[0], recv_sem=c_r.at[0],
            device_id=(0, lax.rem(zy + i // GX, GY), lax.rem(zx + i, GX)), device_id_type=MESH,
        ).start()
        return c

    lax.fori_loop(0, GY * GX, c_start, 0, unroll=8)

    powers = jnp.concatenate([v0, dot(v0, power[0])], 0)
    last = dot(powers, power[3])
    powers = jnp.concatenate([powers, dot(powers, power[1])], 0)
    powers = jnp.concatenate([powers, dot(powers, power[2]), last], 0)
    both = power[4, 0:64] + power[4, 64:128]
    force = dot(forcing, power[4])
    head = jnp.concatenate([both, force, powers[0:40]], 0)
    left_side = jnp.concatenate([jnp.transpose(head), jnp.transpose(padded_rows(powers[40:80], 128))], 1)[:, 0:168]
    for r in range(H):
        right_side = jnp.concatenate(
            [ya[:, H + r].reshape(64, 128), yc[H + r].reshape(24, 128), bs[r].reshape(80, 128)], 0
        )
        res = dot(left_side, right_side)
        res = jnp.transpose(res)
        out_ref[r] = jnp.where(iota((W, 128), 1) < 64, res[10:50], res[74:114])
    for c in order:
        for s in range(2):
            strip_copy(s, c).wait_send()
    pltpu.make_async_remote_copy(
        src_ref=box, dst_ref=box, send_sem=c_s.at[0], recv_sem=c_r.at[0], device_id=(0, zy, zx), device_id_type=MESH
    ).wait_send()


def parent(
    py, px, up, down, left, right, barrier, arow_ref, acol_ref, out_ref, state, cot, wide, square,
    cells, rows, ends, row_out, row_in, row_pad, window_out, got, g, ring_n, ring_s, ring_e, ring_w, faces_b, coarse, msg, box, boxpad,
    a_s, a_r, ring_snd, ring_rcv, b_s, b_r, c_s, c_r,
):
    r128 = iota((128, 128), 0)
    c128 = iota((128, 128), 1)
    turned = jnp.transpose(jnp.concatenate([wide[...].reshape(2 * H, 128), jnp.zeros((128 - 2 * H, 128), F32)], 0))[0:W]
    lane40 = iota((W, 128), 1)
    for r in range(H):
        cells[r * W : (r + 1) * W] = jnp.where((lane40 >= L) & (lane40 < L + 2), pltpu.roll(turned, L - 2 * r, 1), F32(0.0))
        cells[r * W : (r + 1) * W, 0:L] = state[r]
        cells[r * W : (r + 1) * W, 64 : 64 + L] = cot[r]
    mixed = dot(cells[...], jnp.transpose(square[...]) + only((r128 == c128) & (r128 >= L)))
    rows[0] = jnp.zeros((W, 128), F32)
    rows[H + 1] = jnp.zeros((W, 128), F32)
    for r in range(H):
        rows[1 + r] = mixed[r * W : (r + 1) * W]
    ends[...] = jnp.zeros((2, 16, 128), F32)
    for r in range(H):
        ends[0, r : r + 1] = rows[1 + r, 0:1]
        ends[1, r : r + 1] = rows[1 + r, W - 1 : W]
    for t in range(GY + 2):
        row_out[t] = rows[jnp.clip(t - 1 + arow_ref[0] - H * py, -1, H) + 1]
    row_in[0, py] = row_out[py + 1]
    g[...] = jnp.zeros(g.shape, F32)
    row_pad[...] = jnp.zeros(row_pad.shape, F32)
    pl.semaphore_wait(barrier, GX + GY - 1 + 2)

    def a_copy(t, extra, to):
        return pltpu.make_async_remote_copy(
            src_ref=row_out.at[t], dst_ref=row_in.at[extra, py], send_sem=a_s.at[extra], recv_sem=a_r.at[extra],
            device_id=(0, to, px), device_id_type=MESH,
        )

    def a_start(k, c):
        to = lax.rem(py + k, GY)
        a_copy(to + 1, 0, to).start()
        return c

    for t, to in ((0, 0), (GY + 1, GY - 1)):
        @pl.when(py != to)
        def _():
            a_copy(t, 1, to).start()

        @pl.when(py == to)
        def _():
            row_in[1, to] = row_out[t]

    lax.fori_loop(1, GY, a_start, 0)
    ring = []
    for s, (src, dst, where) in enumerate((
        (rows.at[H], ring_s, (0, up, px)),
        (rows.at[1], ring_n, (0, down, px)),
        (ends.at[1], ring_w, (0, py, right)),
        (ends.at[0], ring_e, (0, py, left)),
    )):
        copy = pltpu.make_async_remote_copy(
            src_ref=src, dst_ref=dst, send_sem=ring_snd.at[s], recv_sem=ring_rcv.at[s],
            device_id=where, device_id_type=MESH,
        )
        copy.start()
        ring.append(copy)
    start = jnp.clip(acol_ref[0] - 2 - W * px, -36, W) + 40

    def all_rows(extra):
        return pltpu.make_async_remote_copy(
            src_ref=row_in.at[extra, pl.ds(0, GY - 1)], dst_ref=row_in.at[extra, pl.ds(0, GY - 1)],
            send_sem=a_s.at[extra], recv_sem=a_r.at[extra], device_id=(0, py, px), device_id_type=MESH,
        )

    def windows_of(extra):
        all_rows(extra).wait_recv()
        row_pad[40:80] = jnp.sum(row_in[extra], axis=0)
        for z in range(GX):
            window_out[extra, z] = row_pad[pl.ds(start + 4 * z, 8)]

    def b_copy(extra, z, zy, i):
        return pltpu.make_async_remote_copy(
            src_ref=window_out.at[extra, z], dst_ref=got.at[i, px], send_sem=b_s.at[0], recv_sem=b_r.at[i],
            device_id=(1, zy, z), device_id_type=MESH,
        )

    def b_each(act):
        def body(k, c):
            z = lax.rem(px + k, GX)
            for d in (-1, 0, 1, -2, 2):
                zy = py + d
                wanted = (zy >= 0) & (zy < GY)

                @pl.when(wanted & far(zy, z) if d in (-2, 2) else wanted)
                def _():
                    act(b_copy(0, z, zy, 2 - d))

            return c

        lax.fori_loop(0, GX, body, 0)

        def extra_body(k, c):
            z = lax.rem(px + k, GX)
            for at, targets in ((0, ((0, 1), (1, 0))), (GY - 1, ((GY - 1, 3), (GY - 2, 4)))):
                @pl.when(py == at)
                def _():
                    for zy, i in targets:
                        act(b_copy(1, z, zy, i))

            return c

        lax.fori_loop(0, GX, extra_body, 0)

    windows_of(0)

    @pl.when((py == 0) | (py == GY - 1))
    def _():
        windows_of(1)

    b_each(lambda copy: copy.start())
    for copy in ring:
        copy.wait()
    g[0, 8:48] = ring_s[...]
    g[H + 1, 8:48] = ring_n[...]
    for r in range(H):
        g[1 + r, 8:48] = rows[1 + r]
        g[1 + r, 7:8] = ring_w[r : r + 1]
        g[1 + r, 48:49] = ring_e[r : r + 1]
    for r in range(H):
        y = g[r + 1]
        e = jnp.broadcast_to(y[:, L : L + 1], y.shape)
        n = jnp.broadcast_to(y[:, L + 1 : L + 2], y.shape)
        s = jnp.broadcast_to(g[r][:, L + 1 : L + 2], y.shape)
        w = pltpu.roll(e, 1, 0)
        faces_b[0, r] = e
        faces_b[1, r] = w
        faces_b[2, r] = n
        faces_b[3, r] = s
        coarse[r] = (
            y + e * (pltpu.roll(y, 55, 0) - y) - w * (y - pltpu.roll(y, 1, 0)) + n * (g[r + 2] - y) - s * (y - g[r])
        )
    for i in range(16):
        boxpad[i, 0:BOX0] = jnp.zeros((BOX0, 128), F32)
        boxpad[i, BOX0 + 32 : 144] = jnp.zeros((56, 128), F32)
    down_mix = pltpu.roll(jnp.concatenate([jnp.zeros((64, 128), F32), square[0:64]], 0), 64, 1)
    row0 = py * H - 1 - arow_ref[0]
    col0 = px * W - 8 - acol_ref[0]
    sub = iota((56, 128), 0)
    lane = iota((56, 128), 1)
    in_cols = (sub + col0 >= 0) & (sub + col0 < 32)
    first = jnp.clip(col0 + BOX0, 0, 88)

    all_rows(0).wait_send()
    for t, to in ((0, 0), (GY + 1, GY - 1)):
        @pl.when(py != to)
        def _():
            a_copy(t, 1, to).wait_send()

    b_each(lambda copy: copy.wait_send())
    pltpu.make_async_remote_copy(
        src_ref=box, dst_ref=box, send_sem=c_s.at[0], recv_sem=c_r.at[0], device_id=(1, py, px), device_id_type=MESH
    ).wait_recv()
    for i in range(16):
        for z in range(GX):
            boxpad[i, BOX0 + 4 * z : BOX0 + 4 + 4 * z] = box[GX * i + z]
    windows = []
    for i in range(H + 2):
        br = row0 + i
        within = in_cols & (br + 0 * sub >= 0) & (br + 0 * sub < 16)
        window = boxpad[jnp.clip(br, 0, 15), pl.ds(first, 56)]
        w = jnp.where(within, window, g[i])
        g[i] = w
        if 1 <= i <= H:
            coarse[i - 1] = jnp.where(within, window, coarse[i - 1])
    y_all = dot(g[...].reshape((H + 2) * 56, 128), down_mix).reshape(H + 2, 56, 128)
    for r in range(H):
        y = y_all[r + 1]
        res = (
            y
            + faces_b[0, r] * (pltpu.roll(y, 55, 0) - y)
            - faces_b[1, r] * (y - pltpu.roll(y, 1, 0))
            + faces_b[2, r] * (y_all[r + 2] - y)
            - faces_b[3, r] * (y - y_all[r])
        )
        res = jnp.where(lane < 64, coarse[r], res)
        out_ref[r] = res[8:48]


def shards(state_in, cotangent, faces, mixing, anchor_row, anchor_col):
    dma = pltpu.SemaphoreType.DMA
    smem = pl.BlockSpec(memory_space=pltpu.SMEM)
    hbm = pl.BlockSpec(memory_space=pltpu.HBM)
    out = pl.pallas_call(
        kernel,
        name="step",
        out_shape=jax.ShapeDtypeStruct((H, W, 128), F32),
        in_specs=[smem, smem, hbm, hbm, hbm, hbm],
        out_specs=pl.BlockSpec(memory_space=VMEM),
        scratch_shapes=[
            VMEM((H, W, L), F32),
            VMEM((H, W, L), F32),
            VMEM((H, 2, W), F32),
            VMEM((L, 1, L), F32),
            dma((4,)),
            VMEM((H, 64, 128), F32),
            VMEM((H // 2, 128, 128), F32),
            VMEM((H, 2, 128), F32),
            VMEM((128, 128), F32),
            VMEM((CHUNKS, ROWS, 2, 8, 128), F32),
            VMEM((ROWS, 2, 8, 128), F32),
            VMEM((ROWS, 3, 8, 128), F32),
            VMEM((ROWS, 3, 8, 128), F32),
            VMEM((5, 32, 128), F32),
            VMEM((6, ROWS, 1, 8, 128), F32),
            VMEM((2, 48, 128), F32),
            VMEM((H, SUB, 8, 128), F32),
            VMEM((SUB, 16, 8, 128), F32),
            VMEM((5, 128, 128), F32),
            VMEM((2, CHUNKS, 2, 2, 8, 128), F32),
            VMEM((2, CHUNKS, 2, 2, 8, 128), F32),
            VMEM((5, GX, 8, 128), F32),
            VMEM((4, 128), F32),
            VMEM((H * W, 128), F32),
            VMEM((H + 2, W, 128), F32),
            VMEM((2, 16, 128), F32),
            VMEM((GY + 2, W, 128), F32),
            VMEM((2, GY, W, 128), F32),
            VMEM((120, 128), F32),
            VMEM((2, GX, 8, 128), F32),
            VMEM((H + 2, 56, 128), F32),
            VMEM((W, 128), F32),
            VMEM((W, 128), F32),
            VMEM((16, 128), F32),
            VMEM((16, 128), F32),
            VMEM((4, H, 56, 128), F32),
            VMEM((H, 56, 128), F32),
            VMEM((GY * GX, 4, 128), F32),
            VMEM((16, 144, 128), F32),
            dma((2, CHUNKS)), dma((2, CHUNKS)), dma((2, CHUNKS)), dma((2, CHUNKS)),
            dma((2,)), dma((2,)), dma((4,)), dma((4,)), dma((1,)), dma((5,)), dma((1,)), dma((1,)),
        ],
        compiler_params=pltpu.CompilerParams(collective_id=0, has_side_effects=True, vmem_limit_bytes=56291328),
    )(
        anchor_row, anchor_col, state_in[0].transpose(1, 2, 0), cotangent[0].transpose(1, 2, 0),
        faces[0].transpose(1, 0, 2), mixing.transpose(1, 0, 2),
    )
    both = (out[:, :, 0:L], out[:, :, 64 : 64 + L])
    return tuple(half.transpose(2, 0, 1)[None] for half in both)


def solution(mesh):
    placed = (
        P("grp", None, "gy", "gx"),
        P("grp", None, "gy", "gx"),
        P("grp", None, "gy", "gx"),
        P("grp", None, None),
        P(),
        P(),
    )
    return jax.shard_map(
        shards,
        mesh=mesh,
        in_specs=placed,
        out_specs=(P("grp", None, "gy", "gx"), P("grp", None, "gy", "gx")),
        check_vma=False,
    )
```

```python
import jax
import jax.numpy as jnp
from jax import lax
from jax.experimental import pallas as pl
from jax.experimental.pallas import tpu as pltpu
from jax.sharding import PartitionSpec as P

MESH = pl.DeviceIdType.MESH
HIGHEST = lax.Precision.HIGHEST
F32 = jnp.float32
VMEM = pltpu.VMEM
L = 60
H = 10
W = 40
NY = 160
NX = 320
GY = 16
GX = 8
FRAME = 2
SUB = 10
CHUNKS = 4
ROWS = 3 * H
BLOCK = 4
BOX0 = 56
EDGES = 2 * GX + 2 * (GY - 2)
INNER = GY * GX - EDGES


def dot(a, b):
    return lax.dot_general(a, b, (((1,), (0,)), ((), ())), precision=HIGHEST, preferred_element_type=F32)


def dot_t(a, b):
    return lax.dot_general(a, b, (((1,), (1,)), ((), ())), precision=HIGHEST, preferred_element_type=F32)


def iota(shape, dim):
    return lax.broadcasted_iota(jnp.int32, shape, dim)


def only(keep, value=1.0):
    return jnp.where(keep, F32(value), F32(0.0))


def padded_rows(a, rows):
    return jnp.concatenate([a, jnp.zeros((rows - a.shape[0], a.shape[1]), F32)], 0)


def lanes_to_rows(a, count):
    return jnp.concatenate([a[:, 128 * k : 128 * k + 128] for k in range(count)], 0)


def rows_to_lanes(a, count):
    return jnp.concatenate([a[8 * k : 8 * k + 8] for k in range(count)], 1)


def kernel(
    arow_ref, acol_ref, state_hbm, cot_hbm, faces_hbm, mix_hbm,
    out_ref,
    state, cot, faces, mixing, load_s, raw, mixed_rows, wide, square,
    ya, yb, yc, yd, cf, cfb, en, bs, ss, power, strip_out, strip_in, face_out, face_in, got, msg, brief,
    cells, rows, ends, row_out, row_in, extra_out, extra_in, row_pad, window_out, g, ring_n, ring_s, ring_e, ring_w, faces_b, coarse, box, inner, boxpad,
    strip_s, strip_r, face_s, face_r, ns_s, ns_r, a_s, a_r, ring_snd, ring_rcv, b_s, b_r, c_s, c_r,
):
    grp = lax.axis_index("grp")
    gy = lax.axis_index("gy")
    gx = lax.axis_index("gx")
    up = lax.rem(gy + 1, GY)
    down = lax.rem(gy + GY - 1, GY)
    right = lax.rem(gx + 1, GX)
    left = lax.rem(gx + GX - 1, GX)
    loads = [
        pltpu.make_async_copy(src, dst, load_s.at[i])
        for i, (src, dst) in enumerate(((state_hbm, state), (cot_hbm, cot), (faces_hbm, faces), (mix_hbm, mixing)))
    ]
    for copy in loads:
        copy.start()
    barrier = pltpu.get_barrier_semaphore()

    def hello(*where):
        pl.semaphore_signal(barrier, inc=1, device_id=where, device_id_type=MESH)

    hello(grp, gy, left)
    hello(grp, gy, right)

    @pl.when(grp == 1)
    def _():
        hello(grp, up, gx)
        hello(grp, down, gx)

        def cross(j, c):
            hello(0, gy, lax.rem(gx + j, GX))
            return c

        lax.fori_loop(0, GX, cross, 0)

    @pl.when(grp == 0)
    def _():
        def peer(k, c):
            hello(0, lax.rem(gy + k, GY), gx)
            return c

        lax.fori_loop(1, GY, peer, 0)

    square[...] = jnp.zeros((128, 128), F32)
    wide[...] = jnp.zeros(wide.shape, F32)

    @pl.when(grp == 1)
    def _():
        mixed_rows[...] = jnp.zeros(mixed_rows.shape, F32)

    for copy in loads:
        copy.wait()
    diagonal = iota((1, L), 1)
    for i in range(L):
        square[i : i + 1, 0:L] = mixing[i] + only(diagonal == i, 0.75)
    col = gx * W + iota((H, 2, W), 2)
    row = gy * H + iota((H, 2, W), 0)
    kind = iota((H, 2, W), 1)
    closed = ((kind == 0) & (col == NX - 1)) | ((kind == 1) & (row == NY - 1))
    wide[:, :, 0:W] = jnp.where(closed, F32(0.0), faces[...])

    @pl.when(grp == 1)
    def _():
        zoom(
            gy, gx, up, down, left, right, barrier, out_ref, state, cot, wide, mixed_rows, raw, square,
            ya, yb, yc, yd, cf, cfb, en, bs, ss, power, strip_out, strip_in, face_out, face_in, got, msg, brief, box, inner,
            strip_s, strip_r, face_s, face_r, ns_s, ns_r, b_s, b_r, c_s, c_r,
        )

    @pl.when(grp == 0)
    def _():
        parent(
            gy, gx, up, down, left, right, barrier, arow_ref, acol_ref, out_ref, state, cot, wide, square,
            cells, rows, ends, row_out, row_in, extra_out, extra_in, row_pad, window_out, got, g, ring_n, ring_s, ring_e, ring_w, faces_b, coarse, box, inner, boxpad,
            a_s, a_r, ring_snd, ring_rcv, b_s, b_r, c_s, c_r,
        )


def sweep(src, dst, cfb, k):
    low, high = k + 1, ROWS - 1 - k
    while low < high:
        n = min(BLOCK, high - low)
        tall = src[low - 1 : low + n + 1]
        line = tall[1 : n + 1]
        dst[low : low + n] = (
            cfb[0, low : low + n] * line
            + cfb[1, low : low + n] * pltpu.roll(line, 127, 3)
            + cfb[2, low : low + n] * pltpu.roll(line, 1, 3)
            + cfb[3, low : low + n] * tall[2:]
            + cfb[4, low : low + n] * tall[:n]
        )
        low += n


def frame_sum(src, cfb):
    return jnp.sum(cfb[5, H : 2 * H] * src[H : 2 * H], axis=0)


def far(zy, zx):
    return (zx == 0) | (zx == GX - 1) | (zy <= 1) | (zy >= GY - 2)


def zoom(
    zy, zx, up, down, left, right, barrier, out_ref, state, cot, wide, mixed_rows, raw, square,
    ya, yb, yc, yd, cf, cfb, en, bs, ss, power, strip_out, strip_in, face_out, face_in, got, msg, brief, box, inner,
    strip_s, strip_r, face_s, face_r, ns_s, ns_r, b_s, b_r, c_s, c_r,
):
    lane = iota((64, 128), 1)
    lane64 = lane % 64
    for q in range(H // 2):
        for i in range(2):
            mixed_rows[q, 10:50, 64 * i : 64 * i + L] = state[2 * q + i]
            mixed_rows[q, 74:114, 64 * i : 64 * i + L] = cot[2 * q + i]
        turned = jnp.transpose(mixed_rows[q])
        for i in range(2):
            face = wide[2 * q + i]
            raw[2 * q + i] = turned[64 * i : 64 * i + 64]
            raw[2 * q + i, L : L + 2] = pltpu.roll(face, 10, 1) + pltpu.roll(face, 74, 1)
    for q in range(2):
        east = jnp.zeros((64, 128), F32)
        west = jnp.zeros((64, 128), F32)
        for k in range(5):
            row = raw[5 * q + k]
            here = (lane64 >= 10 * k) & (lane64 < 10 * k + 10)
            east = jnp.where(here, pltpu.roll(row, (10 * k - 40) % 128, 1), east)
            west = jnp.where(here, pltpu.roll(row, (10 * k - 10) % 128, 1), west)
        strip_out[0, :, q] = east.reshape(CHUNKS, 2, 8, 128)
        strip_out[1, :, q] = west.reshape(CHUNKS, 2, 8, 128)
    pl.semaphore_wait(barrier, 4)

    def strip_copy(s, c):
        return pltpu.make_async_remote_copy(
            src_ref=strip_out.at[s, c], dst_ref=strip_in.at[s, c], send_sem=strip_s.at[s, c], recv_sem=strip_r.at[s, c],
            device_id=(1, zy, (right, left)[s]), device_id_type=MESH,
        )

    def end_copy(s, c):
        return pltpu.make_async_remote_copy(
            src_ref=ya.at[c, pl.ds(H, H)], dst_ref=ya.at[c, pl.ds(2 * H * s, H)],
            send_sem=ns_s.at[s, c], recv_sem=ns_r.at[s, c],
            device_id=(1, (up, down)[s], zx), device_id_type=MESH,
        )

    def face_copy(s):
        return pltpu.make_async_remote_copy(
            src_ref=face_out, dst_ref=face_in.at[s], send_sem=face_s.at[s], recv_sem=face_r.at[s],
            device_id=(1, (up, down)[s], zx), device_id_type=MESH,
        )

    order = (3, 0, 1, 2)
    for c in order:
        for s in range(2):
            strip_copy(s, c).start()
    lane16 = iota((2, 8, 128), 2)
    for c in order:
        for s in range(2):
            strip_copy(s, c).wait_recv()
        for q in range(2):
            from_west = strip_in[0, c, q]
            from_east = strip_in[1, c, q]
            for k in range(5):
                row = raw[5 * q + k, 16 * c : 16 * c + 16].reshape(2, 8, 128)
                row = jnp.where(lane16 % 64 < 10, pltpu.roll(from_west, (-10 * k) % 128, 2), row)
                here = (lane16 % 64 >= 50) & (lane16 % 64 < 60)
                row = jnp.where(here, pltpu.roll(from_east, (50 - 10 * k) % 128, 2), row)
                ya[c, H + 5 * q + k] = row
        if c == 3:
            for r in range(H):
                face_out[r] = ya[3, H + r, 1, 4:6]
            for s in range(2):
                face_copy(s).start()
        for s in range(2):
            end_copy(s, c).start()

    b1 = jnp.transpose(square[...]) + pltpu.roll(jnp.concatenate([jnp.zeros((64, 128), F32), square[0:64]], 0), 64, 1)
    b2 = dot(b1, b1)
    b4 = dot(b2, b2)
    b8 = dot(b4, b4)
    for i, value in enumerate((b1, b2, b4, b8, dot(b8, b2))):
        power[i] = value

    row2 = iota((ROWS, 128), 0)
    lane2 = iota((ROWS, 128), 1)
    tangent = lane2 < 64

    def interior(dr, dc):
        gr = row2 + (dr - H) + zy * H
        gc = lane2 % 64 + (dc - H) + zx * W
        return only((gr >= FRAME) & (gr < NY - FRAME) & (gc >= FRAME) & (gc < NX - FRAME))

    def incoming(dr, dc):
        return jnp.where(tangent, F32(1.0), interior(dr, dc))

    inside = interior(0, 0)
    outgoing = jnp.where(tangent, inside, F32(1.0))
    edge = 1.0 - inside
    for r in range(ROWS):
        cfb[5, r, 0] = jnp.broadcast_to(edge[r : r + 1], (8, 128))
    star = jnp.where(zy == 1, 0, jnp.where(zy == GY - 2, 2, 1))
    other0 = jnp.where(zy == 1, 1, 0)
    other1 = jnp.where(zy == GY - 2, 1, 2)
    corner = jnp.where(zx == 0, 2, 5)
    sub8 = iota((8, 128), 0)
    lane8 = iota((8, 128), 1)
    column8 = (lane8 % 64) // 10 + 1
    for r in range(ROWS):
        br = r // H
        middle = (sub8 >= 1) & (sub8 <= 6) & (column8 == sub8) & (star + 0 * sub8 == br)
        first = (sub8 == 0) & (column8 == corner) & (other0 + 0 * sub8 == br)
        second = (sub8 == 7) & (column8 == corner) & (other1 + 0 * sub8 == br)
        tan_slot = jnp.where((middle | first | second) & (lane8 < 60), cfb[5, r, 0], F32(0.0))
        adj_slot = only((column8 == sub8) & (lane8 >= 64) & (lane8 < 124), 0.01)
        for b in range(3):
            value = adj_slot if b == br else jnp.zeros((8, 128), F32)
            yc[r, b] = value + tan_slot if b == 0 else value

    for s in range(2):
        face_copy(s).wait()
    for i in range(2):
        en[i] = jnp.zeros((48, 128), F32)
        for r in range(H):
            en[i, 8 + r : 9 + r] = face_in[0, r, i : i + 1]
            en[i, 8 + H + r : 9 + H + r] = face_out[r, i : i + 1]
            en[i, 8 + 2 * H + r : 9 + 2 * H + r] = face_in[1, r, i : i + 1]
    east = en[0, 8:38]
    west = pltpu.roll(east, 1, 1)
    north = en[1, 8:38]
    south = en[1, 7:37]
    cf[0, 0:ROWS] = outgoing * incoming(0, 0) * (1.0 - east - west - north - south)
    cf[1, 0:ROWS] = outgoing * incoming(0, 1) * east
    cf[2, 0:ROWS] = outgoing * incoming(0, -1) * west
    cf[3, 0:ROWS] = outgoing * incoming(1, 0) * north
    cf[4, 0:ROWS] = outgoing * incoming(-1, 0) * south
    for i in range(5):
        for r in range(ROWS):
            cfb[i, r, 0] = jnp.broadcast_to(cf[i, r : r + 1], (8, 128))

    for k in range(SUB):
        src, dst = (yc, yd) if k % 2 == 0 else (yd, yc)
        bs[:, k] = src[H : 2 * H, 0]
        ss[k, 8:11] = frame_sum(src, cfb)
        ss[k, 11:16] = jnp.zeros((5, 8, 128), F32)
        sweep(src, dst, cfb, k)

    def chunk(i, carry):
        c = lax.rem(i + 3, CHUNKS)

        for s in range(2):
            end_copy(s, c).wait()

        for k in range(SUB):
            src, dst = (ya.at[c], yb) if k % 2 == 0 else (yb, ya.at[c])
            ss[k, pl.ds(2 * c, 2)] = frame_sum(src, cfb)
            sweep(src, dst, cfb, k)
        return carry

    lax.fori_loop(0, CHUNKS, chunk, 0)

    pick_tan = only((lane8 >= 10) & (lane8 < 50) & (lane8 // 10 - 1 == sub8), 0.01)
    pick_adj = only((lane8 >= 74) & (lane8 < 114) & ((lane8 - 64) // 10 - 1 == sub8))
    sums = dot_t(pick_adj, ss[...].reshape(SUB * 128, 128))
    sums = lanes_to_rows(sums, SUB)
    lane80 = iota((8 * SUB, 128), 1)
    level_sum = jnp.sum(ya[:, H : 2 * H], axis=1).reshape(64, 128)
    slot_sum = jnp.sum(bs[...], axis=0).reshape(8 * SUB, 128)
    means = dot_t(pick_tan, jnp.concatenate([slot_sum, jnp.zeros((48, 128), F32)], 0))
    means = jnp.concatenate([pltpu.roll(means, (-8 * k) % 128, 1) for k in range(SUB)], 0)
    weights = jnp.where(lane80 < 32, jnp.where(lane80 < 8, means, pltpu.roll(sums, 72, 1)), F32(0.0))
    own_sums = pltpu.roll(jnp.where(lane80 < L, sums, F32(0.0)), 64, 1)
    own_mean = dot_t(pick_tan, padded_rows(level_sum, 128))
    own_mean = jnp.where(lane8 < L, own_mean, F32(0.0))

    def row_wait(i):
        pltpu.make_async_remote_copy(
            src_ref=got.at[i], dst_ref=got.at[i], send_sem=b_s.at[0], recv_sem=b_r.at[i],
            device_id=(0, zy, zx), device_id_type=MESH,
        ).wait_recv()

    for i, absent in ((0, 0), (4, GY - 1)):
        wanted = far(zy, zx) & (zy != absent)

        @pl.when(wanted)
        def _():
            row_wait(i)

        @pl.when(jnp.logical_not(wanted))
        def _():
            got[i] = jnp.zeros((GX, 8, 128), F32)

    for i in range(1, 4):
        row_wait(i)
    patch = jnp.sum(got[...], axis=1)
    e3 = jnp.broadcast_to(patch[:, :, L : L + 1], patch.shape)
    n3 = jnp.broadcast_to(patch[:, :, L + 1 : L + 2], patch.shape)
    here = patch[1:4]
    e_here = e3[1:4]
    values = (
        here
        + e_here * (pltpu.roll(here, 7, 1) - here)
        - pltpu.roll(e_here, 1, 1) * (here - pltpu.roll(here, 1, 1))
        + n3[1:4] * (patch[2:5] - here)
        - n3[0:3] * (here - patch[0:3])
    )
    values = jnp.where(iota((3, 8, 128), 2) < L, values, F32(0.0))
    flag = zy + 0 * sub8
    main = jnp.where(flag == 1, values[0], jnp.where(flag == GY - 2, values[2], values[1]))
    side0 = jnp.where(flag == 1, values[1], values[0])
    side1 = jnp.where(flag == GY - 2, values[1], values[2])
    west_most = zx + 0 * iota((1, 128), 1) == 0
    side0 = jnp.where(west_most, side0[2:3], side0[5:6])
    side1 = jnp.where(west_most, side1[2:3], side1[5:6])
    v0 = jnp.where(sub8 == 0, side0, jnp.where(sub8 == 7, side1, main))
    forcing = jnp.where(iota((24, 128), 1) >= 64, here.reshape(24, 128), F32(0.0))
    u = dot(weights, padded_rows(jnp.concatenate([v0, forcing], 0), 128)) + own_sums
    u = [u[8 * k : 8 * k + 8] for k in range(SUB)] + [own_mean]
    p = dot(jnp.concatenate(u[1::2], 0), power[0])
    p = [u[2 * i] + p[8 * i : 8 * i + 8] for i in range(5)] + [own_mean]
    q = dot(jnp.concatenate(p[1::2], 0), power[1])
    q = [p[2 * i] + q[8 * i : 8 * i + 8] for i in range(3)]
    line = q[0] + dot(q[1], power[2]) + dot(q[2], power[3])
    swapped = pltpu.roll(line, 64, 1)
    on_edge = (zy == 0) | (zy == GY - 1) | (zx == 0) | (zx == GX - 1)

    def c_copy(src, dst, kind, i):
        return pltpu.make_async_remote_copy(
            src_ref=src, dst_ref=dst, send_sem=c_s.at[kind], recv_sem=c_r.at[kind],
            device_id=(0, (zy + (i >> 3)) & (GY - 1), (zx + i) & (GX - 1)), device_id_type=MESH,
        )

    @pl.when(on_edge)
    def _():
        msg[...] = line[0:4]
        side = 2 * GX + 2 * (zy - 1) + jnp.where(zx == 0, 0, 1)
        at = jnp.where(zy == 0, zx, jnp.where(zy == GY - 1, GX + zx, side))

        def c_start(i, c):
            c_copy(msg, box.at[at], 0, i).start()
            return c

        lax.fori_loop(0, GY * GX, c_start, 0, unroll=8)

    @pl.when(jnp.logical_not(on_edge))
    def _():
        brief[...] = jnp.where(lane8 < 64, line, jnp.concatenate([swapped[2:4], swapped[0:6]], 0))[0:2]
        at = (GX - 2) * (zy - 1) + zx - 1

        def c_start(i, c):
            c_copy(brief, inner.at[at], 1, i).start()
            return c

        lax.fori_loop(0, GY * GX, c_start, 0, unroll=8)

    powers = jnp.concatenate([v0, dot(v0, power[0])], 0)
    last = dot(powers, power[3])
    powers = jnp.concatenate([powers, dot(powers, power[1])], 0)
    powers = jnp.concatenate([powers, dot(powers, power[2]), last], 0)
    both = power[4, 0:64] + power[4, 64:128]
    force = dot(forcing, power[4])
    head = jnp.concatenate([both, force, powers[0:40]], 0)
    left_side = jnp.concatenate([jnp.transpose(head), jnp.transpose(padded_rows(powers[40:80], 128))], 1)[:, 0:168]
    for r in range(H):
        right_side = jnp.concatenate(
            [ya[:, H + r].reshape(64, 128), yc[H + r].reshape(24, 128), bs[r].reshape(80, 128)], 0
        )
        res = dot(left_side, right_side)
        res = jnp.transpose(res)
        out_ref[r] = jnp.where(iota((W, 128), 1) < 64, res[10:50], res[74:114])
    for c in order:
        for s in range(2):
            strip_copy(s, c).wait_send()

    @pl.when(on_edge)
    def _():
        c_copy(power.at[pl.ds(0, 4)], power.at[pl.ds(0, 4)], 0, 0).wait_send()

    @pl.when(jnp.logical_not(on_edge))
    def _():
        c_copy(power.at[pl.ds(0, 2)], power.at[pl.ds(0, 2)], 1, 0).wait_send()


def parent(
    py, px, up, down, left, right, barrier, arow_ref, acol_ref, out_ref, state, cot, wide, square,
    cells, rows, ends, row_out, row_in, extra_out, extra_in, row_pad, window_out, got, g, ring_n, ring_s, ring_e, ring_w, faces_b, coarse, box, inner, boxpad,
    a_s, a_r, ring_snd, ring_rcv, b_s, b_r, c_s, c_r,
):
    r128 = iota((128, 128), 0)
    c128 = iota((128, 128), 1)
    turned = jnp.transpose(jnp.concatenate([wide[...].reshape(2 * H, 128), jnp.zeros((128 - 2 * H, 128), F32)], 0))[0:W]
    lane40 = iota((W, 128), 1)
    for r in range(H):
        cells[r * W : (r + 1) * W] = jnp.where((lane40 >= L) & (lane40 < L + 2), pltpu.roll(turned, L - 2 * r, 1), F32(0.0))
        cells[r * W : (r + 1) * W, 0:L] = state[r]
        cells[r * W : (r + 1) * W, 64 : 64 + L] = cot[r]
    mixed = dot(cells[...], jnp.transpose(square[...]) + only((r128 == c128) & (r128 >= L)))
    rows[0] = jnp.zeros((W, 128), F32)
    rows[H + 1] = jnp.zeros((W, 128), F32)
    for r in range(H):
        rows[1 + r] = mixed[r * W : (r + 1) * W]
    ends[...] = jnp.zeros((2, 16, 128), F32)
    for r in range(H):
        ends[0, r : r + 1] = rows[1 + r, 0:1]
        ends[1, r : r + 1] = rows[1 + r, W - 1 : W]
    for t in range(GY + 2):
        row_out[t] = rows[jnp.clip(t - 1 + arow_ref[0] - H * py, -1, H) + 1]
    row_in[py] = row_out[py + 1]
    lane24 = iota((24, 128), 1)
    for s, t in enumerate((0, GY + 1)):
        extra_out[s] = jnp.where(lane24 < 64, row_out[t, 0:24], pltpu.roll(row_out[t, 16:40], 64, 1))
    g[...] = jnp.zeros(g.shape, F32)
    row_pad[...] = jnp.zeros(row_pad.shape, F32)
    pl.semaphore_wait(barrier, GX + GY - 1 + 2)

    def a_copy(to):
        return pltpu.make_async_remote_copy(
            src_ref=row_out.at[to + 1], dst_ref=row_in.at[py], send_sem=a_s.at[0], recv_sem=a_r.at[0],
            device_id=(0, to, px), device_id_type=MESH,
        )

    def x_copy(s):
        return pltpu.make_async_remote_copy(
            src_ref=extra_out.at[s], dst_ref=extra_in.at[py], send_sem=a_s.at[1 + s], recv_sem=a_r.at[1],
            device_id=(0, 2 * px + s, px), device_id_type=MESH,
        )

    def a_start(k, c):
        a_copy((py + k) & (GY - 1)).start()
        return c

    for s in range(2):
        @pl.when(py != 2 * px + s)
        def _():
            x_copy(s).start()

        @pl.when(py == 2 * px + s)
        def _():
            extra_in[py] = extra_out[s]

    lax.fori_loop(1, GY, a_start, 0, unroll=5)
    ring = []
    for s, (src, dst, where) in enumerate((
        (rows.at[H], ring_s, (0, up, px)),
        (rows.at[1], ring_n, (0, down, px)),
        (ends.at[1], ring_w, (0, py, right)),
        (ends.at[0], ring_e, (0, py, left)),
    )):
        copy = pltpu.make_async_remote_copy(
            src_ref=src, dst_ref=dst, send_sem=ring_snd.at[s], recv_sem=ring_rcv.at[s],
            device_id=where, device_id_type=MESH,
        )
        copy.start()
        ring.append(copy)
    start = jnp.clip(acol_ref[0] - 2 - W * px, -36, W) + 40

    def all_rows(ref, i):
        return pltpu.make_async_remote_copy(
            src_ref=ref.at[pl.ds(0, GY - 1)], dst_ref=ref.at[pl.ds(0, GY - 1)],
            send_sem=a_s.at[i], recv_sem=a_r.at[i], device_id=(0, py, px), device_id_type=MESH,
        )

    def cut(extra):
        for z in range(GX):
            window_out[extra, z] = row_pad[pl.ds(start + 4 * z, 8)]

    def b_copy(extra, z, zy, i):
        return pltpu.make_async_remote_copy(
            src_ref=window_out.at[extra, z], dst_ref=got.at[i, px], send_sem=b_s.at[0], recv_sem=b_r.at[i],
            device_id=(1, zy, z), device_id_type=MESH,
        )

    def b_each(act):
        def body(k, c):
            z = (px + k) & (GX - 1)
            for d in (-1, 0, 1, -2, 2):
                zy = py + d
                wanted = (zy >= 0) & (zy < GY)

                @pl.when(wanted & far(zy, z) if d in (-2, 2) else wanted)
                def _():
                    act(b_copy(0, z, zy, 2 - d))

            return c

        lax.fori_loop(0, GX, body, 0, unroll=4)

        def extra_body(k, c):
            z = (px + k) & (GX - 1)
            for s, targets in enumerate((((0, 1), (1, 0)), ((GY - 1, 3), (GY - 2, 4)))):
                @pl.when(py == 2 * px + s)
                def _():
                    for zy, i in targets:
                        act(b_copy(1, z, zy, i))

            return c

        lax.fori_loop(0, GX, extra_body, 0)

    all_rows(row_in, 0).wait_recv()
    row_pad[40:80] = jnp.sum(row_in[...], axis=0)
    cut(0)

    @pl.when((py == 2 * px) | (py == 2 * px + 1))
    def _():
        all_rows(extra_in, 1).wait_recv()
        both = jnp.sum(extra_in[...], axis=0)
        row_pad[40:64] = jnp.where(lane24 < 64, both, F32(0.0))
        row_pad[64:80] = jnp.where(lane24 < 64, pltpu.roll(both, 64, 1), F32(0.0))[8:24]
        cut(1)

    b_each(lambda copy: copy.start())
    for copy in ring:
        copy.wait()
    g[0, 8:48] = ring_s[...]
    g[H + 1, 8:48] = ring_n[...]
    for r in range(H):
        g[1 + r, 8:48] = rows[1 + r]
        g[1 + r, 7:8] = ring_w[r : r + 1]
        g[1 + r, 48:49] = ring_e[r : r + 1]
    for r in range(H):
        y = g[r + 1]
        e = jnp.broadcast_to(y[:, L : L + 1], y.shape)
        n = jnp.broadcast_to(y[:, L + 1 : L + 2], y.shape)
        s = jnp.broadcast_to(g[r][:, L + 1 : L + 2], y.shape)
        w = pltpu.roll(e, 1, 0)
        faces_b[0, r] = e
        faces_b[1, r] = w
        faces_b[2, r] = n
        faces_b[3, r] = s
        coarse[r] = (
            y + e * (pltpu.roll(y, 55, 0) - y) - w * (y - pltpu.roll(y, 1, 0)) + n * (g[r + 2] - y) - s * (y - g[r])
        )
    for i in range(16):
        boxpad[i, 0:BOX0] = jnp.zeros((BOX0, 128), F32)
        boxpad[i, BOX0 + 32 : 144] = jnp.zeros((56, 128), F32)
    down_mix = pltpu.roll(jnp.concatenate([jnp.zeros((64, 128), F32), square[0:64]], 0), 64, 1)
    row0 = py * H - 1 - arow_ref[0]
    col0 = px * W - 8 - acol_ref[0]
    sub = iota((56, 128), 0)
    lane = iota((56, 128), 1)
    in_cols = (sub + col0 >= 0) & (sub + col0 < 32)
    first = jnp.clip(col0 + BOX0, 0, 88)

    all_rows(row_in, 0).wait_send()
    for s in range(2):
        @pl.when(py != 2 * px + s)
        def _():
            x_copy(s).wait_send()

    b_each(lambda copy: copy.wait_send())
    for i, ref in enumerate((box, inner)):
        pltpu.make_async_remote_copy(
            src_ref=ref, dst_ref=ref, send_sem=c_s.at[i], recv_sem=c_r.at[i], device_id=(1, py, px), device_id_type=MESH
        ).wait_recv()
    lane2 = iota((2, 128), 1)
    for i in range(16):
        for z in range(GX):
            to = BOX0 + 4 * z
            if i in (0, 15):
                boxpad[i, to : to + 4] = box[z + (GX if i else 0)]
            elif z in (0, GX - 1):
                boxpad[i, to : to + 4] = box[2 * GX + 2 * (i - 1) + (1 if z else 0)]
            else:
                pair = inner[(GX - 2) * (i - 1) + z - 1]
                boxpad[i, to : to + 2] = jnp.where(lane2 < 64, pair, F32(0.0))
                boxpad[i, to + 2 : to + 4] = jnp.where(lane2 < 64, pltpu.roll(pair, 64, 1), F32(0.0))
    windows = []
    for i in range(H + 2):
        br = row0 + i
        within = in_cols & (br + 0 * sub >= 0) & (br + 0 * sub < 16)
        window = boxpad[jnp.clip(br, 0, 15), pl.ds(first, 56)]
        w = jnp.where(within, window, g[i])
        g[i] = w
        if 1 <= i <= H:
            coarse[i - 1] = jnp.where(within, window, coarse[i - 1])
    y_all = dot(g[...].reshape((H + 2) * 56, 128), down_mix).reshape(H + 2, 56, 128)
    for r in range(H):
        y = y_all[r + 1]
        res = (
            y
            + faces_b[0, r] * (pltpu.roll(y, 55, 0) - y)
            - faces_b[1, r] * (y - pltpu.roll(y, 1, 0))
            + faces_b[2, r] * (y_all[r + 2] - y)
            - faces_b[3, r] * (y - y_all[r])
        )
        res = jnp.where(lane < 64, coarse[r], res)
        out_ref[r] = res[8:48]


def shards(state_in, cotangent, faces, mixing, anchor_row, anchor_col):
    dma = pltpu.SemaphoreType.DMA
    smem = pl.BlockSpec(memory_space=pltpu.SMEM)
    hbm = pl.BlockSpec(memory_space=pltpu.HBM)
    out = pl.pallas_call(
        kernel,
        name="step",
        out_shape=jax.ShapeDtypeStruct((H, W, 128), F32),
        in_specs=[smem, smem, hbm, hbm, hbm, hbm],
        out_specs=pl.BlockSpec(memory_space=VMEM),
        scratch_shapes=[
            VMEM((H, W, L), F32),
            VMEM((H, W, L), F32),
            VMEM((H, 2, W), F32),
            VMEM((L, 1, L), F32),
            dma((4,)),
            VMEM((H, 64, 128), F32),
            VMEM((H // 2, 128, 128), F32),
            VMEM((H, 2, 128), F32),
            VMEM((128, 128), F32),
            VMEM((CHUNKS, ROWS, 2, 8, 128), F32),
            VMEM((ROWS, 2, 8, 128), F32),
            VMEM((ROWS, 3, 8, 128), F32),
            VMEM((ROWS, 3, 8, 128), F32),
            VMEM((5, 32, 128), F32),
            VMEM((6, ROWS, 1, 8, 128), F32),
            VMEM((2, 48, 128), F32),
            VMEM((H, SUB, 8, 128), F32),
            VMEM((SUB, 16, 8, 128), F32),
            VMEM((5, 128, 128), F32),
            VMEM((2, CHUNKS, 2, 2, 8, 128), F32),
            VMEM((2, CHUNKS, 2, 2, 8, 128), F32),
            VMEM((H, 2, 128), F32),
            VMEM((2, H, 2, 128), F32),
            VMEM((5, GX, 8, 128), F32),
            VMEM((4, 128), F32),
            VMEM((2, 128), F32),
            VMEM((H * W, 128), F32),
            VMEM((H + 2, W, 128), F32),
            VMEM((2, 16, 128), F32),
            VMEM((GY + 2, W, 128), F32),
            VMEM((GY, W, 128), F32),
            VMEM((2, 24, 128), F32),
            VMEM((GY, 24, 128), F32),
            VMEM((120, 128), F32),
            VMEM((2, GX, 8, 128), F32),
            VMEM((H + 2, 56, 128), F32),
            VMEM((W, 128), F32),
            VMEM((W, 128), F32),
            VMEM((16, 128), F32),
            VMEM((16, 128), F32),
            VMEM((4, H, 56, 128), F32),
            VMEM((H, 56, 128), F32),
            VMEM((EDGES, 4, 128), F32),
            VMEM((INNER, 2, 128), F32),
            VMEM((16, 144, 128), F32),
            dma((2, CHUNKS)), dma((2, CHUNKS)), dma((2,)), dma((2,)), dma((2, CHUNKS)), dma((2, CHUNKS)),
            dma((3,)), dma((2,)), dma((4,)), dma((4,)), dma((1,)), dma((5,)), dma((2,)), dma((2,)),
        ],
        compiler_params=pltpu.CompilerParams(collective_id=0, has_side_effects=True, vmem_limit_bytes=56291328),
    )(
        anchor_row, anchor_col, state_in[0].transpose(1, 2, 0), cotangent[0].transpose(1, 2, 0),
        faces[0].transpose(1, 0, 2), mixing.transpose(1, 0, 2),
    )
    both = (out[:, :, 0:L], out[:, :, 64 : 64 + L])
    return tuple(half.transpose(2, 0, 1)[None] for half in both)


def solution(mesh):
    placed = (
        P("grp", None, "gy", "gx"),
        P("grp", None, "gy", "gx"),
        P("grp", None, "gy", "gx"),
        P("grp", None, None),
        P(),
        P(),
    )
    return jax.shard_map(
        shards,
        mesh=mesh,
        in_specs=placed,
        out_specs=(P("grp", None, "gy", "gx"), P("grp", None, "gy", "gx")),
        check_vma=False,
    )
```

```python
import jax
import jax.numpy as jnp
from jax import lax
from jax.experimental import pallas as pl
from jax.experimental.pallas import tpu as pltpu
from jax.sharding import PartitionSpec as P

MESH = pl.DeviceIdType.MESH
HIGHEST = lax.Precision.HIGHEST
F32 = jnp.float32
VMEM = pltpu.VMEM
L = 60
H = 10
W = 40
NY = 160
NX = 320
GY = 16
GX = 8
FRAME = 2
SUB = 10
CHUNKS = 4
ROWS = 3 * H
BLOCK = 4
BOX0 = 56
EDGES = 2 * GX + 2 * (GY - 2)
INNER = GY * GX - EDGES


def dot(a, b):
    return lax.dot_general(a, b, (((1,), (0,)), ((), ())), precision=HIGHEST, preferred_element_type=F32)


def dot_t(a, b):
    return lax.dot_general(a, b, (((1,), (1,)), ((), ())), precision=HIGHEST, preferred_element_type=F32)


def iota(shape, dim):
    return lax.broadcasted_iota(jnp.int32, shape, dim)


def only(keep, value=1.0):
    return jnp.where(keep, F32(value), F32(0.0))


def padded_rows(a, rows):
    return jnp.concatenate([a, jnp.zeros((rows - a.shape[0], a.shape[1]), F32)], 0)


def lanes_to_rows(a, count):
    return jnp.concatenate([a[:, 128 * k : 128 * k + 128] for k in range(count)], 0)


def rows_to_lanes(a, count):
    return jnp.concatenate([a[8 * k : 8 * k + 8] for k in range(count)], 1)


def kernel(
    arow_ref, acol_ref, state_hbm, cot_hbm, faces_hbm, mix_hbm,
    out_ref,
    state, cot, faces, mixing, load_s, raw, mixed_rows, wide, square,
    ya, yb, yc, yd, cf, cfb, en, bs, ss, power, strip_out, strip_in, face_out, face_in, got, msg, brief,
    cells, rows, ends, row_out, row_in, extra_out, extra_in, row_pad, window_out, g, ring_n, ring_s, ring_e, ring_w, faces_b, coarse, box, inner, boxpad,
    strip_s, strip_r, face_s, face_r, ns_s, ns_r, a_s, a_r, ring_snd, ring_rcv, b_s, b_r, c_s, c_r,
):
    grp = lax.axis_index("grp")
    gy = lax.axis_index("gy")
    gx = lax.axis_index("gx")
    up = lax.rem(gy + 1, GY)
    down = lax.rem(gy + GY - 1, GY)
    right = lax.rem(gx + 1, GX)
    left = lax.rem(gx + GX - 1, GX)
    loads = [
        pltpu.make_async_copy(src, dst, load_s.at[i])
        for i, (src, dst) in enumerate(((state_hbm, state), (cot_hbm, cot), (faces_hbm, faces), (mix_hbm, mixing)))
    ]
    for copy in loads:
        copy.start()
    barrier = pltpu.get_barrier_semaphore()

    def hello(*where):
        pl.semaphore_signal(barrier, inc=1, device_id=where, device_id_type=MESH)

    hello(grp, gy, left)
    hello(grp, gy, right)

    @pl.when(grp == 1)
    def _():
        hello(grp, up, gx)
        hello(grp, down, gx)

        def cross(j, c):
            hello(0, gy, lax.rem(gx + j, GX))
            return c

        lax.fori_loop(0, GX, cross, 0)

    @pl.when(grp == 0)
    def _():
        def peer(k, c):
            hello(0, lax.rem(gy + k, GY), gx)
            return c

        lax.fori_loop(1, GY, peer, 0)

    square[...] = jnp.zeros((128, 128), F32)
    wide[...] = jnp.zeros(wide.shape, F32)

    @pl.when(grp == 1)
    def _():
        mixed_rows[...] = jnp.zeros(mixed_rows.shape, F32)

    for copy in loads:
        copy.wait()
    diagonal = iota((1, L), 1)
    for i in range(L):
        square[i : i + 1, 0:L] = mixing[i] + only(diagonal == i, 0.75)
    col = gx * W + iota((H, 2, W), 2)
    row = gy * H + iota((H, 2, W), 0)
    kind = iota((H, 2, W), 1)
    closed = ((kind == 0) & (col == NX - 1)) | ((kind == 1) & (row == NY - 1))
    wide[:, :, 0:W] = jnp.where(closed, F32(0.0), faces[...])

    @pl.when(grp == 1)
    def _():
        zoom(
            gy, gx, up, down, left, right, barrier, out_ref, state, cot, wide, mixed_rows, raw, square,
            ya, yb, yc, yd, cf, cfb, en, bs, ss, power, strip_out, strip_in, face_out, face_in, got, msg, brief, box, inner,
            strip_s, strip_r, face_s, face_r, ns_s, ns_r, b_s, b_r, c_s, c_r,
        )

    @pl.when(grp == 0)
    def _():
        parent(
            gy, gx, up, down, left, right, barrier, arow_ref, acol_ref, out_ref, state, cot, wide, square,
            cells, rows, ends, row_out, row_in, extra_out, extra_in, row_pad, window_out, got, g, ring_n, ring_s, ring_e, ring_w, faces_b, coarse, box, inner, boxpad,
            a_s, a_r, ring_snd, ring_rcv, b_s, b_r, c_s, c_r,
        )


def sweep(src, dst, cfb, k):
    low, high = k + 1, ROWS - 1 - k
    while low < high:
        n = min(BLOCK, high - low)
        tall = src[low - 1 : low + n + 1]
        line = tall[1 : n + 1]
        dst[low : low + n] = (
            cfb[0, low : low + n] * line
            + cfb[1, low : low + n] * pltpu.roll(line, 127, 3)
            + cfb[2, low : low + n] * pltpu.roll(line, 1, 3)
            + cfb[3, low : low + n] * tall[2:]
            + cfb[4, low : low + n] * tall[:n]
        )
        low += n


def frame_sum(src, cfb):
    return jnp.sum(cfb[5, H : 2 * H] * src[H : 2 * H], axis=0)


def far(zy, zx):
    return (zx == 0) | (zx == GX - 1) | (zy <= 1) | (zy >= GY - 2)


def zoom(
    zy, zx, up, down, left, right, barrier, out_ref, state, cot, wide, mixed_rows, raw, square,
    ya, yb, yc, yd, cf, cfb, en, bs, ss, power, strip_out, strip_in, face_out, face_in, got, msg, brief, box, inner,
    strip_s, strip_r, face_s, face_r, ns_s, ns_r, b_s, b_r, c_s, c_r,
):
    lane = iota((64, 128), 1)
    lane64 = lane % 64
    for q in range(H // 2):
        for i in range(2):
            mixed_rows[q, 10:50, 64 * i : 64 * i + L] = state[2 * q + i]
            mixed_rows[q, 74:114, 64 * i : 64 * i + L] = cot[2 * q + i]
        turned = jnp.transpose(mixed_rows[q])
        for i in range(2):
            face = wide[2 * q + i]
            raw[2 * q + i] = turned[64 * i : 64 * i + 64]
            raw[2 * q + i, L : L + 2] = pltpu.roll(face, 10, 1) + pltpu.roll(face, 74, 1)
    for q in range(2):
        east = jnp.zeros((64, 128), F32)
        west = jnp.zeros((64, 128), F32)
        for k in range(5):
            row = raw[5 * q + k]
            here = (lane64 >= 10 * k) & (lane64 < 10 * k + 10)
            east = jnp.where(here, pltpu.roll(row, (10 * k - 40) % 128, 1), east)
            west = jnp.where(here, pltpu.roll(row, (10 * k - 10) % 128, 1), west)
        strip_out[0, :, q] = east.reshape(CHUNKS, 2, 8, 128)
        strip_out[1, :, q] = west.reshape(CHUNKS, 2, 8, 128)
    pl.semaphore_wait(barrier, 4)

    def strip_copy(s, c):
        return pltpu.make_async_remote_copy(
            src_ref=strip_out.at[s, c], dst_ref=strip_in.at[s, c], send_sem=strip_s.at[s, c], recv_sem=strip_r.at[s, c],
            device_id=(1, zy, (right, left)[s]), device_id_type=MESH,
        )

    def end_copy(s, c):
        return pltpu.make_async_remote_copy(
            src_ref=ya.at[c, pl.ds(H, H)], dst_ref=ya.at[c, pl.ds(2 * H * s, H)],
            send_sem=ns_s.at[s, c], recv_sem=ns_r.at[s, c],
            device_id=(1, (up, down)[s], zx), device_id_type=MESH,
        )

    def face_copy(s):
        return pltpu.make_async_remote_copy(
            src_ref=face_out, dst_ref=face_in.at[s], send_sem=face_s.at[s], recv_sem=face_r.at[s],
            device_id=(1, (up, down)[s], zx), device_id_type=MESH,
        )

    order = (3, 0, 1, 2)
    for c in order:
        for s in range(2):
            strip_copy(s, c).start()
    lane16 = iota((2, 8, 128), 2)
    for c in order:
        for s in range(2):
            strip_copy(s, c).wait_recv()
        for q in range(2):
            from_west = strip_in[0, c, q]
            from_east = strip_in[1, c, q]
            for k in range(5):
                row = raw[5 * q + k, 16 * c : 16 * c + 16].reshape(2, 8, 128)
                row = jnp.where(lane16 % 64 < 10, pltpu.roll(from_west, (-10 * k) % 128, 2), row)
                here = (lane16 % 64 >= 50) & (lane16 % 64 < 60)
                row = jnp.where(here, pltpu.roll(from_east, (50 - 10 * k) % 128, 2), row)
                ya[c, H + 5 * q + k] = row
        if c == 3:
            for r in range(H):
                face_out[r] = ya[3, H + r, 1, 4:6]
            for s in range(2):
                face_copy(s).start()
        for s in range(2):
            end_copy(s, c).start()

    b1 = jnp.transpose(square[...]) + pltpu.roll(jnp.concatenate([jnp.zeros((64, 128), F32), square[0:64]], 0), 64, 1)
    b2 = dot(b1, b1)
    b4 = dot(b2, b2)
    b8 = dot(b4, b4)
    for i, value in enumerate((b1, b2, b4, b8, dot(b8, b2))):
        power[i] = value

    row2 = iota((ROWS, 128), 0)
    lane2 = iota((ROWS, 128), 1)
    tangent = lane2 < 64

    def interior(dr, dc):
        gr = row2 + (dr - H) + zy * H
        gc = lane2 % 64 + (dc - H) + zx * W
        return only((gr >= FRAME) & (gr < NY - FRAME) & (gc >= FRAME) & (gc < NX - FRAME))

    def incoming(dr, dc):
        return jnp.where(tangent, F32(1.0), interior(dr, dc))

    inside = interior(0, 0)
    outgoing = jnp.where(tangent, inside, F32(1.0))
    edge = 1.0 - inside
    for r in range(ROWS):
        cfb[5, r, 0] = jnp.broadcast_to(edge[r : r + 1], (8, 128))
    star = jnp.where(zy == 1, 0, jnp.where(zy == GY - 2, 2, 1))
    other0 = jnp.where(zy == 1, 1, 0)
    other1 = jnp.where(zy == GY - 2, 1, 2)
    corner = jnp.where(zx == 0, 2, 5)
    sub8 = iota((8, 128), 0)
    lane8 = iota((8, 128), 1)
    column8 = (lane8 % 64) // 10 + 1
    for r in range(ROWS):
        br = r // H
        middle = (sub8 >= 1) & (sub8 <= 6) & (column8 == sub8) & (star + 0 * sub8 == br)
        first = (sub8 == 0) & (column8 == corner) & (other0 + 0 * sub8 == br)
        second = (sub8 == 7) & (column8 == corner) & (other1 + 0 * sub8 == br)
        tan_slot = jnp.where((middle | first | second) & (lane8 < 60), cfb[5, r, 0], F32(0.0))
        adj_slot = only((column8 == sub8) & (lane8 >= 64) & (lane8 < 124), 0.01)
        for b in range(3):
            value = adj_slot if b == br else jnp.zeros((8, 128), F32)
            yc[r, b] = value + tan_slot if b == 0 else value

    for s in range(2):
        face_copy(s).wait()
    for i in range(2):
        en[i] = jnp.zeros((48, 128), F32)
        for r in range(H):
            en[i, 8 + r : 9 + r] = face_in[0, r, i : i + 1]
            en[i, 8 + H + r : 9 + H + r] = face_out[r, i : i + 1]
            en[i, 8 + 2 * H + r : 9 + 2 * H + r] = face_in[1, r, i : i + 1]
    east = en[0, 8:38]
    west = pltpu.roll(east, 1, 1)
    north = en[1, 8:38]
    south = en[1, 7:37]
    cf[0, 0:ROWS] = outgoing * incoming(0, 0) * (1.0 - east - west - north - south)
    cf[1, 0:ROWS] = outgoing * incoming(0, 1) * east
    cf[2, 0:ROWS] = outgoing * incoming(0, -1) * west
    cf[3, 0:ROWS] = outgoing * incoming(1, 0) * north
    cf[4, 0:ROWS] = outgoing * incoming(-1, 0) * south
    for i in range(5):
        for r in range(ROWS):
            cfb[i, r, 0] = jnp.broadcast_to(cf[i, r : r + 1], (8, 128))

    for k in range(SUB):
        src, dst = (yc, yd) if k % 2 == 0 else (yd, yc)
        bs[:, k] = src[H : 2 * H, 0]
        ss[k, 8:11] = frame_sum(src, cfb)
        ss[k, 11:16] = jnp.zeros((5, 8, 128), F32)
        sweep(src, dst, cfb, k)

    pick_tan = only((lane8 >= 10) & (lane8 < 50) & (lane8 // 10 - 1 == sub8), 0.01)
    slot_sum = jnp.sum(bs[...], axis=0).reshape(8 * SUB, 128)
    means = dot_t(pick_tan, jnp.concatenate([slot_sum, jnp.zeros((48, 128), F32)], 0))
    means = jnp.concatenate([pltpu.roll(means, (-8 * k) % 128, 1) for k in range(SUB)], 0)

    def chunk(i, carry):
        c = lax.rem(i + 3, CHUNKS)

        for s in range(2):
            end_copy(s, c).wait()

        for k in range(SUB):
            src, dst = (ya.at[c], yb) if k % 2 == 0 else (yb, ya.at[c])
            ss[k, pl.ds(2 * c, 2)] = frame_sum(src, cfb)
            sweep(src, dst, cfb, k)
        return carry

    lax.fori_loop(0, CHUNKS, chunk, 0)

    pick_adj = only((lane8 >= 74) & (lane8 < 114) & ((lane8 - 64) // 10 - 1 == sub8))
    sums = dot_t(pick_adj, ss[...].reshape(SUB * 128, 128))
    sums = lanes_to_rows(sums, SUB)
    lane80 = iota((8 * SUB, 128), 1)
    level_sum = jnp.sum(ya[:, H : 2 * H], axis=1).reshape(64, 128)
    weights = jnp.where(lane80 < 32, jnp.where(lane80 < 8, means, pltpu.roll(sums, 72, 1)), F32(0.0))
    own_sums = pltpu.roll(jnp.where(lane80 < L, sums, F32(0.0)), 64, 1)
    own_mean = dot_t(pick_tan, padded_rows(level_sum, 128))
    own_mean = jnp.where(lane8 < L, own_mean, F32(0.0))

    def row_wait(i):
        pltpu.make_async_remote_copy(
            src_ref=got.at[i], dst_ref=got.at[i], send_sem=b_s.at[0], recv_sem=b_r.at[i],
            device_id=(0, zy, zx), device_id_type=MESH,
        ).wait_recv()

    for i, absent in ((0, 0), (4, GY - 1)):
        wanted = far(zy, zx) & (zy != absent)

        @pl.when(wanted)
        def _():
            row_wait(i)

        @pl.when(jnp.logical_not(wanted))
        def _():
            got[i] = jnp.zeros((GX, 8, 128), F32)

    for i in range(1, 4):
        row_wait(i)
    patch = jnp.sum(got[...], axis=1)
    e3 = jnp.broadcast_to(patch[:, :, L : L + 1], patch.shape)
    n3 = jnp.broadcast_to(patch[:, :, L + 1 : L + 2], patch.shape)
    here = patch[1:4]
    e_here = e3[1:4]
    values = (
        here
        + e_here * (pltpu.roll(here, 7, 1) - here)
        - pltpu.roll(e_here, 1, 1) * (here - pltpu.roll(here, 1, 1))
        + n3[1:4] * (patch[2:5] - here)
        - n3[0:3] * (here - patch[0:3])
    )
    values = jnp.where(iota((3, 8, 128), 2) < L, values, F32(0.0))
    flag = zy + 0 * sub8
    main = jnp.where(flag == 1, values[0], jnp.where(flag == GY - 2, values[2], values[1]))
    side0 = jnp.where(flag == 1, values[1], values[0])
    side1 = jnp.where(flag == GY - 2, values[1], values[2])
    west_most = zx + 0 * iota((1, 128), 1) == 0
    side0 = jnp.where(west_most, side0[2:3], side0[5:6])
    side1 = jnp.where(west_most, side1[2:3], side1[5:6])
    v0 = jnp.where(sub8 == 0, side0, jnp.where(sub8 == 7, side1, main))
    forcing = jnp.where(iota((24, 128), 1) >= 64, here.reshape(24, 128), F32(0.0))
    u = dot(weights, padded_rows(jnp.concatenate([v0, forcing], 0), 128)) + own_sums
    u = [u[8 * k : 8 * k + 8] for k in range(SUB)] + [own_mean]
    p = dot(jnp.concatenate(u[1::2], 0), power[0])
    p = [u[2 * i] + p[8 * i : 8 * i + 8] for i in range(5)] + [own_mean]
    q = dot(jnp.concatenate(p[1::2], 0), power[1])
    q = [p[2 * i] + q[8 * i : 8 * i + 8] for i in range(3)]
    line = q[0] + dot(q[1], power[2]) + dot(q[2], power[3])
    swapped = pltpu.roll(line, 64, 1)
    on_edge = (zy == 0) | (zy == GY - 1) | (zx == 0) | (zx == GX - 1)

    def c_copy(src, dst, kind, i):
        return pltpu.make_async_remote_copy(
            src_ref=src, dst_ref=dst, send_sem=c_s.at[kind], recv_sem=c_r.at[kind],
            device_id=(0, (zy + (i >> 3)) & (GY - 1), (zx + i) & (GX - 1)), device_id_type=MESH,
        )

    @pl.when(on_edge)
    def _():
        msg[...] = line[0:4]
        side = 2 * GX + 2 * (zy - 1) + jnp.where(zx == 0, 0, 1)
        at = jnp.where(zy == 0, zx, jnp.where(zy == GY - 1, GX + zx, side))

        def c_start(i, c):
            c_copy(msg, box.at[at], 0, i).start()
            return c

        lax.fori_loop(0, GY * GX, c_start, 0, unroll=8)

    @pl.when(jnp.logical_not(on_edge))
    def _():
        brief[...] = jnp.where(lane8 < 64, line, jnp.concatenate([swapped[2:4], swapped[0:6]], 0))[0:2]
        at = (GX - 2) * (zy - 1) + zx - 1

        def c_start(i, c):
            c_copy(brief, inner.at[at], 1, i).start()
            return c

        lax.fori_loop(0, GY * GX, c_start, 0, unroll=8)

    powers = jnp.concatenate([v0, dot(v0, power[0])], 0)
    last = dot(powers, power[3])
    powers = jnp.concatenate([powers, dot(powers, power[1])], 0)
    powers = jnp.concatenate([powers, dot(powers, power[2]), last], 0)
    both = power[4, 0:64] + power[4, 64:128]
    force = dot(forcing, power[4])
    head = jnp.concatenate([both, force, powers[0:40]], 0)
    left_side = jnp.concatenate([jnp.transpose(head), jnp.transpose(padded_rows(powers[40:80], 128))], 1)[:, 0:168]
    for r in range(H):
        right_side = jnp.concatenate(
            [ya[:, H + r].reshape(64, 128), yc[H + r].reshape(24, 128), bs[r].reshape(80, 128)], 0
        )
        res = dot(left_side, right_side)
        res = jnp.transpose(res)
        out_ref[r] = jnp.where(iota((W, 128), 1) < 64, res[10:50], res[74:114])
    for c in order:
        for s in range(2):
            strip_copy(s, c).wait_send()

    @pl.when(on_edge)
    def _():
        c_copy(power.at[pl.ds(0, 4)], power.at[pl.ds(0, 4)], 0, 0).wait_send()

    @pl.when(jnp.logical_not(on_edge))
    def _():
        c_copy(power.at[pl.ds(0, 2)], power.at[pl.ds(0, 2)], 1, 0).wait_send()


def parent(
    py, px, up, down, left, right, barrier, arow_ref, acol_ref, out_ref, state, cot, wide, square,
    cells, rows, ends, row_out, row_in, extra_out, extra_in, row_pad, window_out, got, g, ring_n, ring_s, ring_e, ring_w, faces_b, coarse, box, inner, boxpad,
    a_s, a_r, ring_snd, ring_rcv, b_s, b_r, c_s, c_r,
):
    r128 = iota((128, 128), 0)
    c128 = iota((128, 128), 1)
    turned = jnp.transpose(jnp.concatenate([wide[...].reshape(2 * H, 128), jnp.zeros((128 - 2 * H, 128), F32)], 0))[0:W]
    lane40 = iota((W, 128), 1)
    for r in range(H):
        cells[r * W : (r + 1) * W] = jnp.where((lane40 >= L) & (lane40 < L + 2), pltpu.roll(turned, L - 2 * r, 1), F32(0.0))
        cells[r * W : (r + 1) * W, 0:L] = state[r]
        cells[r * W : (r + 1) * W, 64 : 64 + L] = cot[r]
    mixed = dot(cells[...], jnp.transpose(square[...]) + only((r128 == c128) & (r128 >= L)))
    rows[0] = jnp.zeros((W, 128), F32)
    rows[H + 1] = jnp.zeros((W, 128), F32)
    for r in range(H):
        rows[1 + r] = mixed[r * W : (r + 1) * W]
    ends[...] = jnp.zeros((2, 16, 128), F32)
    for r in range(H):
        ends[0, r : r + 1] = rows[1 + r, 0:1]
        ends[1, r : r + 1] = rows[1 + r, W - 1 : W]
    for t in range(GY + 2):
        row_out[t] = rows[jnp.clip(t - 1 + arow_ref[0] - H * py, -1, H) + 1]
    row_in[py] = row_out[py + 1]
    lane24 = iota((24, 128), 1)
    for s, t in enumerate((0, GY + 1)):
        extra_out[s] = jnp.where(lane24 < 64, row_out[t, 0:24], pltpu.roll(row_out[t, 16:40], 64, 1))
    g[...] = jnp.zeros(g.shape, F32)
    row_pad[...] = jnp.zeros(row_pad.shape, F32)
    pl.semaphore_wait(barrier, GX + GY - 1 + 2)

    def a_copy(to):
        return pltpu.make_async_remote_copy(
            src_ref=row_out.at[to + 1], dst_ref=row_in.at[py], send_sem=a_s.at[0], recv_sem=a_r.at[0],
            device_id=(0, to, px), device_id_type=MESH,
        )

    def x_copy(s):
        return pltpu.make_async_remote_copy(
            src_ref=extra_out.at[s], dst_ref=extra_in.at[py], send_sem=a_s.at[1 + s], recv_sem=a_r.at[1],
            device_id=(0, 2 * px + s, px), device_id_type=MESH,
        )

    def a_start(k, c):
        a_copy((py + k) & (GY - 1)).start()
        return c

    for s in range(2):
        @pl.when(py != 2 * px + s)
        def _():
            x_copy(s).start()

        @pl.when(py == 2 * px + s)
        def _():
            extra_in[py] = extra_out[s]

    lax.fori_loop(1, GY, a_start, 0, unroll=5)
    ring = []
    for s, (src, dst, where) in enumerate((
        (rows.at[H], ring_s, (0, up, px)),
        (rows.at[1], ring_n, (0, down, px)),
        (ends.at[1], ring_w, (0, py, right)),
        (ends.at[0], ring_e, (0, py, left)),
    )):
        copy = pltpu.make_async_remote_copy(
            src_ref=src, dst_ref=dst, send_sem=ring_snd.at[s], recv_sem=ring_rcv.at[s],
            device_id=where, device_id_type=MESH,
        )
        copy.start()
        ring.append(copy)
    start = jnp.clip(acol_ref[0] - 2 - W * px, -36, W) + 40

    def all_rows(ref, i):
        return pltpu.make_async_remote_copy(
            src_ref=ref.at[pl.ds(0, GY - 1)], dst_ref=ref.at[pl.ds(0, GY - 1)],
            send_sem=a_s.at[i], recv_sem=a_r.at[i], device_id=(0, py, px), device_id_type=MESH,
        )

    def cut(extra):
        for z in range(GX):
            window_out[extra, z] = row_pad[pl.ds(start + 4 * z, 8)]

    def b_copy(extra, z, zy, i):
        return pltpu.make_async_remote_copy(
            src_ref=window_out.at[extra, z], dst_ref=got.at[i, px], send_sem=b_s.at[0], recv_sem=b_r.at[i],
            device_id=(1, zy, z), device_id_type=MESH,
        )

    def b_each(act):
        def body(k, c):
            z = (px + k) & (GX - 1)
            for d in (-1, 0, 1, -2, 2):
                zy = py + d
                wanted = (zy >= 0) & (zy < GY)

                @pl.when(wanted & far(zy, z) if d in (-2, 2) else wanted)
                def _():
                    act(b_copy(0, z, zy, 2 - d))

            return c

        lax.fori_loop(0, GX, body, 0, unroll=4)

        def extra_body(k, c):
            z = (px + k) & (GX - 1)
            for s, targets in enumerate((((0, 1), (1, 0)), ((GY - 1, 3), (GY - 2, 4)))):
                @pl.when(py == 2 * px + s)
                def _():
                    for zy, i in targets:
                        act(b_copy(1, z, zy, i))

            return c

        lax.fori_loop(0, GX, extra_body, 0)

    all_rows(row_in, 0).wait_recv()
    row_pad[40:80] = jnp.sum(row_in[...], axis=0)
    cut(0)

    @pl.when((py == 2 * px) | (py == 2 * px + 1))
    def _():
        all_rows(extra_in, 1).wait_recv()
        both = jnp.sum(extra_in[...], axis=0)
        row_pad[40:64] = jnp.where(lane24 < 64, both, F32(0.0))
        row_pad[64:80] = jnp.where(lane24 < 64, pltpu.roll(both, 64, 1), F32(0.0))[8:24]
        cut(1)

    b_each(lambda copy: copy.start())
    for copy in ring:
        copy.wait()
    g[0, 8:48] = ring_s[...]
    g[H + 1, 8:48] = ring_n[...]
    for r in range(H):
        g[1 + r, 8:48] = rows[1 + r]
        g[1 + r, 7:8] = ring_w[r : r + 1]
        g[1 + r, 48:49] = ring_e[r : r + 1]
    for r in range(H):
        y = g[r + 1]
        e = jnp.broadcast_to(y[:, L : L + 1], y.shape)
        n = jnp.broadcast_to(y[:, L + 1 : L + 2], y.shape)
        s = jnp.broadcast_to(g[r][:, L + 1 : L + 2], y.shape)
        w = pltpu.roll(e, 1, 0)
        faces_b[0, r] = e
        faces_b[1, r] = w
        faces_b[2, r] = n
        faces_b[3, r] = s
        coarse[r] = (
            y + e * (pltpu.roll(y, 55, 0) - y) - w * (y - pltpu.roll(y, 1, 0)) + n * (g[r + 2] - y) - s * (y - g[r])
        )
    for i in range(16):
        boxpad[i, 0:BOX0] = jnp.zeros((BOX0, 128), F32)
        boxpad[i, BOX0 + 32 : 144] = jnp.zeros((56, 128), F32)
    down_mix = pltpu.roll(jnp.concatenate([jnp.zeros((64, 128), F32), square[0:64]], 0), 64, 1)
    row0 = py * H - 1 - arow_ref[0]
    col0 = px * W - 8 - acol_ref[0]
    sub = iota((56, 128), 0)
    lane = iota((56, 128), 1)
    in_cols = (sub + col0 >= 0) & (sub + col0 < 32)
    first = jnp.clip(col0 + BOX0, 0, 88)

    all_rows(row_in, 0).wait_send()
    for s in range(2):
        @pl.when(py != 2 * px + s)
        def _():
            x_copy(s).wait_send()

    b_each(lambda copy: copy.wait_send())
    for i, ref in enumerate((box, inner)):
        pltpu.make_async_remote_copy(
            src_ref=ref, dst_ref=ref, send_sem=c_s.at[i], recv_sem=c_r.at[i], device_id=(1, py, px), device_id_type=MESH
        ).wait_recv()
    lane2 = iota((2, 128), 1)
    for i in range(16):
        for z in range(GX):
            to = BOX0 + 4 * z
            if i in (0, 15):
                boxpad[i, to : to + 4] = box[z + (GX if i else 0)]
            elif z in (0, GX - 1):
                boxpad[i, to : to + 4] = box[2 * GX + 2 * (i - 1) + (1 if z else 0)]
            else:
                pair = inner[(GX - 2) * (i - 1) + z - 1]
                boxpad[i, to : to + 2] = jnp.where(lane2 < 64, pair, F32(0.0))
                boxpad[i, to + 2 : to + 4] = jnp.where(lane2 < 64, pltpu.roll(pair, 64, 1), F32(0.0))
    windows = []
    for i in range(H + 2):
        br = row0 + i
        within = in_cols & (br + 0 * sub >= 0) & (br + 0 * sub < 16)
        window = boxpad[jnp.clip(br, 0, 15), pl.ds(first, 56)]
        w = jnp.where(within, window, g[i])
        g[i] = w
        if 1 <= i <= H:
            coarse[i - 1] = jnp.where(within, window, coarse[i - 1])
    y_all = dot(g[...].reshape((H + 2) * 56, 128), down_mix).reshape(H + 2, 56, 128)
    for r in range(H):
        y = y_all[r + 1]
        res = (
            y
            + faces_b[0, r] * (pltpu.roll(y, 55, 0) - y)
            - faces_b[1, r] * (y - pltpu.roll(y, 1, 0))
            + faces_b[2, r] * (y_all[r + 2] - y)
            - faces_b[3, r] * (y - y_all[r])
        )
        res = jnp.where(lane < 64, coarse[r], res)
        out_ref[r] = res[8:48]


def shards(state_in, cotangent, faces, mixing, anchor_row, anchor_col):
    dma = pltpu.SemaphoreType.DMA
    smem = pl.BlockSpec(memory_space=pltpu.SMEM)
    hbm = pl.BlockSpec(memory_space=pltpu.HBM)
    out = pl.pallas_call(
        kernel,
        name="step",
        out_shape=jax.ShapeDtypeStruct((H, W, 128), F32),
        in_specs=[smem, smem, hbm, hbm, hbm, hbm],
        out_specs=pl.BlockSpec(memory_space=VMEM),
        scratch_shapes=[
            VMEM((H, W, L), F32),
            VMEM((H, W, L), F32),
            VMEM((H, 2, W), F32),
            VMEM((L, 1, L), F32),
            dma((4,)),
            VMEM((H, 64, 128), F32),
            VMEM((H // 2, 128, 128), F32),
            VMEM((H, 2, 128), F32),
            VMEM((128, 128), F32),
            VMEM((CHUNKS, ROWS, 2, 8, 128), F32),
            VMEM((ROWS, 2, 8, 128), F32),
            VMEM((ROWS, 3, 8, 128), F32),
            VMEM((ROWS, 3, 8, 128), F32),
            VMEM((5, 32, 128), F32),
            VMEM((6, ROWS, 1, 8, 128), F32),
            VMEM((2, 48, 128), F32),
            VMEM((H, SUB, 8, 128), F32),
            VMEM((SUB, 16, 8, 128), F32),
            VMEM((5, 128, 128), F32),
            VMEM((2, CHUNKS, 2, 2, 8, 128), F32),
            VMEM((2, CHUNKS, 2, 2, 8, 128), F32),
            VMEM((H, 2, 128), F32),
            VMEM((2, H, 2, 128), F32),
            VMEM((5, GX, 8, 128), F32),
            VMEM((4, 128), F32),
            VMEM((2, 128), F32),
            VMEM((H * W, 128), F32),
            VMEM((H + 2, W, 128), F32),
            VMEM((2, 16, 128), F32),
            VMEM((GY + 2, W, 128), F32),
            VMEM((GY, W, 128), F32),
            VMEM((2, 24, 128), F32),
            VMEM((GY, 24, 128), F32),
            VMEM((120, 128), F32),
            VMEM((2, GX, 8, 128), F32),
            VMEM((H + 2, 56, 128), F32),
            VMEM((W, 128), F32),
            VMEM((W, 128), F32),
            VMEM((16, 128), F32),
            VMEM((16, 128), F32),
            VMEM((4, H, 56, 128), F32),
            VMEM((H, 56, 128), F32),
            VMEM((EDGES, 4, 128), F32),
            VMEM((INNER, 2, 128), F32),
            VMEM((16, 144, 128), F32),
            dma((2, CHUNKS)), dma((2, CHUNKS)), dma((2,)), dma((2,)), dma((2, CHUNKS)), dma((2, CHUNKS)),
            dma((3,)), dma((2,)), dma((4,)), dma((4,)), dma((1,)), dma((5,)), dma((2,)), dma((2,)),
        ],
        compiler_params=pltpu.CompilerParams(collective_id=0, has_side_effects=True, vmem_limit_bytes=56291328),
    )(
        anchor_row, anchor_col, state_in[0].transpose(1, 2, 0), cotangent[0].transpose(1, 2, 0),
        faces[0].transpose(1, 0, 2), mixing.transpose(1, 0, 2),
    )
    both = (out[:, :, 0:L], out[:, :, 64 : 64 + L])
    return tuple(half.transpose(2, 0, 1)[None] for half in both)


def solution(mesh):
    placed = (
        P("grp", None, "gy", "gx"),
        P("grp", None, "gy", "gx"),
        P("grp", None, "gy", "gx"),
        P("grp", None, None),
        P(),
        P(),
    )
    return jax.shard_map(
        shards,
        mesh=mesh,
        in_specs=placed,
        out_specs=(P("grp", None, "gy", "gx"), P("grp", None, "gy", "gx")),
        check_vma=False,
    )
```
